32 devices in a mesh: dp: 2 (over x), seq: 4 (over z), mp: 4 (over y, core).
Axes of the slice: x: 2, y: 2, z: 4, core: 2. Of those that a mesh axis runs over, the one named last changes fastest.
Arguments:
- inputs: bfloat16 [2, 8192, 768], P('dp', 'seq'), may hold values from -6 to 6
- selection: int32 [2, 64, 4], P('dp', 'seq'), may hold values from 0 to 63, as said below
- gain1: float32 [768], replicated, may hold values from 0.5 to 1.5
- shift1: float32 [768], replicated, may hold values from -3 to 3
- w_qkv: bfloat16 [768, 3, 768], P(None, None, 'mp'), may hold values from -0.21875 to 0.21875
- b_qv: float32 [2, 768], P(None, 'mp'), may hold values from -3 to 3
- w_score: bfloat16 [768, 12], P(None, 'mp'), may hold values from -0.3125 to 0.3125
- b_score: float32 [12], P('mp'), may hold values from -3 to 3
- w_out: bfloat16 [768, 768], P('mp'), may hold values from -2 to 2
- b_out: float32 [768], replicated, may hold values from -3 to 3
- gain2: float32 [768], replicated, may hold values from 0.5 to 1.5
- shift2: float32 [768], replicated, may hold values from -3 to 3
- w_up: bfloat16 [768, 3072], P(None, 'mp'), may hold values from -0.21875 to 0.21875
- b_up: float32 [3072], P('mp'), may hold values from -3 to 3
- w_down: bfloat16 [3072, 768], P('mp'), may hold values from -0.109375 to 0.109375
- b_down: float32 [768], replicated, may hold values from -3 to 3
- cotangent: bfloat16 [2, 8192, 768], P('dp', 'seq'), may hold values from -6 to 6
Outputs:
- output: bfloat16 [2, 8192, 768], P('dp', 'seq')
- input_grad: bfloat16 [2, 8192, 768], P('dp', 'seq')
- gain1_grad: float32 [768], replicated
- shift1_grad: float32 [768], replicated
- qkv_grad: float32 [768, 3, 768], P(None, None, 'mp')
- qv_bias_grad: float32 [2, 768], P(None, 'mp')
- score_grad: float32 [768, 12], P(None, 'mp')
- score_bias_grad: float32 [12], P('mp')
- out_grad: float32 [768, 768], P('mp')
- out_bias_grad: float32 [768], replicated
- gain2_grad: float32 [768], replicated
- shift2_grad: float32 [768], replicated
- up_grad: float32 [768, 3072], P(None, 'mp')
- up_bias_grad: float32 [3072], P('mp')
- down_grad: float32 [3072, 768], P('mp')
- down_bias_grad: float32 [768], replicated
The draws below stay inside these ranges and needn't reach their ends.
Inputs may be any that keep to these rules, and one draw needn't show every extreme that they name: selection[s, b, t] names a block of 128 keys of sequence s at or before query block b; selection[s, b, 0] = b.
All inputs are finite; a program needn't handle non-finite values.
Results may differ from the reference program's by a relative error of at most 0.017.
Values may be sent and summed in bfloat16 or wider, within the bound.
No kernel may reach another device: no remote copies, remote signals or barrier semaphores. Data moves between devices by JAX's collectives and lax.ppermute only.
A program may use at most 384 MiB of HBM per device.

```python
import math
import jax
import jax.numpy as jnp
from jax import lax

D = 768
HEADS = 12
HD = 64
FF = 3072
KB = 128
WINDOW = 64
NSEL = 4
SEQS = 2
LEN = 8192


def draw_selection(key, part):
    key = jax.random.fold_in(key, 7)
    blocks = LEN // KB
    block_ids = jnp.arange(blocks, dtype=jnp.int32)[None, :, None]
    upper = jnp.broadcast_to(block_ids + 1, (SEQS, blocks, NSEL))
    picked = jax.random.randint(key, (SEQS, blocks, NSEL), 0, upper, dtype=jnp.int32)
    slot_ids = jnp.arange(NSEL, dtype=jnp.int32)[None, None, :]
    return jnp.where(slot_ids == 0, jnp.broadcast_to(block_ids, picked.shape), picked)


def levels(rng, extent, shards, least, largest):
    def one(axis_at, parts):
        heights = jax.random.uniform(jax.random.fold_in(jax.random.fold_in(rng, 6), axis_at), (parts,), jnp.float32, least / len(shards), largest / len(shards))
        return jnp.repeat(jnp.exp(heights), extent[axis_at] // parts).reshape((-1,) + (1,) * (len(extent) - axis_at - 1))

    level = one(*shards[0])
    for cut in shards[1:]:
        level = level * one(*cut)
    return level


def noise(stream_key, shape, deviation, bound, pieces=(), kind=jnp.bfloat16):
    values = jax.random.normal(stream_key, shape, jnp.float32) * deviation
    if len(pieces) > 0:
        values = levels(stream_key, shape, pieces, -0.22, 0.18) * values
    return jnp.clip(values, min=-bound, max=bound).astype(kind)


def setup_inputs(seed: int = 0) -> dict:
    key_of = jax.random.split(jax.random.key(seed), 18)
    inputs = noise(key_of[0], (SEQS, LEN, D), 1.0, 6.0, ((0, 2), (1, 4)))
    selection = draw_selection(jax.random.fold_in(key_of[17], 71), 0)
    gain1 = jnp.clip(1.0 + 0.1 * jax.random.normal(key_of[2], (D,), jnp.float32), 0.5, 1.5)
    shift1 = noise(key_of[3], (D,), 0.3, 3.0, (), jnp.float32)
    w_qkv = noise(key_of[4], (D, 3, D), D ** -0.5, 0.21875, ((2, 4),))
    b_qv = noise(key_of[5], (2, D), 0.3, 3.0, ((1, 4),), jnp.float32)
    w_score = noise(key_of[6], (D, HEADS), (D // 2) ** -0.5, 0.3125, ((1, 4),))
    b_score = noise(key_of[7], (HEADS,), 1.0, 3.0, ((0, 4),), jnp.float32)
    w_out = noise(key_of[8], (D, D), 8 ** -0.5, 2.0, ((0, 4),))
    b_out = noise(key_of[9], (D,), 0.3, 3.0, (), jnp.float32)
    gain2 = jnp.clip(1.0 + 0.1 * jax.random.normal(key_of[10], (D,), jnp.float32), 0.5, 1.5)
    shift2 = noise(key_of[11], (D,), 0.3, 3.0, (), jnp.float32)
    w_up = noise(key_of[12], (D, FF), D ** -0.5, 0.21875, ((1, 4),))
    b_up = noise(key_of[13], (FF,), 0.3, 3.0, ((0, 4),), jnp.float32)
    w_down = noise(key_of[14], (FF, D), FF ** -0.5, 0.109375, ((0, 4),))
    b_down = noise(key_of[15], (D,), 0.3, 3.0, (), jnp.float32)
    cotangent = noise(key_of[16], (SEQS, LEN, D), 1.0, 6.0, ((0, 2), (1, 4)))
    return dict(inputs=inputs, selection=selection, gain1=gain1, shift1=shift1, w_qkv=w_qkv, b_qv=b_qv, w_score=w_score, b_score=b_score, w_out=w_out, b_out=b_out, gain2=gain2, shift2=shift2, w_up=w_up, b_up=b_up, w_down=w_down, b_down=b_down, cotangent=cotangent)


@jax.custom_vjp
def low(v):
    return lax.optimization_barrier(v.astype(jnp.bfloat16)).astype(jnp.float32)

@jax.custom_vjp
def low_back(v):
    return v

def low_keep(v):
    return (low(v), None)

def low_pass(kept, grad):
    return (grad,)

def back_keep(v):
    return (v, None)

def back_low(kept, grad):
    return (low(grad),)
low.defvjp(low_keep, low_pass)
low_back.defvjp(back_keep, back_low)
EPSILON = 1e-05
NEGATIVE = -1e+30
HIGHEST = lax.Precision.HIGHEST

def layer_norm(value, gain, shift):
    center = lax.optimization_barrier(jnp.mean(value, axis=-1, keepdims=True))
    centered = value - center
    spread = lax.optimization_barrier(jnp.mean(centered * centered, axis=-1, keepdims=True))
    return centered * lax.rsqrt(spread + EPSILON) * gain + shift

def block_masks(block_ids, picked_raw):
    offsets = jnp.arange(KB, dtype=jnp.int32)
    query_pos = block_ids[:, None] * KB + offsets
    key_pos = jnp.maximum(picked_raw, 0)[:, :, None] * KB + offsets
    slot_ids = jnp.arange(picked_raw.shape[1], dtype=jnp.int32)[None, None, :, None]
    query_at = query_pos[:, :, None, None]
    key_at = key_pos[:, None]
    window_mask = (key_at <= query_at) & (key_at > query_at - WINDOW) & (slot_ids < 2) & (picked_raw >= 0)[:, None, :, None]
    chosen_mask = (key_at <= query_at - WINDOW) & (slot_ids >= 2)
    return (window_mask, chosen_mask)

def attend_group(item, key_blocks, value_blocks, mark_blocks):
    query_group, picked_raw, block_ids = item
    picked = jnp.maximum(picked_raw, 0)
    key_cand = jnp.take(key_blocks, picked, axis=0)
    value_cand = jnp.take(value_blocks, picked, axis=0)
    mark_cand = jnp.take(mark_blocks, picked, axis=0)
    window_mask, chosen_mask = block_masks(block_ids, picked_raw)
    logits = jnp.einsum('gihd,gcjhd->ghicj', query_group, key_cand, precision=HIGHEST) * HD ** (-0.5)
    logits = low_back(logits)
    mark_term = mark_cand.transpose(0, 3, 1, 2)[:, :, None]
    scores = jnp.where(window_mask[:, None], logits, jnp.where(chosen_mask[:, None], logits + mark_term, NEGATIVE))
    shape = scores.shape
    weights = jax.nn.softmax(scores.reshape(shape[0], shape[1], shape[2], shape[3] * shape[4]), axis=-1).reshape(shape)
    return jnp.einsum('ghicj,gcjhd->gihd', low(weights), value_cand, precision=HIGHEST)

def forward(tokens, chosen_blocks, gain1, shift1, w_qkv, b_qv, w_score, b_score, w_out, b_out, gain2, shift2, w_up, b_up, w_down, b_down):
    length = tokens.shape[0]
    blocks = length // KB
    first_in = low(layer_norm(tokens, gain1, shift1))
    projected = jnp.einsum('td,dsk->tsk', first_in, w_qkv, precision=HIGHEST)
    query_rows = low_back(low(projected[:, 0] + b_qv[0]))
    key_rows = low_back(low(projected[:, 1]))
    value_rows = low_back(low(projected[:, 2] + b_qv[1]))
    rating = jnp.dot(first_in, w_score, precision=HIGHEST) + b_score
    marks = low(jax.nn.log_sigmoid(rating))
    key_blocks = key_rows.reshape(blocks, KB, HEADS, HD)
    value_blocks = value_rows.reshape(blocks, KB, HEADS, HD)
    mark_blocks = marks.reshape(blocks, KB, HEADS)
    block_ids = jnp.arange(blocks, dtype=jnp.int32)
    picked_raw = jnp.concatenate([block_ids[:, None] - 1, block_ids[:, None], chosen_blocks.astype(jnp.int32)], axis=1)
    group = math.gcd(blocks, 4)
    steps_count = blocks // group
    query_groups = query_rows.reshape(steps_count, group, KB, HEADS, HD)
    attended = lax.map(jax.checkpoint(lambda item: attend_group(item, key_blocks, value_blocks, mark_blocks)), (query_groups, picked_raw.reshape(steps_count, group, -1), block_ids.reshape(steps_count, group)))
    mixed = low_back(low(attended.reshape(length, HEADS * HD)))
    branch = low_back(jnp.dot(mixed, w_out, precision=HIGHEST))
    hidden = tokens + branch + b_out
    second_in = low(layer_norm(hidden, gain2, shift2))
    pre = low_back(jnp.dot(second_in, w_up, precision=HIGHEST) + b_up)
    act = low(jax.nn.gelu(pre, approximate=True))
    return hidden + jnp.dot(act, w_down, precision=HIGHEST) + b_down

def reference(inputs, selection, gain1, shift1, w_qkv, b_qv, w_score, b_score, w_out, b_out, gain2, shift2, w_up, b_up, w_down, b_down, cotangent):
    params = tuple((weight.astype(jnp.float32) for weight in (gain1, shift1, w_qkv, b_qv, w_score, b_score, w_out, b_out, gain2, shift2, w_up, b_up, w_down, b_down)))

    def one_sequence(sums, item):
        tokens, chosen_blocks, upstream = item

        def apply(tokens_in, *weights):
            return forward(tokens_in, chosen_blocks, *weights)
        result, pull = jax.vjp(apply, tokens.astype(jnp.float32), *params)
        grads = pull(upstream.astype(jnp.float32))
        sums = jax.tree.map(lambda left, right: left + right, sums, tuple(grads[1:]))
        return (sums, (result.astype(jnp.bfloat16), grads[0].astype(jnp.bfloat16)))
    zeros = tuple((jnp.zeros_like(weight) for weight in params))
    sums, (outputs, input_grads) = lax.scan(one_sequence, zeros, (inputs, selection, cotangent))
    return (outputs, input_grads, sums[0], sums[1], sums[2], sums[3], sums[4], sums[5], sums[6], sums[7], sums[8], sums[9], sums[10], sums[11], sums[12], sums[13])
```

```python
import functools

import jax
import jax.numpy as jnp
from jax import lax
from jax.experimental import pallas as pl
from jax.experimental.pallas import tpu as pltpu
from jax.sharding import PartitionSpec as P

HD = 64
KB = 128
WINDOW = 64


EPSILON = 1e-05
NEGATIVE = -1e30
HIGHEST = lax.Precision.HIGHEST


def layer_norm(value, gain, shift):
    center = jnp.mean(value, axis=-1, keepdims=True)
    centered = value - center
    spread = jnp.mean(centered * centered, axis=-1, keepdims=True)
    return centered * lax.rsqrt(spread + EPSILON) * gain + shift


def gelu_tanh(value):
    return jax.nn.gelu(value, approximate=True)


def rows_inner(left, right):
    return lax.dot_general(
        left, right, (((0,), (0,)), ((), ())), preferred_element_type=jnp.float32
    )


def cols_inner(left, right):
    return lax.dot_general(
        left, right, (((1,), (1,)), ((), ())), preferred_element_type=jnp.float32
    )


def block_masks(block_ids, picked_raw):
    offsets = jnp.arange(KB, dtype=jnp.int32)
    query_pos = block_ids[:, None] * KB + offsets
    key_pos = jnp.maximum(picked_raw, 0)[:, :, None] * KB + offsets
    slot_ids = jnp.arange(picked_raw.shape[1], dtype=jnp.int32)[None, None, :, None]
    query_at = query_pos[:, :, None, None]
    key_at = key_pos[:, None]
    window_mask = (
        (key_at <= query_at)
        & (key_at > query_at - WINDOW)
        & (slot_ids < 2)
        & (picked_raw >= 0)[:, None, :, None]
    )
    chosen_mask = (key_at <= query_at - WINDOW) & (slot_ids >= 2)
    return (window_mask, chosen_mask)


def block_scores(query_blocks, key_cand, mark_cand, window_mask, chosen_mask):
    logits = jnp.einsum(
        "gihd,gcjhd->ghicj", query_blocks, key_cand, preferred_element_type=jnp.float32
    ) * HD ** (-0.5)
    mark_term = mark_cand.astype(jnp.float32).transpose(0, 3, 1, 2)[:, :, None]
    return jnp.where(
        window_mask[:, None], logits, jnp.where(chosen_mask[:, None], logits + mark_term, NEGATIVE)
    )


def body_general(
    inputs,
    selection,
    gain1,
    shift1,
    w_qkv,
    b_qv,
    w_score,
    b_score,
    w_out,
    b_out,
    gain2,
    shift2,
    w_up,
    b_up,
    w_down,
    b_down,
    cotangent,
):
    seq_rank = lax.axis_index("seq")
    tokens = inputs[0].astype(jnp.float32)
    row_count = tokens.shape[0]
    local_blocks = row_count // KB
    local_width = w_qkv.shape[2]
    local_heads = local_width // HD
    scale = HD ** (-0.5)
    normed1, pull_norm1 = jax.vjp(layer_norm, tokens, gain1, shift1)
    first_in = normed1.astype(jnp.bfloat16)
    projected = jnp.einsum("td,dsk->tsk", first_in, w_qkv, preferred_element_type=jnp.float32)
    query_rows = (projected[:, 0] + b_qv[0]).astype(jnp.bfloat16)
    key_rows = projected[:, 1].astype(jnp.bfloat16)
    value_rows = (projected[:, 2] + b_qv[1]).astype(jnp.bfloat16)
    rating = jnp.dot(first_in, w_score, preferred_element_type=jnp.float32) + b_score
    marks = jax.nn.log_sigmoid(rating).astype(jnp.bfloat16)
    all_keys, all_values, all_marks = (
        lax.all_gather(key_rows, "seq", axis=0, tiled=True),
        lax.all_gather(value_rows, "seq", axis=0, tiled=True),
        lax.all_gather(marks, "seq", axis=0, tiled=True),
    )
    total_blocks = all_keys.shape[0] // KB
    key_blocks = all_keys.reshape(total_blocks, KB, local_heads, HD)
    value_blocks = all_values.reshape(total_blocks, KB, local_heads, HD)
    mark_blocks = all_marks.reshape(total_blocks, KB, local_heads)
    block_ids = seq_rank * local_blocks + jnp.arange(local_blocks, dtype=jnp.int32)
    picked_raw = jnp.concatenate([block_ids[:, None] - 1, block_ids[:, None], selection[0]], axis=1)
    picked = jnp.maximum(picked_raw, 0)
    key_cand = jnp.take(key_blocks, picked, axis=0)
    value_cand = jnp.take(value_blocks, picked, axis=0)
    mark_cand = jnp.take(mark_blocks, picked, axis=0)
    window_mask, chosen_mask = block_masks(block_ids, picked_raw)
    query_blocks = query_rows.reshape(local_blocks, KB, local_heads, HD)
    scores = block_scores(query_blocks, key_cand, mark_cand, window_mask, chosen_mask)
    highest = jnp.max(scores, axis=(3, 4), keepdims=True)
    exponent = jnp.exp(scores - highest)
    summed = jnp.sum(exponent, axis=(3, 4), keepdims=True)
    weights = exponent / summed
    log_norm = highest + jnp.log(summed)
    attended = jnp.einsum(
        "ghicj,gcjhd->gihd",
        weights.astype(jnp.bfloat16),
        value_cand,
        preferred_element_type=jnp.float32,
    )
    mixed = attended.reshape(row_count, local_width).astype(jnp.bfloat16)
    branch = lax.psum(jnp.dot(mixed, w_out, preferred_element_type=jnp.float32), "mp")
    hidden = tokens + branch + b_out
    normed2, pull_norm2 = jax.vjp(layer_norm, hidden, gain2, shift2)
    second_in = normed2.astype(jnp.bfloat16)
    pre = jnp.dot(second_in, w_up, preferred_element_type=jnp.float32) + b_up
    activated, pull_gelu = jax.vjp(gelu_tanh, pre)
    act_low = activated.astype(jnp.bfloat16)
    feed = lax.psum(
        jnp.dot(act_low, w_down, preferred_element_type=jnp.float32).astype(jnp.bfloat16), "mp"
    ).astype(jnp.float32)
    output = (hidden + feed + b_down).astype(jnp.bfloat16)
    upstream = cotangent[0]
    upstream_f = upstream.astype(jnp.float32)
    down_grad = rows_inner(act_low, upstream)
    down_bias_grad = jnp.sum(upstream_f, axis=0)
    act_grad = cols_inner(upstream, w_down)
    pre_grad = pull_gelu(act_grad)[0].astype(jnp.bfloat16)
    up_grad = rows_inner(second_in, pre_grad)
    up_bias_grad = jnp.sum(pre_grad.astype(jnp.float32), axis=0)
    second_grad = lax.psum(cols_inner(pre_grad, w_up), "mp")
    hidden_back, gain2_grad, shift2_grad = pull_norm2(second_grad)
    hidden_grad = upstream_f + hidden_back
    out_bias_grad = jnp.sum(hidden_grad, axis=0)
    branch_grad = hidden_grad.astype(jnp.bfloat16)
    out_grad = rows_inner(mixed, branch_grad)
    mixed_grad = cols_inner(branch_grad, w_out).astype(jnp.bfloat16)
    grad_blocks = mixed_grad.reshape(local_blocks, KB, local_heads, HD)
    again = block_scores(query_blocks, key_cand, mark_cand, window_mask, chosen_mask)
    prob_again = jnp.exp(again - log_norm)
    grad_prob = jnp.einsum(
        "gihd,gcjhd->ghicj", grad_blocks, value_cand, preferred_element_type=jnp.float32
    )
    delta = jnp.sum(prob_again * grad_prob, axis=(3, 4), keepdims=True)
    score_full = prob_again * (grad_prob - delta)
    score_low = score_full.astype(jnp.bfloat16)
    query_grad = (
        (
            jnp.einsum("ghicj,gcjhd->gihd", score_low, key_cand, preferred_element_type=jnp.float32)
            * scale
        )
        .reshape(row_count, local_width)
        .astype(jnp.bfloat16)
    )
    prob_low = prob_again.astype(jnp.bfloat16)
    key_part = (
        jnp.einsum("ghicj,gihd->gcjhd", score_low, query_blocks, preferred_element_type=jnp.float32)
        * scale
    )
    value_part = jnp.einsum(
        "ghicj,gihd->gcjhd", prob_low, grad_blocks, preferred_element_type=jnp.float32
    )
    mark_part = jnp.sum(jnp.where(chosen_mask[:, None], score_full, 0.0), axis=2).transpose(
        0, 2, 3, 1
    )
    key_spread = (
        jnp.zeros((total_blocks, KB, local_heads, HD), jnp.float32).at[picked].add(key_part)
    )
    value_spread = (
        jnp.zeros((total_blocks, KB, local_heads, HD), jnp.float32).at[picked].add(value_part)
    )
    mark_spread = jnp.zeros((total_blocks, KB, local_heads), jnp.float32).at[picked].add(mark_part)
    key_total, value_total, mark_total = (
        lax.psum_scatter(
            key_spread.reshape(total_blocks * KB, local_width),
            "seq",
            scatter_dimension=0,
            tiled=True,
        ),
        lax.psum_scatter(
            value_spread.reshape(total_blocks * KB, local_width),
            "seq",
            scatter_dimension=0,
            tiled=True,
        ),
        lax.psum_scatter(
            mark_spread.reshape(total_blocks * KB, local_heads),
            "seq",
            scatter_dimension=0,
            tiled=True,
        ),
    )
    key_grad = key_total.astype(jnp.bfloat16)
    value_grad = value_total.astype(jnp.bfloat16)
    rating_grad = mark_total * jax.nn.sigmoid(-rating)
    score_grad = lax.dot_general(
        first_in.astype(jnp.float32),
        rating_grad,
        (((0,), (0,)), ((), ())),
        precision=HIGHEST,
        preferred_element_type=jnp.float32,
    )
    score_bias_grad = jnp.sum(rating_grad, axis=0)
    stacked = jnp.stack([query_grad, key_grad, value_grad], axis=1)
    qkv_grad = jnp.einsum("td,tsk->dsk", first_in, stacked, preferred_element_type=jnp.float32)
    qv_bias_grad = jnp.stack(
        [
            jnp.sum(query_grad.astype(jnp.float32), axis=0),
            jnp.sum(value_grad.astype(jnp.float32), axis=0),
        ],
        axis=0,
    )
    first_part = jnp.einsum("tsk,dsk->td", stacked, w_qkv, preferred_element_type=jnp.float32)
    first_part = first_part + jnp.dot(rating_grad, w_score.astype(jnp.float32).T, precision=HIGHEST)
    first_grad = lax.psum(first_part.astype(jnp.bfloat16), "mp").astype(jnp.float32)
    token_back, gain1_grad, shift1_grad = pull_norm1(first_grad)
    input_grad = (hidden_grad + token_back).astype(jnp.bfloat16)
    summed_grads = lax.psum(
        (
            gain1_grad,
            shift1_grad,
            qkv_grad,
            qv_bias_grad,
            score_grad,
            score_bias_grad,
            out_grad,
            out_bias_grad,
            gain2_grad,
            shift2_grad,
            up_grad,
            up_bias_grad,
            down_grad,
            down_bias_grad,
        ),
        ("dp", "seq"),
    )
    return (
        output[None],
        input_grad[None],
        summed_grads[0],
        summed_grads[1],
        summed_grads[2],
        summed_grads[3],
        summed_grads[4],
        summed_grads[5],
        summed_grads[6],
        summed_grads[7],
        summed_grads[8],
        summed_grads[9],
        summed_grads[10],
        summed_grads[11],
        summed_grads[12],
        summed_grads[13],
    )


WIDE = 256
BF = jnp.bfloat16
F32 = jnp.float32


def matmul(left, right):
    return jnp.dot(left, right, preferred_element_type=F32)


def near_far(left, right):
    return lax.dot_general(left, right, (((1,), (1,)), ((), ())), preferred_element_type=F32)


def project_kernel(first, *refs):
    if first:
        (x, gain, shift, wk, wkt, wv, wvt, wqt, bk, bv, bvt, bqt, fi, ka, va, kt, vt, qt) = refs
    else:
        (x, gain, shift, wk, wkt, wv, wvt, bk, bv, bvt) = refs[:10]
        (fi, ka, va, kt, vt) = refs[15:]
    value = x[...].astype(F32)
    center = jnp.mean(value, axis=-1, keepdims=True)
    centered = value - center
    spread = jnp.mean(centered * centered, axis=-1, keepdims=True)
    normed = (centered * lax.rsqrt(spread + EPSILON) * gain[...] + shift[...]).astype(BF)
    fi[...] = normed
    width = kt.shape[0]
    half = WIDE // 2
    heads = width // HD
    base = width - half
    keys = matmul(normed, wk[...]) + bk[...]
    values = matmul(normed, wv[...]) + bv[...]
    low, high = keys[:, :half], keys[:, half:]
    lane = lax.broadcasted_iota(jnp.int32, high.shape, 1) - base
    small = jnp.exp(-jnp.abs(high))
    mark = jnp.minimum(high, 0.0) - jnp.log1p(small)
    slope = jnp.where(high >= 0, small, 1.0) / (1.0 + small)
    ones = jnp.where((lane >= heads) & (lane < heads + 3), 1.0, 0.0)
    marked = (lane >= 0) & (lane < heads)
    ka[:, :half] = low.astype(BF)
    ka[:, half:] = jnp.where(lane < 0, high, jnp.where(marked, mark, ones)).astype(BF)
    va[:, :half] = values[:, :half].astype(BF)
    va[:, half:] = jnp.where(
        lane < 0, values[:, half:], jnp.where(marked, slope, ones)
    ).astype(BF)
    kt[...] = near_far(wkt[...], normed).astype(BF)
    vt[...] = (near_far(wvt[...], normed) + bvt[...]).astype(BF)
    if first:
        query = (near_far(wqt[...], normed) + bqt[...]).astype(BF)
        qt[...] = (query.astype(F32) * HD ** (-0.5)).astype(BF)


def whole(array):
    shape = array.shape
    return pl.BlockSpec(shape, lambda *_: (0,) * len(shape), pipeline_mode=pl.Buffered(1))


def project(x, weights, buffers, place, total, block, queries=None):
    (gain, shift, wk, wkt, wv, wvt, bk, bv, bvt) = weights
    width = wkt.shape[0]
    steps = x.shape[0] // block
    rows = lambda cols: pl.BlockSpec((block, cols), lambda j: (place(j), 0))
    flat = pl.BlockSpec((width, block), lambda j: (0, place(j)))
    out_shape = [
        jax.ShapeDtypeStruct((total, x.shape[1]), BF),
        jax.ShapeDtypeStruct((total, WIDE), BF),
        jax.ShapeDtypeStruct((total, WIDE), BF),
        jax.ShapeDtypeStruct((width, total), BF),
        jax.ShapeDtypeStruct((width, total), BF),
    ]
    out_specs = [rows(x.shape[1]), rows(WIDE), rows(WIDE), flat, flat]
    if buffers is None:
        wqt, bqt = queries
        operands = [x, gain, shift, wk, wkt, wv, wvt, wqt, bk, bv, bvt, bqt]
        extra, aliases = [], {}
        out_shape.append(jax.ShapeDtypeStruct((width, x.shape[0]), BF))
        out_specs.append(pl.BlockSpec((width, block), lambda j: (0, j)))
    else:
        operands = [x, gain, shift, wk, wkt, wv, wvt, bk, bv, bvt]
        extra = list(buffers)
        aliases = {len(operands) + i: i for i in range(len(extra))}
    return pl.pallas_call(
        functools.partial(project_kernel, buffers is None),
        grid=(steps,),
        in_specs=[pl.BlockSpec((block, x.shape[1]), lambda j: (j, 0))]
        + [whole(a) for a in operands[1:]]
        + [pl.BlockSpec(memory_space=pl.ANY) for _ in extra],
        out_specs=out_specs,
        out_shape=out_shape,
        input_output_aliases=aliases,
        compiler_params=pltpu.CompilerParams(vmem_limit_bytes=32 * 1024 * 1024),
        cost_estimate=pl.CostEstimate(
            flops=8 * x.shape[0] * x.shape[1] * WIDE,
            bytes_accessed=x.shape[0] * 2 * (2 * x.shape[1] + 4 * WIDE),
            transcendentals=0,
        ),
        name="project",
    )(*operands, *extra)


def head_diagonal(rows, tail):
    width = rows.shape[0]
    heads = width // HD
    columns = []
    for h in range(heads):
        parts = []
        if h > 0:
            parts.append(jnp.zeros((h * HD, KB), BF))
        parts.append(rows[h * HD : (h + 1) * HD])
        if h < heads - 1:
            parts.append(jnp.zeros(((heads - 1 - h) * HD, KB), BF))
        columns.append(jnp.concatenate(parts, axis=0))
    top = jnp.concatenate(columns, axis=1)
    rest = jnp.zeros((WIDE - width - 16, heads * KB), BF)
    return jnp.concatenate([top, tail.astype(BF), rest], axis=0)


def tail_rows(heads, marked, term):
    shape = (16, heads * KB)
    row = lax.broadcasted_iota(jnp.int32, shape, 0)
    column = lax.broadcasted_iota(jnp.int32, shape, 1) // KB
    tail = jnp.where(row == column, 1.0, 0.0) if marked else jnp.zeros(shape, F32)
    if term is not None:
        for piece in range(3):
            part = term.astype(BF).astype(F32)
            tail = jnp.where(row == heads + piece, part, tail)
            term = term - part
    return tail


def offsets_tile(heads):
    shape = (KB, heads * KB)
    key = lax.broadcasted_iota(jnp.int32, shape, 0)
    query = lax.rem(lax.broadcasted_iota(jnp.int32, shape, 1), KB)
    return key - query


def masks_of(gap, bounds, step):
    previous = gap > bounds[4 * step]
    own = gap <= 0
    return [previous, own] + [gap <= bounds[4 * step + 1 + t] for t in range(3)]


def diagonal_of(full, heads):
    return jnp.concatenate(
        [full[h * HD : (h + 1) * HD, h * KB : (h + 1) * KB] for h in range(heads)], axis=0
    )


def attend_kernel(places, bounds, ka, vt, qt, mixed, norm):
    step = pl.program_id(0)
    width = qt.shape[0]
    heads = width // HD
    query = qt[...]
    plain = head_diagonal(query, tail_rows(heads, False, None))
    marked = head_diagonal(query, tail_rows(heads, True, None))
    starts = [pl.multiple_of(places[5 * step + c] * KB, KB) for c in range(5)]
    tiles = [ka[pl.ds(s, KB), :] for s in starts]
    near = matmul(jnp.concatenate(tiles[:2], axis=0), plain)
    far = matmul(jnp.concatenate(tiles[1:], axis=0), marked)
    gap = offsets_tile(heads)
    masks = masks_of(gap, bounds, step)
    scores = [near[:KB], jnp.where(gap > -WINDOW, near[KB:], far[:KB])]
    scores += [far[KB * (1 + t) : KB * (2 + t)] for t in range(3)]
    scores = [jnp.where(m, s, NEGATIVE) for m, s in zip(masks, scores)]
    top = functools.reduce(jnp.maximum, scores)
    top = jnp.max(top, axis=0, keepdims=True)
    weights = [jnp.exp(s - top) for s in scores]
    total = jnp.sum(functools.reduce(jnp.add, weights), axis=0, keepdims=True)
    stacked = jnp.concatenate([w.astype(BF) for w in weights], axis=0)
    values = jnp.concatenate([vt[:, pl.ds(s, KB)] for s in starts], axis=1)
    full = matmul(values, stacked) / total
    mixed[...] = diagonal_of(full, heads).astype(BF)
    norm[0] = top + jnp.log(total)


def attend(places, bounds, ka, vt, qt, blocks):
    width = qt.shape[0]
    heads = width // HD
    return pl.pallas_call(
        attend_kernel,
        grid_spec=pltpu.PrefetchScalarGridSpec(
            num_scalar_prefetch=2,
            grid=(blocks,),
            in_specs=[whole(ka), whole(vt), pl.BlockSpec((width, KB), lambda i, *_: (0, i))],
            out_specs=[
                pl.BlockSpec((width, KB), lambda i, *_: (0, i)),
                pl.BlockSpec((1, 1, heads * KB), lambda i, *_: (i, 0, 0)),
            ],
        ),
        out_shape=[
            jax.ShapeDtypeStruct((width, blocks * KB), BF),
            jax.ShapeDtypeStruct((blocks, 1, heads * KB), F32),
        ],
        compiler_params=pltpu.CompilerParams(vmem_limit_bytes=40 * 1024 * 1024),
        cost_estimate=pl.CostEstimate(
            flops=4 * blocks * 5 * KB * heads * KB * WIDE,
            bytes_accessed=ka.shape[0] * 4 * WIDE,
            transcendentals=blocks * 5 * KB * heads * KB,
        ),
        name="attend",
    )(places, bounds, ka, vt, qt)


def attend_back_kernel(
    blocks, places, bounds, ka, va, kt, qt, mixed, grad, norm, spread, query_grad, key_sum, value_sum
):
    step = pl.program_id(0)
    width = qt.shape[0]
    heads = width // HD

    @pl.when(step == 0)
    def _():
        key_sum[...] = jnp.zeros_like(key_sum)
        value_sum[...] = jnp.zeros_like(value_sum)

    @pl.when(step < blocks)
    def _():
        query = qt[...]
        upstream = grad[...]
        product = upstream.astype(F32) * mixed[...].astype(F32)
        delta = jnp.concatenate(
            [
                jnp.sum(product[h * HD : (h + 1) * HD], axis=0, keepdims=True)
                for h in range(heads)
            ],
            axis=1,
        )
        plain = head_diagonal(query, tail_rows(heads, False, -norm[0]))
        marked = head_diagonal(query, tail_rows(heads, True, -norm[0]))
        back = head_diagonal(upstream, tail_rows(heads, False, -delta))
        starts = [pl.multiple_of(places[5 * step + c] * KB, KB) for c in range(5)]
        tiles = [ka[pl.ds(s, KB), :] for s in starts]
        near = matmul(jnp.concatenate(tiles[:2], axis=0), plain)
        far = matmul(jnp.concatenate(tiles[1:], axis=0), marked)
        slopes = matmul(jnp.concatenate([va[pl.ds(s, KB), :] for s in starts], axis=0), back)
        gap = offsets_tile(heads)
        masks = masks_of(gap, bounds, step)
        window = gap > -WINDOW
        scores = [near[:KB], jnp.where(window, near[KB:], far[:KB])]
        scores += [far[KB * (1 + t) : KB * (2 + t)] for t in range(3)]
        probs = [jnp.where(m, jnp.exp(s), 0.0) for m, s in zip(masks, scores)]
        signals = [p * slopes[c * KB : (c + 1) * KB] for c, p in enumerate(probs)]
        own = signals[1]
        near_signal = jnp.concatenate([signals[0], jnp.where(window, own, 0.0)], axis=0).astype(BF)
        far_signal = jnp.concatenate(
            [jnp.where(window, 0.0, own)] + signals[2:], axis=0
        ).astype(BF)
        signal = jnp.concatenate(signals, axis=0).astype(BF)
        prob = jnp.concatenate(probs, axis=0).astype(BF)
        near_keys = near_far(near_signal, plain)
        far_keys = near_far(far_signal, marked)
        value_parts = near_far(prob, back)
        key_parts = [near_keys[:KB], near_keys[KB:] + far_keys[:KB]]
        key_parts += [far_keys[KB * (1 + t) : KB * (2 + t)] for t in range(3)]
        for c, s in enumerate(starts):
            key_sum[pl.ds(s, KB), :] += key_parts[c]
            value_sum[pl.ds(s, KB), :] += value_parts[c * KB : (c + 1) * KB]
        keys = jnp.concatenate([kt[:, pl.ds(s, KB)] for s in starts], axis=1)
        full = diagonal_of(matmul(keys, signal), heads) * HD ** (-0.5)
        query_grad[...] = full.astype(BF)

    @pl.when(step >= blocks)
    def _():
        rows = spread.shape[0]
        at = pl.ds(pl.multiple_of((step - blocks) * rows, rows), rows)
        lane = lax.broadcasted_iota(jnp.int32, (rows, WIDE), 1)
        marks = (lane >= width) & (lane < width + heads)
        keys = jnp.where(lane < width, key_sum[at, :], 0.0)
        keys = jnp.where(marks, key_sum[at, :] * va[at, :].astype(F32), keys)
        spread[:, :WIDE] = keys.astype(BF)
        spread[:, WIDE:] = jnp.where(lane < width, value_sum[at, :], 0.0).astype(BF)


def attend_back(places, bounds, ka, va, kt, qt, mixed, grad, norm, blocks):
    width = qt.shape[0]
    heads = width // HD
    total = ka.shape[0]
    rows = 4 * KB
    lanes = pl.BlockSpec((width, KB), lambda i, *_: (0, jnp.minimum(i, blocks - 1)))
    return pl.pallas_call(
        functools.partial(attend_back_kernel, blocks),
        grid_spec=pltpu.PrefetchScalarGridSpec(
            num_scalar_prefetch=2,
            grid=(blocks + total // rows,),
            in_specs=[
                whole(ka),
                whole(va),
                whole(kt),
                lanes,
                lanes,
                lanes,
                pl.BlockSpec(
                    (1, 1, heads * KB), lambda i, *_: (jnp.minimum(i, blocks - 1), 0, 0)
                ),
            ],
            out_specs=[
                pl.BlockSpec((rows, 2 * WIDE), lambda i, *_: (jnp.maximum(i - blocks, 0), 0)),
                lanes,
            ],
            scratch_shapes=[pltpu.VMEM((total, WIDE), F32), pltpu.VMEM((total, WIDE), F32)],
        ),
        out_shape=[
            jax.ShapeDtypeStruct((total, 2 * WIDE), BF),
            jax.ShapeDtypeStruct((width, blocks * KB), BF),
        ],
        compiler_params=pltpu.CompilerParams(vmem_limit_bytes=56 * 1024 * 1024),
        cost_estimate=pl.CostEstimate(
            flops=10 * blocks * 5 * KB * heads * KB * WIDE,
            bytes_accessed=total * 10 * WIDE,
            transcendentals=blocks * 5 * KB * heads * KB,
        ),
        name="attend_back",
    )(places, bounds, ka, va, kt, qt, mixed, grad, norm)


def swap(array, flip):
    return lax.ppermute(array, "mp", [(i, i ^ flip) for i in range(4)])


def upward(array, ranks):
    return lax.ppermute(array, "seq", [(i, i + 1) for i in range(ranks - 1)])


def downward(array, ranks):
    return lax.ppermute(array, "seq", [(i + 1, i) for i in range(ranks - 1)])


def spread_over_mp(part):
    across = swap(part, 2)
    return [part, swap(part, 1), across, swap(across, 1)]


def quarters(array, me, axis=0):
    size = array.shape[axis] // 4
    return [lax.dynamic_slice_in_dim(array, (me ^ j) * size, size, axis) for j in range(4)]


def ordered(parts, me):
    size = parts[0].shape[0]
    out = jnp.zeros((4 * size,) + parts[0].shape[1:], parts[0].dtype)
    for j, part in enumerate(parts):
        out = lax.dynamic_update_slice_in_dim(out, part, (me ^ j) * size, 0)
    return out


def normed_parts(value):
    center = jnp.mean(value, axis=-1, keepdims=True)
    centered = value - center
    spread = jnp.mean(centered * centered, axis=-1, keepdims=True)
    scale = lax.rsqrt(spread + EPSILON)
    return centered * scale, scale


def norm_back(grad, hat, scale, gain):
    g = gain * grad
    return scale * (
        g
        - jnp.mean(g, axis=-1, keepdims=True)
        - hat * jnp.mean(g * hat, axis=-1, keepdims=True)
    )


def body_resident(
    inputs,
    selection,
    gain1,
    shift1,
    w_qkv,
    b_qv,
    w_score,
    b_score,
    w_out,
    b_out,
    gain2,
    shift2,
    w_up,
    b_up,
    w_down,
    b_down,
    cotangent,
):
    ranks = lax.axis_size("seq")
    me, rank = lax.axis_index("mp"), lax.axis_index("seq")
    rows, model = inputs.shape[1:]
    quarter = rows // 4
    total = ranks * rows
    blocks = rows // KB
    per = blocks // 4
    width = w_qkv.shape[2]
    heads = width // HD

    w_ups, w_downs, w_outs = spread_over_mp(w_up), spread_over_mp(w_down), spread_over_mp(w_out)
    b_ups = spread_over_mp(b_up)

    own = quarters(inputs[0], me)
    block = quarter // 2
    arriving = []
    for h in range(2):
        part = own[0][h * block : (h + 1) * block]
        for k in range(1, ranks):
            part = upward(part, ranks)
            arriving.append((k, h, spread_over_mp(part)))

    pad = lambda a, n: jnp.pad(a, ((0, 0), (0, n - a.shape[1])))
    wq, wk, wv = w_qkv[:, 0], w_qkv[:, 1], w_qkv[:, 2]
    wqt, wkt, wvt = wq.T, wk.T, wv.T
    bk = jnp.pad(b_score[None], ((0, 0), (width, WIDE - width - heads)))
    bv = pad(b_qv[1:2], WIDE)
    weights = (
        gain1[None],
        shift1[None],
        pad(jnp.concatenate([wk, w_score], axis=1), WIDE),
        wkt,
        pad(wv, WIDE),
        wvt,
        bk,
        bv,
        b_qv[1][:, None],
    )
    *buffers, qt = project(
        jnp.concatenate(own, axis=0),
        weights,
        None,
        lambda j: j,
        total,
        block,
        (wqt, b_qv[0][:, None]),
    )
    for k, h, parts in sorted(arriving, key=lambda a: a[:2]):
        buffers = project(
            jnp.concatenate(parts, axis=0),
            weights,
            buffers,
            lambda j, k=k, h=h: 8 * k + 2 * j + h,
            total,
            block,
        )
    first_in, ka, va, kt, vt = buffers

    at = jnp.arange(blocks, dtype=jnp.int32)
    natural = ((at // per) ^ me) * per + at % per
    block_ids = rank * blocks + natural
    chosen = jnp.take(selection[0], natural, axis=0)[:, 1:]
    named = jnp.concatenate([block_ids[:, None] - 1, block_ids[:, None], chosen], axis=1)
    named = jnp.maximum(named, 0)
    inner = named % blocks
    places = (rank - named // blocks) * blocks + ((inner // per) ^ me) * per + inner % per
    bounds = jnp.concatenate(
        [
            jnp.where(block_ids[:, None] >= 1, KB - WINDOW, 2 * KB),
            (block_ids[:, None] - chosen) * KB - WINDOW,
        ],
        axis=1,
    )
    places, bounds = places.reshape(-1), bounds.reshape(-1)

    mixed, norm = attend(places, bounds, ka, vt, qt, blocks)

    pieces = [mixed[:, j * quarter : (j + 1) * quarter] for j in range(4)]
    gathered = [pieces[0]] + [swap(pieces[j], j) for j in (1, 2, 3)]
    features = jnp.concatenate(gathered, axis=0)
    w_out_all = jnp.concatenate(w_outs, axis=0)
    tokens = own[0].astype(F32)
    hidden = tokens + rows_inner(features, w_out_all) + b_out
    hat2, scale2 = normed_parts(hidden)
    second_in = (hat2 * gain2 + shift2).astype(BF)
    upstream = lax.dynamic_slice_in_dim(cotangent[0], me * quarter, quarter, 0)
    upstream_f = upstream.astype(F32)
    feed = 0.0
    second_grad = 0.0
    up_grads, down_grads, up_biases = [], [], []
    for j in range(4):
        pre = matmul(second_in, w_ups[j]) + b_ups[j]
        activated, pull_gelu = jax.vjp(gelu_tanh, pre)
        act = activated.astype(BF)
        feed = feed + matmul(act, w_downs[j])
        down_grads.append(rows_inner(act, upstream))
        pre_grad = pull_gelu(cols_inner(upstream, w_downs[j]))[0].astype(BF)
        up_grads.append(rows_inner(second_in, pre_grad))
        up_biases.append(jnp.sum(pre_grad.astype(F32), axis=0))
        second_grad = second_grad + cols_inner(pre_grad, w_ups[j])
    output = (hidden + feed + b_down).astype(BF)
    output_parts = spread_over_mp(output)
    hidden_grad = upstream_f + norm_back(second_grad, hat2, scale2, gain2)
    branch_grad = hidden_grad.astype(BF)
    mixed_grads = cols_inner(w_out_all, branch_grad).astype(BF)
    sent = [mixed_grads[j * width : (j + 1) * width] for j in range(4)]
    returned = jnp.concatenate([sent[0]] + [swap(sent[j], j) for j in (1, 2, 3)], axis=1)

    out_grads = matmul(features, branch_grad)
    sums = [
        jnp.sum(second_grad * hat2, axis=0),
        jnp.sum(second_grad, axis=0),
        jnp.sum(hidden_grad, axis=0),
        jnp.sum(upstream_f, axis=0),
    ]
    packs = []
    for j in range(4):
        lines = jnp.stack([up_biases[j]] + sums + [jnp.zeros_like(sums[0])] * 11, axis=0)
        packs.append(
            jnp.concatenate(
                [
                    up_grads[j].astype(BF),
                    down_grads[j].astype(BF),
                    out_grads[j * width : (j + 1) * width].astype(BF),
                    lines.astype(BF),
                ],
                axis=0,
            )
        )
    kept = [packs[0] + swap(packs[1], 1), packs[2] + swap(packs[3], 1)]
    dense = lax.psum(kept[0] + swap(kept[1], 2), ("dp", "seq"))

    spread, query_grad = attend_back(places, bounds, ka, va, kt, qt, mixed, returned, norm, blocks)

    w_back = jnp.concatenate(
        [wkt, w_score.T, jnp.zeros((WIDE - width - heads, model), BF), wvt]
        + [jnp.zeros((WIDE - width, model), BF)],
        axis=0,
    )
    carried = None
    for k in range(ranks - 1, -1, -1):
        part = matmul(spread[k * rows : (k + 1) * rows], w_back)
        if k == 0:
            part = part + rows_inner(query_grad, wqt)
        part = part.astype(BF)
        parts = [part[j * quarter : (j + 1) * quarter] for j in range(4)]
        mine = parts[0] + swap(parts[1], 1) + swap(parts[2] + swap(parts[3], 1), 2)
        carried = mine if carried is None else mine + downward(carried, ranks)
    first_grad = carried.astype(F32)

    key_value_grad = rows_inner(first_in, spread)
    query_weight_grad = lax.dot_general(
        first_in[:rows], query_grad, (((0,), (1,)), ((), ())), preferred_element_type=F32
    )
    spread_sum = jnp.sum(spread.astype(F32), axis=0)
    query_sum = jnp.sum(query_grad.astype(F32), axis=1)
    score_at = width + heads
    qkv_pack = jnp.concatenate(
        [
            jnp.concatenate(
                [
                    query_weight_grad,
                    key_value_grad[:, :score_at],
                    key_value_grad[:, WIDE : WIDE + width],
                ],
                axis=1,
            ),
            jnp.concatenate(
                [query_sum, spread_sum[:score_at], spread_sum[WIDE : WIDE + width]], axis=0
            )[None],
        ],
        axis=0,
    )
    dense, qkv_pack = lax.optimization_barrier((dense, qkv_pack.astype(BF)))
    qkv_sum = lax.psum(qkv_pack, ("dp", "seq")).astype(F32)

    hat1, scale1 = normed_parts(tokens)
    input_part = (hidden_grad + norm_back(first_grad, hat1, scale1, gain1)).astype(BF)
    input_grad = ordered(spread_over_mp(input_part), me)
    norm1 = lax.psum(
        jnp.stack([jnp.sum(first_grad * hat1, axis=0), jnp.sum(first_grad, axis=0)], axis=0),
        ("dp", "seq", "mp"),
    )
    dense = dense.astype(F32)
    hidden_units = w_up.shape[1]
    at_down = model + hidden_units
    lines = dense[at_down + width :]
    qkv_grad = jnp.stack(
        [
            qkv_sum[:model, :width],
            qkv_sum[:model, width : 2 * width],
            qkv_sum[:model, 2 * width + heads :],
        ],
        axis=1,
    )
    qv_bias_grad = jnp.stack([qkv_sum[model, :width], qkv_sum[model, 2 * width + heads :]], axis=0)
    return (
        ordered(output_parts, me)[None],
        input_grad[None],
        norm1[0],
        norm1[1],
        qkv_grad,
        qv_bias_grad,
        qkv_sum[:model, 2 * width : 2 * width + heads],
        qkv_sum[model, 2 * width : 2 * width + heads],
        dense[at_down : at_down + width],
        lines[3],
        lines[1],
        lines[2],
        dense[:model],
        lines[0],
        dense[model:at_down],
        lines[4],
    )


RESIDENT_TOKENS = 8192


def solution(mesh):
    def body(*args):
        tokens = args[0].shape[1] * mesh.shape["seq"]
        resident = mesh.shape["mp"] == 4 and tokens <= RESIDENT_TOKENS
        return (body_resident if resident else body_general)(*args)

    return jax.shard_map(
        body,
        mesh=mesh,
        in_specs=(
            P("dp", "seq", None),
            P("dp", "seq", None),
            P(),
            P(),
            P(None, None, "mp"),
            P(None, "mp"),
            P(None, "mp"),
            P("mp"),
            P("mp", None),
            P(),
            P(),
            P(),
            P(None, "mp"),
            P("mp"),
            P("mp", None),
            P(),
            P("dp", "seq", None),
        ),
        out_specs=(
            P("dp", "seq", None),
            P("dp", "seq", None),
            P(),
            P(),
            P(None, None, "mp"),
            P(None, "mp"),
            P(None, "mp"),
            P("mp"),
            P("mp", None),
            P(),
            P(),
            P(),
            P(None, "mp"),
            P("mp"),
            P("mp", None),
            P(),
        ),
        check_vma=False,
    )
```

```python
import functools

import jax
import jax.numpy as jnp
from jax import lax
from jax.experimental import pallas as pl
from jax.experimental.pallas import tpu as pltpu
from jax.sharding import PartitionSpec as P

HD = 64
KB = 128
WINDOW = 64


EPSILON = 1e-05
NEGATIVE = -1e30
HIGHEST = lax.Precision.HIGHEST


def layer_norm(value, gain, shift):
    center = jnp.mean(value, axis=-1, keepdims=True)
    centered = value - center
    spread = jnp.mean(centered * centered, axis=-1, keepdims=True)
    return centered * lax.rsqrt(spread + EPSILON) * gain + shift


def gelu_tanh(value):
    return jax.nn.gelu(value, approximate=True)


def rows_inner(left, right):
    return lax.dot_general(
        left, right, (((0,), (0,)), ((), ())), preferred_element_type=jnp.float32
    )


def cols_inner(left, right):
    return lax.dot_general(
        left, right, (((1,), (1,)), ((), ())), preferred_element_type=jnp.float32
    )


def block_masks(block_ids, picked_raw):
    offsets = jnp.arange(KB, dtype=jnp.int32)
    query_pos = block_ids[:, None] * KB + offsets
    key_pos = jnp.maximum(picked_raw, 0)[:, :, None] * KB + offsets
    slot_ids = jnp.arange(picked_raw.shape[1], dtype=jnp.int32)[None, None, :, None]
    query_at = query_pos[:, :, None, None]
    key_at = key_pos[:, None]
    window_mask = (
        (key_at <= query_at)
        & (key_at > query_at - WINDOW)
        & (slot_ids < 2)
        & (picked_raw >= 0)[:, None, :, None]
    )
    chosen_mask = (key_at <= query_at - WINDOW) & (slot_ids >= 2)
    return (window_mask, chosen_mask)


def block_scores(query_blocks, key_cand, mark_cand, window_mask, chosen_mask):
    logits = jnp.einsum(
        "gihd,gcjhd->ghicj", query_blocks, key_cand, preferred_element_type=jnp.float32
    ) * HD ** (-0.5)
    mark_term = mark_cand.astype(jnp.float32).transpose(0, 3, 1, 2)[:, :, None]
    return jnp.where(
        window_mask[:, None], logits, jnp.where(chosen_mask[:, None], logits + mark_term, NEGATIVE)
    )


def body_general(
    inputs,
    selection,
    gain1,
    shift1,
    w_qkv,
    b_qv,
    w_score,
    b_score,
    w_out,
    b_out,
    gain2,
    shift2,
    w_up,
    b_up,
    w_down,
    b_down,
    cotangent,
):
    seq_rank = lax.axis_index("seq")
    tokens = inputs[0].astype(jnp.float32)
    row_count = tokens.shape[0]
    local_blocks = row_count // KB
    local_width = w_qkv.shape[2]
    local_heads = local_width // HD
    scale = HD ** (-0.5)
    normed1, pull_norm1 = jax.vjp(layer_norm, tokens, gain1, shift1)
    first_in = normed1.astype(jnp.bfloat16)
    projected = jnp.einsum("td,dsk->tsk", first_in, w_qkv, preferred_element_type=jnp.float32)
    query_rows = (projected[:, 0] + b_qv[0]).astype(jnp.bfloat16)
    key_rows = projected[:, 1].astype(jnp.bfloat16)
    value_rows = (projected[:, 2] + b_qv[1]).astype(jnp.bfloat16)
    rating = jnp.dot(first_in, w_score, preferred_element_type=jnp.float32) + b_score
    marks = jax.nn.log_sigmoid(rating).astype(jnp.bfloat16)
    all_keys, all_values, all_marks = (
        lax.all_gather(key_rows, "seq", axis=0, tiled=True),
        lax.all_gather(value_rows, "seq", axis=0, tiled=True),
        lax.all_gather(marks, "seq", axis=0, tiled=True),
    )
    total_blocks = all_keys.shape[0] // KB
    key_blocks = all_keys.reshape(total_blocks, KB, local_heads, HD)
    value_blocks = all_values.reshape(total_blocks, KB, local_heads, HD)
    mark_blocks = all_marks.reshape(total_blocks, KB, local_heads)
    block_ids = seq_rank * local_blocks + jnp.arange(local_blocks, dtype=jnp.int32)
    picked_raw = jnp.concatenate([block_ids[:, None] - 1, block_ids[:, None], selection[0]], axis=1)
    picked = jnp.maximum(picked_raw, 0)
    key_cand = jnp.take(key_blocks, picked, axis=0)
    value_cand = jnp.take(value_blocks, picked, axis=0)
    mark_cand = jnp.take(mark_blocks, picked, axis=0)
    window_mask, chosen_mask = block_masks(block_ids, picked_raw)
    query_blocks = query_rows.reshape(local_blocks, KB, local_heads, HD)
    scores = block_scores(query_blocks, key_cand, mark_cand, window_mask, chosen_mask)
    highest = jnp.max(scores, axis=(3, 4), keepdims=True)
    exponent = jnp.exp(scores - highest)
    summed = jnp.sum(exponent, axis=(3, 4), keepdims=True)
    weights = exponent / summed
    log_norm = highest + jnp.log(summed)
    attended = jnp.einsum(
        "ghicj,gcjhd->gihd",
        weights.astype(jnp.bfloat16),
        value_cand,
        preferred_element_type=jnp.float32,
    )
    mixed = attended.reshape(row_count, local_width).astype(jnp.bfloat16)
    branch = lax.psum(jnp.dot(mixed, w_out, preferred_element_type=jnp.float32), "mp")
    hidden = tokens + branch + b_out
    normed2, pull_norm2 = jax.vjp(layer_norm, hidden, gain2, shift2)
    second_in = normed2.astype(jnp.bfloat16)
    pre = jnp.dot(second_in, w_up, preferred_element_type=jnp.float32) + b_up
    activated, pull_gelu = jax.vjp(gelu_tanh, pre)
    act_low = activated.astype(jnp.bfloat16)
    feed = lax.psum(
        jnp.dot(act_low, w_down, preferred_element_type=jnp.float32).astype(jnp.bfloat16), "mp"
    ).astype(jnp.float32)
    output = (hidden + feed + b_down).astype(jnp.bfloat16)
    upstream = cotangent[0]
    upstream_f = upstream.astype(jnp.float32)
    down_grad = rows_inner(act_low, upstream)
    down_bias_grad = jnp.sum(upstream_f, axis=0)
    act_grad = cols_inner(upstream, w_down)
    pre_grad = pull_gelu(act_grad)[0].astype(jnp.bfloat16)
    up_grad = rows_inner(second_in, pre_grad)
    up_bias_grad = jnp.sum(pre_grad.astype(jnp.float32), axis=0)
    second_grad = lax.psum(cols_inner(pre_grad, w_up), "mp")
    hidden_back, gain2_grad, shift2_grad = pull_norm2(second_grad)
    hidden_grad = upstream_f + hidden_back
    out_bias_grad = jnp.sum(hidden_grad, axis=0)
    branch_grad = hidden_grad.astype(jnp.bfloat16)
    out_grad = rows_inner(mixed, branch_grad)
    mixed_grad = cols_inner(branch_grad, w_out).astype(jnp.bfloat16)
    grad_blocks = mixed_grad.reshape(local_blocks, KB, local_heads, HD)
    again = block_scores(query_blocks, key_cand, mark_cand, window_mask, chosen_mask)
    prob_again = jnp.exp(again - log_norm)
    grad_prob = jnp.einsum(
        "gihd,gcjhd->ghicj", grad_blocks, value_cand, preferred_element_type=jnp.float32
    )
    delta = jnp.sum(prob_again * grad_prob, axis=(3, 4), keepdims=True)
    score_full = prob_again * (grad_prob - delta)
    score_low = score_full.astype(jnp.bfloat16)
    query_grad = (
        (
            jnp.einsum("ghicj,gcjhd->gihd", score_low, key_cand, preferred_element_type=jnp.float32)
            * scale
        )
        .reshape(row_count, local_width)
        .astype(jnp.bfloat16)
    )
    prob_low = prob_again.astype(jnp.bfloat16)
    key_part = (
        jnp.einsum("ghicj,gihd->gcjhd", score_low, query_blocks, preferred_element_type=jnp.float32)
        * scale
    )
    value_part = jnp.einsum(
        "ghicj,gihd->gcjhd", prob_low, grad_blocks, preferred_element_type=jnp.float32
    )
    mark_part = jnp.sum(jnp.where(chosen_mask[:, None], score_full, 0.0), axis=2).transpose(
        0, 2, 3, 1
    )
    key_spread = (
        jnp.zeros((total_blocks, KB, local_heads, HD), jnp.float32).at[picked].add(key_part)
    )
    value_spread = (
        jnp.zeros((total_blocks, KB, local_heads, HD), jnp.float32).at[picked].add(value_part)
    )
    mark_spread = jnp.zeros((total_blocks, KB, local_heads), jnp.float32).at[picked].add(mark_part)
    key_total, value_total, mark_total = (
        lax.psum_scatter(
            key_spread.reshape(total_blocks * KB, local_width),
            "seq",
            scatter_dimension=0,
            tiled=True,
        ),
        lax.psum_scatter(
            value_spread.reshape(total_blocks * KB, local_width),
            "seq",
            scatter_dimension=0,
            tiled=True,
        ),
        lax.psum_scatter(
            mark_spread.reshape(total_blocks * KB, local_heads),
            "seq",
            scatter_dimension=0,
            tiled=True,
        ),
    )
    key_grad = key_total.astype(jnp.bfloat16)
    value_grad = value_total.astype(jnp.bfloat16)
    rating_grad = mark_total * jax.nn.sigmoid(-rating)
    score_grad = lax.dot_general(
        first_in.astype(jnp.float32),
        rating_grad,
        (((0,), (0,)), ((), ())),
        precision=HIGHEST,
        preferred_element_type=jnp.float32,
    )
    score_bias_grad = jnp.sum(rating_grad, axis=0)
    stacked = jnp.stack([query_grad, key_grad, value_grad], axis=1)
    qkv_grad = jnp.einsum("td,tsk->dsk", first_in, stacked, preferred_element_type=jnp.float32)
    qv_bias_grad = jnp.stack(
        [
            jnp.sum(query_grad.astype(jnp.float32), axis=0),
            jnp.sum(value_grad.astype(jnp.float32), axis=0),
        ],
        axis=0,
    )
    first_part = jnp.einsum("tsk,dsk->td", stacked, w_qkv, preferred_element_type=jnp.float32)
    first_part = first_part + jnp.dot(rating_grad, w_score.astype(jnp.float32).T, precision=HIGHEST)
    first_grad = lax.psum(first_part.astype(jnp.bfloat16), "mp").astype(jnp.float32)
    token_back, gain1_grad, shift1_grad = pull_norm1(first_grad)
    input_grad = (hidden_grad + token_back).astype(jnp.bfloat16)
    summed_grads = lax.psum(
        (
            gain1_grad,
            shift1_grad,
            qkv_grad,
            qv_bias_grad,
            score_grad,
            score_bias_grad,
            out_grad,
            out_bias_grad,
            gain2_grad,
            shift2_grad,
            up_grad,
            up_bias_grad,
            down_grad,
            down_bias_grad,
        ),
        ("dp", "seq"),
    )
    return (
        output[None],
        input_grad[None],
        summed_grads[0],
        summed_grads[1],
        summed_grads[2],
        summed_grads[3],
        summed_grads[4],
        summed_grads[5],
        summed_grads[6],
        summed_grads[7],
        summed_grads[8],
        summed_grads[9],
        summed_grads[10],
        summed_grads[11],
        summed_grads[12],
        summed_grads[13],
    )


WIDE = 256
BF = jnp.bfloat16
F32 = jnp.float32
ANYWHERE = pl.BlockSpec(memory_space=pl.ANY)


def matmul(left, right):
    return jnp.dot(left, right, preferred_element_type=F32)


def near_far(left, right):
    return lax.dot_general(left, right, (((1,), (1,)), ((), ())), preferred_element_type=F32)


def taking(microseconds):
    return pl.CostEstimate(
        flops=int(microseconds * 1.1e9), bytes_accessed=int(microseconds * 1e5), transcendentals=0
    )


def vmem(mebibytes):
    return pltpu.CompilerParams(vmem_limit_bytes=mebibytes * 1024 * 1024)


def ordered_after(kernel, at, count):
    return lambda *refs: kernel(*refs[:at], *refs[at + count :])


def whole(array):
    shape = array.shape
    return pl.BlockSpec(shape, lambda *_: (0,) * len(shape), pipeline_mode=pl.Buffered(1))


def normed_parts(value):
    center = jnp.mean(value, axis=-1, keepdims=True)
    centered = value - center
    spread = jnp.mean(centered * centered, axis=-1, keepdims=True)
    scale = lax.rsqrt(spread + EPSILON)
    return centered * scale, scale


def norm_back(grad, hat, scale, gain):
    g = gain * grad
    return scale * (
        g
        - jnp.mean(g, axis=-1, keepdims=True)
        - hat * jnp.mean(g * hat, axis=-1, keepdims=True)
    )


def column_sums(array):
    return jnp.sum(array, axis=0, keepdims=True)


def project_rows(width, value, vectors, lines, weights, fi, ka, va, kt, vt, qt):
    hat, _ = normed_parts(value.astype(F32))
    normed = (hat * vectors[0:1, :] + vectors[1:2, :]).astype(BF)
    fi[...] = normed
    half = WIDE // 2
    heads = width // HD
    keys = matmul(normed, weights[0][...]) + lines[0:1, :]
    values = matmul(normed, weights[1][...]) + lines[1:2, :]
    high = keys[:, half:]
    lane = lax.broadcasted_iota(jnp.int32, high.shape, 1) - (width - half)
    small = jnp.exp(-jnp.abs(high))
    mark = jnp.minimum(high, 0.0) - jnp.log1p(small)
    slope = jnp.where(high >= 0, small, 1.0) / (1.0 + small)
    ones = jnp.where((lane >= heads) & (lane < heads + 3), 1.0, 0.0)
    marked = (lane >= 0) & (lane < heads)
    ka[:, :half] = keys[:, :half].astype(BF)
    ka[:, half:] = jnp.where(lane < 0, high, jnp.where(marked, mark, ones)).astype(BF)
    va[:, :half] = values[:, :half].astype(BF)
    va[:, half:] = jnp.where(
        lane < 0, values[:, half:], jnp.where(marked, slope, ones)
    ).astype(BF)
    kt[...] = keys.T[:width].astype(BF)
    vt[...] = values.T[:width].astype(BF)
    if qt is not None:
        query = (matmul(normed, weights[2][...]) + lines[2:3, :]).astype(BF).astype(F32)
        qt[...] = (query * HD ** (-0.5)).T[:width].astype(BF)


def project_own_kernel(ids, x, vectors, lines, wk, wv, wq, fi, ka, va, kt, vt, qt):
    del ids
    project_rows(qt.shape[0], x[...], vectors, lines, (wk, wv, wq), fi, ka, va, kt, vt, qt)


def project_kernel(count, *refs):
    vectors, lines, wk, wv = refs[:4]
    pieces = refs[4 : 4 + count]
    fi, ka, va, kt, vt, held, sems = refs[9 + count :]
    step = pl.program_id(0)

    def copy(j):
        return pltpu.make_async_copy(pieces[j], held.at[j], sems.at[j])

    @pl.when(step == 0)
    def _():
        for j in range(count):
            copy(j).start()

    for j in range(count):

        @pl.when(step == j)
        def _(j=j):
            copy(j).wait()

    project_rows(kt.shape[0], held[step], vectors, lines, (wk, wv), fi, ka, va, kt, vt, None)


def project_shapes(total, model, width):
    return [
        jax.ShapeDtypeStruct((total, model), BF),
        jax.ShapeDtypeStruct((total, WIDE), BF),
        jax.ShapeDtypeStruct((total, WIDE), BF),
        jax.ShapeDtypeStruct((width, total), BF),
        jax.ShapeDtypeStruct((width, total), BF),
    ]


def project_specs(block, model, width, place):
    rows = lambda cols: pl.BlockSpec((block, cols), lambda j, *_: (place(j), 0))
    flat = pl.BlockSpec((width, block), lambda j, *_: (0, place(j)))
    return [rows(model), rows(WIDE), rows(WIDE), flat, flat]


def project_own(ids, x, vectors, lines, weights, width, total, block, after):
    rows, model = x.shape
    per = rows // 4 // block
    operands = [vectors, lines, *weights]
    return pl.pallas_call(
        ordered_after(project_own_kernel, 2 + len(operands), len(after)),
        grid_spec=pltpu.PrefetchScalarGridSpec(
            num_scalar_prefetch=1,
            grid=(rows // block,),
            in_specs=[
                pl.BlockSpec(
                    (block, model),
                    lambda j, ids: (
                        jnp.bitwise_xor(lax.div(j, per), ids[0]) * per + lax.rem(j, per),
                        0,
                    ),
                )
            ]
            + [whole(a) for a in operands]
            + [ANYWHERE] * len(after),
            out_specs=project_specs(block, model, width, lambda j: j)
            + [pl.BlockSpec((width, block), lambda j, *_: (0, j))],
        ),
        out_shape=project_shapes(total, model, width) + [jax.ShapeDtypeStruct((width, rows), BF)],
        compiler_params=vmem(32),
        cost_estimate=taking(8),
        name="project_own",
    )(ids, x, *operands, *after)


def project(pieces, place, vectors, lines, weights, buffers, after=()):
    block, model = pieces[0].shape
    total, width = buffers[0].shape[0], buffers[3].shape[0]
    count = len(pieces)
    operands = [vectors, lines, *weights]
    return pl.pallas_call(
        ordered_after(
            functools.partial(project_kernel, count), len(operands) + count + 5, len(after)
        ),
        grid=(count,),
        in_specs=[whole(a) for a in operands] + [ANYWHERE] * (count + 5 + len(after)),
        out_specs=project_specs(block, model, width, place),
        out_shape=project_shapes(total, model, width),
        scratch_shapes=[
            pltpu.VMEM((count, block, model), BF),
            pltpu.SemaphoreType.DMA((count,)),
        ],
        input_output_aliases={len(operands) + count + i: i for i in range(5)},
        compiler_params=vmem(32),
        cost_estimate=taking(count),
        name="project",
    )(*operands, *pieces, *buffers, *after)


def head_diagonal(rows, tail):
    width = rows.shape[0]
    heads = width // HD
    columns = []
    for h in range(heads):
        parts = []
        if h > 0:
            parts.append(jnp.zeros((h * HD, KB), BF))
        parts.append(rows[h * HD : (h + 1) * HD])
        if h < heads - 1:
            parts.append(jnp.zeros(((heads - 1 - h) * HD, KB), BF))
        columns.append(jnp.concatenate(parts, axis=0))
    top = jnp.concatenate(columns, axis=1)
    rest = jnp.zeros((WIDE - width - 16, heads * KB), BF)
    return jnp.concatenate([top, tail.astype(BF), rest], axis=0)


def tail_rows(heads, marked, term):
    shape = (16, heads * KB)
    row = lax.broadcasted_iota(jnp.int32, shape, 0)
    column = lax.broadcasted_iota(jnp.int32, shape, 1) // KB
    tail = jnp.where(row == column, 1.0, 0.0) if marked else jnp.zeros(shape, F32)
    if term is not None:
        for piece in range(3):
            part = term.astype(BF).astype(F32)
            tail = jnp.where(row == heads + piece, part, tail)
            term = term - part
    return tail


def offsets_tile(heads):
    shape = (KB, heads * KB)
    key = lax.broadcasted_iota(jnp.int32, shape, 0)
    query = lax.rem(lax.broadcasted_iota(jnp.int32, shape, 1), KB)
    return key - query


def spots(ids, chosen, step, blocks):
    me, rank, per = ids[0], ids[1], blocks // 4
    natural = jnp.bitwise_xor(lax.div(step, per), me) * per + lax.rem(step, per)
    block = rank * blocks + natural
    picked = [chosen[natural, t] for t in (1, 2, 3)]
    starts = []
    for name in [jnp.maximum(block - 1, 0), block, *picked]:
        inner = lax.rem(name, blocks)
        place = (rank - lax.div(name, blocks)) * blocks + lax.rem(inner, per)
        place = place + jnp.bitwise_xor(lax.div(inner, per), me) * per
        starts.append(pl.multiple_of(place * KB, KB))
    first = jnp.where(block >= 1, KB - WINDOW, 2 * KB)
    return starts, [first] + [(block - c) * KB - WINDOW for c in picked]


def masks_of(gap, bounds):
    return [gap > bounds[0], gap <= 0] + [gap <= b for b in bounds[1:]]


def diagonal_of(full, heads):
    return jnp.concatenate(
        [full[h * HD : (h + 1) * HD, h * KB : (h + 1) * KB] for h in range(heads)], axis=0
    )


def attend_kernel(blocks, ids, chosen, ka, vt, qt, *outs):
    *mixed, norm = outs
    step = pl.program_id(0)
    width = qt.shape[0]
    heads = width // HD
    query = qt[...]
    plain = head_diagonal(query, tail_rows(heads, False, None))
    marked = head_diagonal(query, tail_rows(heads, True, None))
    starts, bounds = spots(ids, chosen, step, blocks)
    tiles = [ka[pl.ds(s, KB), :] for s in starts]
    near = matmul(jnp.concatenate(tiles[:2], axis=0), plain)
    far = matmul(jnp.concatenate(tiles[1:], axis=0), marked)
    gap = offsets_tile(heads)
    scores = [near[:KB], jnp.where(gap > -WINDOW, near[KB:], far[:KB])]
    scores += [far[KB * (1 + t) : KB * (2 + t)] for t in range(3)]
    scores = [jnp.where(m, s, NEGATIVE) for m, s in zip(masks_of(gap, bounds), scores)]
    top = functools.reduce(jnp.maximum, scores)
    top = jnp.max(top, axis=0, keepdims=True)
    weights = [jnp.exp(s - top) for s in scores]
    total = jnp.sum(functools.reduce(jnp.add, weights), axis=0, keepdims=True)
    stacked = jnp.concatenate([w.astype(BF) for w in weights], axis=0)
    values = jnp.concatenate([vt[:, pl.ds(s, KB)] for s in starts], axis=1)
    full = matmul(values, stacked) / total
    result = diagonal_of(full, heads).astype(BF)
    norm[0] = top + jnp.log(total)
    for p in range(4):

        @pl.when(lax.div(step, blocks // 4) == p)
        def _(p=p):
            mixed[p][...] = result


def attend(ids, chosen, ka, vt, qt, blocks):
    width = qt.shape[0]
    heads = width // HD
    per = blocks // 4
    piece = lambda p: pl.BlockSpec(
        (width, KB), lambda i, *_: (0, jnp.clip(i - per * p, 0, per - 1))
    )
    return pl.pallas_call(
        functools.partial(attend_kernel, blocks),
        grid_spec=pltpu.PrefetchScalarGridSpec(
            num_scalar_prefetch=2,
            grid=(blocks,),
            in_specs=[whole(ka), whole(vt), pl.BlockSpec((width, KB), lambda i, *_: (0, i))],
            out_specs=[piece(p) for p in range(4)]
            + [pl.BlockSpec((1, 1, heads * KB), lambda i, *_: (i, 0, 0))],
        ),
        out_shape=[jax.ShapeDtypeStruct((width, per * KB), BF)] * 4
        + [jax.ShapeDtypeStruct((blocks, 1, heads * KB), F32)],
        compiler_params=vmem(40),
        cost_estimate=taking(14),
        name="attend",
    )(ids, chosen, ka, vt, qt)


def attend_back_kernel(
    blocks,
    ids,
    chosen,
    ka,
    va,
    kt,
    qt,
    norm,
    *refs,
):
    grads = refs[:4]
    spread, query_grad, totals, key_sum, value_sum, grad_all, sems = refs[4:]
    step = pl.program_id(0)
    width = qt.shape[0]
    heads = width // HD
    per = blocks // 4

    def copy(j):
        return pltpu.make_async_copy(grads[j], grad_all.at[j], sems.at[j])

    @pl.when(step == 0)
    def _():
        for j in range(4):
            copy(j).start()
        key_sum[...] = jnp.zeros_like(key_sum)
        value_sum[...] = jnp.zeros_like(value_sum)
        totals[...] = jnp.zeros_like(totals)
        for j in range(4):
            copy(j).wait()

    @pl.when(step < blocks)
    def _():
        query = qt[...]
        lanes = pl.ds(pl.multiple_of(lax.rem(step, per) * KB, KB), KB)
        upstream = grad_all[lax.div(step, per), :, lanes]
        plain = head_diagonal(query, tail_rows(heads, False, -norm[0]))
        marked = head_diagonal(query, tail_rows(heads, True, -norm[0]))
        back = head_diagonal(upstream, tail_rows(heads, False, None))
        starts, bounds = spots(ids, chosen, step, blocks)
        tiles = [ka[pl.ds(s, KB), :] for s in starts]
        near = matmul(jnp.concatenate(tiles[:2], axis=0), plain)
        far = matmul(jnp.concatenate(tiles[1:], axis=0), marked)
        slopes = matmul(jnp.concatenate([va[pl.ds(s, KB), :] for s in starts], axis=0), back)
        gap = offsets_tile(heads)
        masks = masks_of(gap, bounds)
        window = gap > -WINDOW
        scores = [near[:KB], jnp.where(window, near[KB:], far[:KB])]
        scores += [far[KB * (1 + t) : KB * (2 + t)] for t in range(3)]
        probs = [jnp.where(m, jnp.exp(s), 0.0) for m, s in zip(masks, scores)]
        terms = [p * slopes[c * KB : (c + 1) * KB] for c, p in enumerate(probs)]
        delta = column_sums(functools.reduce(jnp.add, terms))
        signals = [t - p * delta for t, p in zip(terms, probs)]
        own = signals[1]
        near_signal = jnp.concatenate([signals[0], jnp.where(window, own, 0.0)], axis=0).astype(BF)
        far_exact = jnp.concatenate([jnp.where(window, 0.0, own)] + signals[2:], axis=0)
        far_signal = far_exact.astype(BF)
        signal = jnp.concatenate(signals, axis=0).astype(BF)
        prob = jnp.concatenate(probs, axis=0).astype(BF)
        near_keys = near_far(near_signal, plain)
        far_keys = near_far(far_signal, marked)
        rest = (far_exact - far_signal.astype(F32)).astype(BF)
        far_rest = near_far(rest, marked[WIDE // 2 :])
        value_parts = near_far(prob, back)
        key_parts = [near_keys[:KB], near_keys[KB:] + far_keys[:KB]]
        key_parts += [far_keys[KB * (1 + t) : KB * (2 + t)] for t in range(3)]
        for c, s in enumerate(starts):
            key_sum[pl.ds(s, KB), :] += key_parts[c]
            value_sum[pl.ds(s, KB), :] += value_parts[c * KB : (c + 1) * KB]
            if c > 0:
                key_sum[pl.ds(s, KB), WIDE // 2 :] += far_rest[(c - 1) * KB : c * KB]
        keys = jnp.concatenate([kt[:, pl.ds(s, KB)] for s in starts], axis=1)
        full = diagonal_of(matmul(keys, signal), heads) * HD ** (-0.5)
        full = jnp.concatenate([full, jnp.zeros((WIDE - width, KB), F32)], axis=0).T
        query_grad[...] = full.astype(BF)
        totals[:, 2 * WIDE :] += column_sums(full)

    @pl.when(step >= blocks)
    def _():
        rows = spread.shape[0]
        at = pl.ds(pl.multiple_of((step - blocks) * rows, rows), rows)
        lane = lax.broadcasted_iota(jnp.int32, (rows, WIDE), 1)
        marks = (lane >= width) & (lane < width + heads)
        keys = jnp.where(lane < width, key_sum[at, :], 0.0)
        keys = jnp.where(marks, key_sum[at, :] * va[at, :].astype(F32), keys)
        values = jnp.where(lane < width, value_sum[at, :], 0.0)
        spread[:, :WIDE] = keys.astype(BF)
        spread[:, WIDE:] = values.astype(BF)
        totals[:, :WIDE] += column_sums(keys)
        totals[:, WIDE : 2 * WIDE] += column_sums(values)


def attend_back(ids, chosen, ka, va, kt, qt, norm, grads, blocks, after=()):
    width = qt.shape[0]
    heads = width // HD
    total = ka.shape[0]
    rows = 4 * KB
    last = lambda i: jnp.minimum(i, blocks - 1)
    return pl.pallas_call(
        ordered_after(functools.partial(attend_back_kernel, blocks), 11, len(after)),
        grid_spec=pltpu.PrefetchScalarGridSpec(
            num_scalar_prefetch=2,
            grid=(blocks + total // rows,),
            in_specs=[
                whole(ka),
                whole(va),
                whole(kt),
                pl.BlockSpec((width, KB), lambda i, *_: (0, last(i))),
                pl.BlockSpec((1, 1, heads * KB), lambda i, *_: (last(i), 0, 0)),
            ]
            + [ANYWHERE] * (4 + len(after)),
            out_specs=[
                pl.BlockSpec((rows, 2 * WIDE), lambda i, *_: (jnp.maximum(i - blocks, 0), 0)),
                pl.BlockSpec((KB, WIDE), lambda i, *_: (last(i), 0)),
                pl.BlockSpec((1, 3 * WIDE), lambda i, *_: (0, 0)),
            ],
            scratch_shapes=[
                pltpu.VMEM((total, WIDE), F32),
                pltpu.VMEM((total, WIDE), F32),
                pltpu.VMEM((4, width, blocks // 4 * KB), BF),
                pltpu.SemaphoreType.DMA((4,)),
            ],
        ),
        out_shape=[
            jax.ShapeDtypeStruct((total, 2 * WIDE), BF),
            jax.ShapeDtypeStruct((blocks * KB, WIDE), BF),
            jax.ShapeDtypeStruct((1, 3 * WIDE), F32),
        ],
        compiler_params=vmem(56),
        cost_estimate=taking(36),
        name="attend_back",
    )(ids, chosen, ka, va, kt, qt, norm, *grads, *after)


def feed_forward_kernel(order, ids, vectors, tokens, upstream, *refs):
    features, outs, ups, downs = refs[:4], refs[4:8], refs[8:12], refs[12:16]
    mixed_grads = refs[16:20]
    output, hidden_grad, kept, sent, kept_out, sent_out, sums, up_biases = refs[20:28]
    out_all, up_all, down_all, hidden, hat, scale, second_in, feed, second_grad, sems = refs[28:]
    step = pl.program_id(0)
    width = features[0].shape[0]
    model = tokens.shape[1]

    def copies(j, turned=False):
        slot = order.index(j)
        up, down = (downs[j], ups[j]) if turned else (ups[j], downs[j])
        return [
            pltpu.make_async_copy(up, up_all.at[slot], sems.at[4 + slot]),
            pltpu.make_async_copy(down, down_all.at[slot], sems.at[8 + slot]),
        ]

    def out_copy(j):
        return pltpu.make_async_copy(outs[j], out_all.at[j], sems.at[j])

    @pl.when(step == 0)
    def _():
        for j in range(4):
            out_copy(j).start()
        for j in order:
            if j < 2:
                for copy in copies(j):
                    copy.start()
            else:

                @pl.when(ids[2] == 0)
                def _(j=j):
                    for copy in copies(j):
                        copy.start()

                @pl.when(ids[2] != 0)
                def _(j=j):
                    for copy in copies(j, True):
                        copy.start()

        for j in range(4):
            out_copy(j).wait()
        branch = vectors[2:3, :]
        for j in range(4):
            branch = branch + rows_inner(features[j][...], out_all[j, :width, :])
        value = tokens[...].astype(F32) + branch
        hidden[...] = value
        normed, inverse = normed_parts(value)
        scale[...] = inverse
        hat[...] = normed
        second_in[...] = (normed * vectors[3:4, :] + vectors[4:5, :]).astype(BF)
        feed[...] = jnp.zeros_like(feed)
        second_grad[...] = jnp.zeros_like(second_grad)

    for slot, j in enumerate(order):

        @pl.when(step == slot)
        def _(j=j):
            for copy in copies(j):
                copy.wait()

    bias = jnp.zeros((1, model), F32)
    for slot, j in enumerate(order):
        lines = out_all[j, width : width + 16, :].astype(F32)
        bias = jnp.where(step == slot, lines[0:1] + lines[1:2], bias)
    up, down = up_all[step], down_all[step]
    pre = matmul(second_in[...], up) + bias
    slope = 0.7978845608028654
    square = pre * pre
    bend = jnp.tanh(slope * pre * (1.0 + 0.044715 * square))
    act = (0.5 * pre * (1.0 + bend)).astype(BF)
    derivative = 0.5 * (1.0 + bend) + 0.5 * pre * (1.0 - bend * bend) * slope * (
        1.0 + 3 * 0.044715 * square
    )
    feed[...] += matmul(act, down)
    pre_grad = near_far(upstream[...], down) * derivative
    pre_low = pre_grad.astype(BF)
    up_biases[0] = column_sums(pre_low.astype(F32))
    second_grad[...] += near_far(pre_low, up)
    up_grad = rows_inner(second_in[...], pre_low).astype(BF)
    down_grad = rows_inner(act, upstream[...]).astype(BF)

    @pl.when(step < 2)
    def _():
        sent[0, :model] = up_grad
        sent[0, model:] = down_grad

    @pl.when(step >= 2)
    def _():
        kept[0, :model] = up_grad
        kept[0, model:] = down_grad

    @pl.when(step == 3)
    def _():
        output[...] = (hidden[...] + feed[...] + vectors[5:6, :]).astype(BF)
        grad = second_grad[...]
        normed = hat[...]
        upstream_f = upstream[...].astype(F32)
        back = upstream_f + norm_back(grad, normed, scale[...], vectors[3:4, :])
        hidden_grad[...] = back
        low = back.astype(BF)
        for j in range(4):
            mixed_grads[j][...] = near_far(out_all[j, :width, :], low).astype(BF)
            out_grad = matmul(features[j][...], low).astype(BF)
            (sent_out if j % 2 else kept_out)[j // 2] = out_grad
        sums[...] = jnp.concatenate(
            [column_sums(a) for a in (grad * normed, grad, back, upstream_f)], axis=0
        )


def feed_forward(ids, vectors, tokens, upstream, features, outs, ups, downs):
    width, quarter = features[0].shape
    model = tokens.shape[1]
    order = (1, 3, 0, 2)
    flat = lambda a: pl.BlockSpec(a.shape, lambda j, *_: (0,) * len(a.shape))
    mine = pl.BlockSpec(
        (quarter, model), lambda j, ids: (ids[0], 0), pipeline_mode=pl.Buffered(1)
    )
    shape = jax.ShapeDtypeStruct
    out_shape = [shape((width, quarter), BF)] * 4 + [
        shape((quarter, model), BF),
        shape((quarter, model), F32),
        shape((2, 2 * model, model), BF),
        shape((2, 2 * model, model), BF),
        shape((2, width, model), BF),
        shape((2, width, model), BF),
        shape((4, model), F32),
        shape((4, 1, model), F32),
    ]
    out_specs = [flat(a) for a in out_shape]
    out_specs[6] = pl.BlockSpec((1, 2 * model, model), lambda j, *_: (jnp.maximum(j - 2, 0), 0, 0))
    out_specs[7] = pl.BlockSpec((1, 2 * model, model), lambda j, *_: (jnp.minimum(j, 1), 0, 0))
    out_specs[11] = pl.BlockSpec((1, 1, model), lambda j, *_: (j, 0, 0))
    return pl.pallas_call(
        functools.partial(feed_forward_kernel, order),
        grid_spec=pltpu.PrefetchScalarGridSpec(
            num_scalar_prefetch=1,
            grid=(4,),
            in_specs=[whole(vectors), mine, mine]
            + [whole(a) for a in features]
            + [ANYWHERE] * 12,
            out_specs=out_specs,
            scratch_shapes=[
                pltpu.VMEM((4, width + 16, model), BF),
                pltpu.VMEM((4, model, model), BF),
                pltpu.VMEM((4, model, model), BF),
                pltpu.VMEM((quarter, model), F32),
                pltpu.VMEM((quarter, model), F32),
                pltpu.VMEM((quarter, 1), F32),
                pltpu.VMEM((quarter, model), BF),
                pltpu.VMEM((quarter, model), F32),
                pltpu.VMEM((quarter, model), F32),
                pltpu.SemaphoreType.DMA((12,)),
            ],
        ),
        out_shape=out_shape,
        compiler_params=vmem(56),
        cost_estimate=taking(30),
        name="feed_forward",
    )(ids, vectors, tokens, upstream, *features, *outs, *ups, *downs)


def push_kernel(spread, wk, wv, *refs):
    kept, sent = refs[-2:]
    step = pl.program_id(0)
    part = near_far(spread[:, :WIDE], wk[...]) + near_far(spread[:, WIDE:], wv[...])
    if len(refs) > 2:
        part = part + near_far(refs[0][...], refs[1][...])
    part = part.astype(BF)

    @pl.when(step < 2)
    def _():
        sent[0] = part

    @pl.when(step >= 2)
    def _():
        kept[0] = part


def push(spread, weights, k, quarter, query_grad=None, after=()):
    wk, wv, wq = weights
    model = wk.shape[0]
    quarter_of = lambda j: 2 * j + 1 - jnp.where(j >= 2, 5, 0)
    operands = [spread, wk, wv]
    in_specs = [
        pl.BlockSpec((quarter, 2 * WIDE), lambda j: (4 * k + quarter_of(j), 0)),
        whole(wk),
        whole(wv),
    ]
    if query_grad is not None:
        operands += [query_grad, wq]
        in_specs += [pl.BlockSpec((quarter, WIDE), lambda j: (quarter_of(j), 0)), whole(wq)]
    return pl.pallas_call(
        ordered_after(push_kernel, len(operands), len(after)),
        grid=(4,),
        in_specs=in_specs + [ANYWHERE] * len(after),
        out_specs=[
            pl.BlockSpec((1, quarter, model), lambda j: (jnp.maximum(j - 2, 0), 0, 0)),
            pl.BlockSpec((1, quarter, model), lambda j: (jnp.minimum(j, 1), 0, 0)),
        ],
        out_shape=[jax.ShapeDtypeStruct((2, quarter, model), BF)] * 2,
        compiler_params=vmem(24),
        cost_estimate=taking(3),
        name="push",
    )(*operands, *after)


def finish_kernel(
    ids, vectors, tokens, arrived, mine, hidden_grad, sums, up_biases, totals, input_part, small
):
    first_grad = arrived[...].astype(F32) + mine[...].astype(F32)
    hat, scale = normed_parts(tokens[...].astype(F32))
    back = hidden_grad[...] + norm_back(first_grad, hat, scale, vectors[0:1, :])
    input_part[...] = back.astype(BF)
    small[...] = jnp.zeros_like(small)
    small[0:4, :] = sums[...]
    for slot, j in enumerate((1, 3, 0, 2)):
        small[pl.ds(4 + jnp.bitwise_xor(ids[0], j), 1), :] = up_biases[slot]
    small[pl.ds(8 + ids[0], 1), :] = totals[...]
    small[12:13, :] = column_sums(first_grad * hat)
    small[13:14, :] = column_sums(first_grad)


def finish(ids, vectors, tokens, arrived, mine, hidden_grad, sums, up_biases, totals):
    quarter, model = mine.shape
    operands = [arrived, mine, hidden_grad, sums, up_biases, totals]
    return pl.pallas_call(
        finish_kernel,
        grid_spec=pltpu.PrefetchScalarGridSpec(
            num_scalar_prefetch=1,
            grid=(1,),
            in_specs=[
                whole(vectors),
                pl.BlockSpec((quarter, model), lambda j, ids: (ids[0], 0)),
            ]
            + [whole(a) for a in operands],
            out_specs=[
                pl.BlockSpec((quarter, model), lambda j, *_: (0, 0)),
                pl.BlockSpec((16, model), lambda j, *_: (0, 0)),
            ],
        ),
        out_shape=[
            jax.ShapeDtypeStruct((quarter, model), BF),
            jax.ShapeDtypeStruct((16, model), F32),
        ],
        compiler_params=vmem(32),
        cost_estimate=taking(4),
        name="finish",
    )(ids, vectors, tokens, *operands)


def ordered_kernel(ids, *refs):
    *parts, out = refs
    for j, part in enumerate(parts):

        @pl.when(pl.program_id(0) == j)
        def _(part=part):
            out[...] = part[...].astype(out.dtype)


def ordered(ids, which, parts, kind):
    size, model = parts[0].shape
    count = len(parts)
    return pl.pallas_call(
        ordered_kernel,
        grid_spec=pltpu.PrefetchScalarGridSpec(
            num_scalar_prefetch=1,
            grid=(count,),
            in_specs=[whole(a) for a in parts],
            out_specs=pl.BlockSpec(
                (size, model), lambda j, ids: (jnp.bitwise_xor(ids[which], j), 0)
            ),
        ),
        out_shape=jax.ShapeDtypeStruct((count * size, model), kind),
        compiler_params=vmem(24),
        cost_estimate=taking(3),
        name="ordered",
    )(ids, *parts)


def held_until(array, after):
    return pl.pallas_call(
        lambda *refs: None,
        in_specs=[ANYWHERE] * (1 + len(after)),
        out_specs=ANYWHERE,
        out_shape=jax.ShapeDtypeStruct(array.shape, array.dtype),
        input_output_aliases={0: 0},
        name="held",
    )(array, *after)


def swap(array, flip, axis="mp"):
    return lax.ppermute(array, axis, [(i, i ^ flip) for i in range(lax.axis_size(axis))])


def upward(array, ranks):
    return lax.ppermute(array, "seq", [(i, i + 1) for i in range(ranks - 1)])


def downward(array, ranks):
    return lax.ppermute(array, "seq", [(i + 1, i) for i in range(ranks - 1)])


def spread_over_mp(part):
    across = swap(part, 2)
    return [part, swap(part, 1), across, swap(across, 1)]


def body_resident(
    inputs,
    selection,
    gain1,
    shift1,
    w_qkv,
    b_qv,
    w_score,
    b_score,
    w_out,
    b_out,
    gain2,
    shift2,
    w_up,
    b_up,
    w_down,
    b_down,
    cotangent,
):
    ranks = lax.axis_size("seq")
    me, rank, side = lax.axis_index("mp"), lax.axis_index("seq"), lax.axis_index("dp")
    ids = jnp.stack([me, rank, side]).astype(jnp.int32)
    rows, model = inputs.shape[1:]
    quarter = rows // 4
    block = quarter // 2
    total = ranks * rows
    blocks = rows // KB
    width = w_qkv.shape[2]
    heads = width // HD

    own = lax.dynamic_slice_in_dim(inputs[0], me * quarter, quarter, 0)
    arriving = {}
    for h in range(2):
        part = own[h * block : (h + 1) * block]
        for k in range(1, ranks):
            part = upward(part, ranks)
            arriving[k, h] = spread_over_mp(part)

    b_high = b_up.astype(BF)
    b_low = (b_up - b_high.astype(F32)).astype(BF)
    out_rows = jnp.concatenate(
        [w_out, b_high[None], b_low[None], jnp.zeros((14, model), BF)], axis=0
    )
    w_outs = spread_over_mp(out_rows)
    first = swap(jnp.where(side == 0, w_up, w_down), 2)
    second = swap(first, 1, "dp")
    w_ups = [w_up, swap(w_up, 1), first, swap(first, 1)]
    w_downs = [w_down, swap(w_down, 1), second, swap(second, 1)]

    vectors = jnp.stack([gain1, shift1, b_out, gain2, shift2, b_down] + [gain1] * 2, axis=0)
    lines = jnp.pad(
        jnp.stack([jnp.pad(b_score, (width, WIDE - width - heads))[:width], b_qv[1], b_qv[0]]),
        ((0, 5), (0, WIDE - width)),
    )
    lines = lax.dynamic_update_slice(lines, b_score[None], (0, width))
    wide = lambda a: jnp.pad(a, ((0, 0), (0, WIDE - a.shape[1])))
    wq, wv = wide(w_qkv[:, 0]), wide(w_qkv[:, 2])
    wk = wide(jnp.concatenate([w_qkv[:, 1], w_score], axis=1))

    last = [arriving[ranks - 1, h][0] for h in range(2)]
    *buffers, qt = project_own(
        ids, inputs[0], vectors, lines, (wk, wv, wq), width, total, block, last
    )
    for k in range(1, ranks - 1):
        pieces = [arriving[k, h][j] for j in range(4) for h in range(2)]
        buffers = project(
            pieces, lambda j, k=k: 8 * k + j, vectors, lines, (wk, wv), buffers, [(first, second)[k - 1]]
        )
    for h in range(2):
        buffers = project(
            arriving[ranks - 1, h],
            lambda j, h=h: 8 * (ranks - 1) + 2 * j + h,
            vectors,
            lines,
            (wk, wv),
            buffers,
        )
    first_in, ka, va, kt, vt = buffers

    chosen = selection[0]
    *mixed, norm = attend(ids, chosen, ka, vt, qt, blocks)

    features = [mixed[0]] + [swap(mixed[j], j) for j in (1, 2, 3)]
    *mixed_grads, output, hidden_grad, kept, sent, kept_out, sent_out, sums, up_biases = (
        feed_forward(ids, vectors, inputs[0], cotangent[0], features, w_outs, w_ups, w_downs)
    )
    returned = [mixed_grads[0]] + [swap(mixed_grads[j], j) for j in (1, 2, 3)]

    given, given_out = swap(sent, 1), swap(sent_out, 1)
    part = 3 * model // 2
    across = [kept[1, :part] + given[1, :part], kept[1, part:] + given[1, part:]]
    across_out = kept_out[1] + given_out[1]
    crossing = [swap(a, 2) for a in (*across, across_out)]

    spread, query_grad, totals = attend_back(
        ids, chosen, ka, va, kt, qt, norm, returned, blocks, (*across, across_out)
    )

    carried, crossed = None, []
    for k in range(ranks - 1, -1, -1):
        pushed, pushed_out = push(
            spread,
            (wk, wv, wq),
            k,
            quarter,
            query_grad if k == 0 else None,
            crossing[:1] if k == 2 else crossing[1:] if k == 0 else (),
        )
        arrived = swap(pushed_out, 1)
        crossed.append(swap(pushed[1] + arrived[1], 2))
        mine = pushed[0] + arrived[0] + crossed[-1]
        if k > 0:
            carried = downward(mine if carried is None else mine + carried, ranks)

    key_value_grad = rows_inner(first_in, spread)
    query_weight_grad = rows_inner(first_in[:rows], query_grad)
    qkv_pack = jnp.concatenate(
        [
            key_value_grad[:, :WIDE],
            key_value_grad[:, WIDE : WIDE + width],
            query_weight_grad[:, :width],
        ],
        axis=1,
    )
    qkv_pack = qkv_pack.astype(BF)
    half = model // 2
    qkv_mine = lax.dynamic_slice_in_dim(qkv_pack, side * half, half, 0)
    qkv_sent = lax.dynamic_slice_in_dim(qkv_pack, (1 - side) * half, half, 0)
    qkv_mine = qkv_mine + swap(qkv_sent, 1, "dp")
    for flip in (1, 2):
        qkv_mine = qkv_mine + swap(qkv_mine, flip, "seq")
    qkv_sum = ordered(ids, 2, [qkv_mine, swap(qkv_mine, 1, "dp")], F32)

    dense = [
        kept[0, :part] + given[0, :part] + crossing[0],
        kept[0, part:] + given[0, part:] + crossing[1],
        kept_out[0] + given_out[0] + crossing[2],
    ]
    dense = lax.psum(dense, ("dp", "seq"))
    *dense, out_grad = [a.astype(F32) for a in dense]
    dense = jnp.concatenate(dense, axis=0)

    input_part, small = finish(
        ids, vectors, inputs[0], carried, mine, hidden_grad, sums, up_biases, totals
    )
    output_parts = spread_over_mp(held_until(output, crossed))
    input_grad = ordered(ids, 0, spread_over_mp(input_part), BF)
    for axis, flips in (("mp", (1, 2)), ("dp", (1,)), ("seq", (1, 2))):
        for flip in flips:
            small = small + swap(small, flip, axis)
    up_bias = lax.dynamic_slice_in_dim(small, 4 + me, 1, 0)[0]
    biases = lax.dynamic_slice_in_dim(small, 8 + me, 1, 0)[0]
    query_at, value_at = WIDE + width, WIDE
    qkv_grad = jnp.stack(
        [qkv_sum[:, query_at:], qkv_sum[:, :width], qkv_sum[:, value_at:query_at]], axis=1
    )
    qv_bias_grad = jnp.stack(
        [biases[2 * WIDE : 2 * WIDE + width], biases[WIDE : WIDE + width]], axis=0
    )
    return (
        ordered(ids, 0, output_parts, BF)[None],
        input_grad[None],
        small[12],
        small[13],
        qkv_grad,
        qv_bias_grad,
        qkv_sum[:, width : width + heads],
        biases[width : width + heads],
        out_grad,
        small[2],
        small[0],
        small[1],
        dense[:model],
        up_bias,
        dense[model:],
        small[3],
    )


RESIDENT_TOKENS = 8192


def solution(mesh):
    def body(*args):
        tokens = args[0].shape[1] * mesh.shape["seq"]
        resident = mesh.shape["mp"] == 4 and mesh.shape["dp"] == 2
        resident = resident and mesh.shape["seq"] == 4 and tokens <= RESIDENT_TOKENS
        return (body_resident if resident else body_general)(*args)

    return jax.shard_map(
        body,
        mesh=mesh,
        in_specs=(
            P("dp", "seq", None),
            P("dp", "seq", None),
            P(),
            P(),
            P(None, None, "mp"),
            P(None, "mp"),
            P(None, "mp"),
            P("mp"),
            P("mp", None),
            P(),
            P(),
            P(),
            P(None, "mp"),
            P("mp"),
            P("mp", None),
            P(),
            P("dp", "seq", None),
        ),
        out_specs=(
            P("dp", "seq", None),
            P("dp", "seq", None),
            P(),
            P(),
            P(None, None, "mp"),
            P(None, "mp"),
            P(None, "mp"),
            P("mp"),
            P("mp", None),
            P(),
            P(),
            P(),
            P(None, "mp"),
            P("mp"),
            P("mp", None),
            P(),
        ),
        check_vma=False,
    )
```

```python
import functools

import jax
import jax.numpy as jnp
from jax import lax
from jax.experimental import pallas as pl
from jax.experimental.pallas import tpu as pltpu
from jax.sharding import PartitionSpec as P

HD = 64
KB = 128
WINDOW = 64


EPSILON = 1e-05
NEGATIVE = -1e30
HIGHEST = lax.Precision.HIGHEST


def layer_norm(value, gain, shift):
    center = jnp.mean(value, axis=-1, keepdims=True)
    centered = value - center
    spread = jnp.mean(centered * centered, axis=-1, keepdims=True)
    return centered * lax.rsqrt(spread + EPSILON) * gain + shift


def gelu_tanh(value):
    return jax.nn.gelu(value, approximate=True)


def rows_inner(left, right):
    return lax.dot_general(
        left, right, (((0,), (0,)), ((), ())), preferred_element_type=jnp.float32
    )


def cols_inner(left, right):
    return lax.dot_general(
        left, right, (((1,), (1,)), ((), ())), preferred_element_type=jnp.float32
    )


def block_masks(block_ids, picked_raw):
    offsets = jnp.arange(KB, dtype=jnp.int32)
    query_pos = block_ids[:, None] * KB + offsets
    key_pos = jnp.maximum(picked_raw, 0)[:, :, None] * KB + offsets
    slot_ids = jnp.arange(picked_raw.shape[1], dtype=jnp.int32)[None, None, :, None]
    query_at = query_pos[:, :, None, None]
    key_at = key_pos[:, None]
    window_mask = (
        (key_at <= query_at)
        & (key_at > query_at - WINDOW)
        & (slot_ids < 2)
        & (picked_raw >= 0)[:, None, :, None]
    )
    chosen_mask = (key_at <= query_at - WINDOW) & (slot_ids >= 2)
    return (window_mask, chosen_mask)


def block_scores(query_blocks, key_cand, mark_cand, window_mask, chosen_mask):
    logits = jnp.einsum(
        "gihd,gcjhd->ghicj", query_blocks, key_cand, preferred_element_type=jnp.float32
    ) * HD ** (-0.5)
    mark_term = mark_cand.astype(jnp.float32).transpose(0, 3, 1, 2)[:, :, None]
    return jnp.where(
        window_mask[:, None], logits, jnp.where(chosen_mask[:, None], logits + mark_term, NEGATIVE)
    )


def body_general(
    inputs,
    selection,
    gain1,
    shift1,
    w_qkv,
    b_qv,
    w_score,
    b_score,
    w_out,
    b_out,
    gain2,
    shift2,
    w_up,
    b_up,
    w_down,
    b_down,
    cotangent,
):
    seq_rank = lax.axis_index("seq")
    tokens = inputs[0].astype(jnp.float32)
    row_count = tokens.shape[0]
    local_blocks = row_count // KB
    local_width = w_qkv.shape[2]
    local_heads = local_width // HD
    scale = HD ** (-0.5)
    normed1, pull_norm1 = jax.vjp(layer_norm, tokens, gain1, shift1)
    first_in = normed1.astype(jnp.bfloat16)
    projected = jnp.einsum("td,dsk->tsk", first_in, w_qkv, preferred_element_type=jnp.float32)
    query_rows = (projected[:, 0] + b_qv[0]).astype(jnp.bfloat16)
    key_rows = projected[:, 1].astype(jnp.bfloat16)
    value_rows = (projected[:, 2] + b_qv[1]).astype(jnp.bfloat16)
    rating = jnp.dot(first_in, w_score, preferred_element_type=jnp.float32) + b_score
    marks = jax.nn.log_sigmoid(rating).astype(jnp.bfloat16)
    all_keys, all_values, all_marks = (
        lax.all_gather(key_rows, "seq", axis=0, tiled=True),
        lax.all_gather(value_rows, "seq", axis=0, tiled=True),
        lax.all_gather(marks, "seq", axis=0, tiled=True),
    )
    total_blocks = all_keys.shape[0] // KB
    key_blocks = all_keys.reshape(total_blocks, KB, local_heads, HD)
    value_blocks = all_values.reshape(total_blocks, KB, local_heads, HD)
    mark_blocks = all_marks.reshape(total_blocks, KB, local_heads)
    block_ids = seq_rank * local_blocks + jnp.arange(local_blocks, dtype=jnp.int32)
    picked_raw = jnp.concatenate([block_ids[:, None] - 1, block_ids[:, None], selection[0]], axis=1)
    picked = jnp.maximum(picked_raw, 0)
    key_cand = jnp.take(key_blocks, picked, axis=0)
    value_cand = jnp.take(value_blocks, picked, axis=0)
    mark_cand = jnp.take(mark_blocks, picked, axis=0)
    window_mask, chosen_mask = block_masks(block_ids, picked_raw)
    query_blocks = query_rows.reshape(local_blocks, KB, local_heads, HD)
    scores = block_scores(query_blocks, key_cand, mark_cand, window_mask, chosen_mask)
    highest = jnp.max(scores, axis=(3, 4), keepdims=True)
    exponent = jnp.exp(scores - highest)
    summed = jnp.sum(exponent, axis=(3, 4), keepdims=True)
    weights = exponent / summed
    log_norm = highest + jnp.log(summed)
    attended = jnp.einsum(
        "ghicj,gcjhd->gihd",
        weights.astype(jnp.bfloat16),
        value_cand,
        preferred_element_type=jnp.float32,
    )
    mixed = attended.reshape(row_count, local_width).astype(jnp.bfloat16)
    branch = lax.psum(jnp.dot(mixed, w_out, preferred_element_type=jnp.float32), "mp")
    hidden = tokens + branch + b_out
    normed2, pull_norm2 = jax.vjp(layer_norm, hidden, gain2, shift2)
    second_in = normed2.astype(jnp.bfloat16)
    pre = jnp.dot(second_in, w_up, preferred_element_type=jnp.float32) + b_up
    activated, pull_gelu = jax.vjp(gelu_tanh, pre)
    act_low = activated.astype(jnp.bfloat16)
    feed = lax.psum(
        jnp.dot(act_low, w_down, preferred_element_type=jnp.float32).astype(jnp.bfloat16), "mp"
    ).astype(jnp.float32)
    output = (hidden + feed + b_down).astype(jnp.bfloat16)
    upstream = cotangent[0]
    upstream_f = upstream.astype(jnp.float32)
    down_grad = rows_inner(act_low, upstream)
    down_bias_grad = jnp.sum(upstream_f, axis=0)
    act_grad = cols_inner(upstream, w_down)
    pre_grad = pull_gelu(act_grad)[0].astype(jnp.bfloat16)
    up_grad = rows_inner(second_in, pre_grad)
    up_bias_grad = jnp.sum(pre_grad.astype(jnp.float32), axis=0)
    second_grad = lax.psum(cols_inner(pre_grad, w_up), "mp")
    hidden_back, gain2_grad, shift2_grad = pull_norm2(second_grad)
    hidden_grad = upstream_f + hidden_back
    out_bias_grad = jnp.sum(hidden_grad, axis=0)
    branch_grad = hidden_grad.astype(jnp.bfloat16)
    out_grad = rows_inner(mixed, branch_grad)
    mixed_grad = cols_inner(branch_grad, w_out).astype(jnp.bfloat16)
    grad_blocks = mixed_grad.reshape(local_blocks, KB, local_heads, HD)
    again = block_scores(query_blocks, key_cand, mark_cand, window_mask, chosen_mask)
    prob_again = jnp.exp(again - log_norm)
    grad_prob = jnp.einsum(
        "gihd,gcjhd->ghicj", grad_blocks, value_cand, preferred_element_type=jnp.float32
    )
    delta = jnp.sum(prob_again * grad_prob, axis=(3, 4), keepdims=True)
    score_full = prob_again * (grad_prob - delta)
    score_low = score_full.astype(jnp.bfloat16)
    query_grad = (
        (
            jnp.einsum("ghicj,gcjhd->gihd", score_low, key_cand, preferred_element_type=jnp.float32)
            * scale
        )
        .reshape(row_count, local_width)
        .astype(jnp.bfloat16)
    )
    prob_low = prob_again.astype(jnp.bfloat16)
    key_part = (
        jnp.einsum("ghicj,gihd->gcjhd", score_low, query_blocks, preferred_element_type=jnp.float32)
        * scale
    )
    value_part = jnp.einsum(
        "ghicj,gihd->gcjhd", prob_low, grad_blocks, preferred_element_type=jnp.float32
    )
    mark_part = jnp.sum(jnp.where(chosen_mask[:, None], score_full, 0.0), axis=2).transpose(
        0, 2, 3, 1
    )
    key_spread = (
        jnp.zeros((total_blocks, KB, local_heads, HD), jnp.float32).at[picked].add(key_part)
    )
    value_spread = (
        jnp.zeros((total_blocks, KB, local_heads, HD), jnp.float32).at[picked].add(value_part)
    )
    mark_spread = jnp.zeros((total_blocks, KB, local_heads), jnp.float32).at[picked].add(mark_part)
    key_total, value_total, mark_total = (
        lax.psum_scatter(
            key_spread.reshape(total_blocks * KB, local_width),
            "seq",
            scatter_dimension=0,
            tiled=True,
        ),
        lax.psum_scatter(
            value_spread.reshape(total_blocks * KB, local_width),
            "seq",
            scatter_dimension=0,
            tiled=True,
        ),
        lax.psum_scatter(
            mark_spread.reshape(total_blocks * KB, local_heads),
            "seq",
            scatter_dimension=0,
            tiled=True,
        ),
    )
    key_grad = key_total.astype(jnp.bfloat16)
    value_grad = value_total.astype(jnp.bfloat16)
    rating_grad = mark_total * jax.nn.sigmoid(-rating)
    score_grad = lax.dot_general(
        first_in.astype(jnp.float32),
        rating_grad,
        (((0,), (0,)), ((), ())),
        precision=HIGHEST,
        preferred_element_type=jnp.float32,
    )
    score_bias_grad = jnp.sum(rating_grad, axis=0)
    stacked = jnp.stack([query_grad, key_grad, value_grad], axis=1)
    qkv_grad = jnp.einsum("td,tsk->dsk", first_in, stacked, preferred_element_type=jnp.float32)
    qv_bias_grad = jnp.stack(
        [
            jnp.sum(query_grad.astype(jnp.float32), axis=0),
            jnp.sum(value_grad.astype(jnp.float32), axis=0),
        ],
        axis=0,
    )
    first_part = jnp.einsum("tsk,dsk->td", stacked, w_qkv, preferred_element_type=jnp.float32)
    first_part = first_part + jnp.dot(rating_grad, w_score.astype(jnp.float32).T, precision=HIGHEST)
    first_grad = lax.psum(first_part.astype(jnp.bfloat16), "mp").astype(jnp.float32)
    token_back, gain1_grad, shift1_grad = pull_norm1(first_grad)
    input_grad = (hidden_grad + token_back).astype(jnp.bfloat16)
    summed_grads = lax.psum(
        (
            gain1_grad,
            shift1_grad,
            qkv_grad,
            qv_bias_grad,
            score_grad,
            score_bias_grad,
            out_grad,
            out_bias_grad,
            gain2_grad,
            shift2_grad,
            up_grad,
            up_bias_grad,
            down_grad,
            down_bias_grad,
        ),
        ("dp", "seq"),
    )
    return (
        output[None],
        input_grad[None],
        summed_grads[0],
        summed_grads[1],
        summed_grads[2],
        summed_grads[3],
        summed_grads[4],
        summed_grads[5],
        summed_grads[6],
        summed_grads[7],
        summed_grads[8],
        summed_grads[9],
        summed_grads[10],
        summed_grads[11],
        summed_grads[12],
        summed_grads[13],
    )


WIDE = 256
BF = jnp.bfloat16
F32 = jnp.float32
ANYWHERE = pl.BlockSpec(memory_space=pl.ANY)
PAIR = 4


def matmul(left, right):
    return jnp.dot(left, right, preferred_element_type=F32)


def near_far(left, right):
    return lax.dot_general(left, right, (((1,), (1,)), ((), ())), preferred_element_type=F32)


def taking(microseconds):
    return pl.CostEstimate(
        flops=int(microseconds * 1.1e9), bytes_accessed=int(microseconds * 1e5), transcendentals=0
    )


def vmem(mebibytes):
    return pltpu.CompilerParams(vmem_limit_bytes=mebibytes * 1024 * 1024)


def ordered_after(kernel, at, count):
    return lambda *refs: kernel(*refs[:at], *refs[at + count :])


def whole(array):
    shape = array.shape
    return pl.BlockSpec(shape, lambda *_: (0,) * len(shape), pipeline_mode=pl.Buffered(1))


def normed_parts(value):
    center = jnp.mean(value, axis=-1, keepdims=True)
    centered = value - center
    spread = jnp.mean(centered * centered, axis=-1, keepdims=True)
    scale = lax.rsqrt(spread + EPSILON)
    return centered * scale, scale


def norm_back(grad, hat, scale, gain):
    g = gain * grad
    return scale * (
        g
        - jnp.mean(g, axis=-1, keepdims=True)
        - hat * jnp.mean(g * hat, axis=-1, keepdims=True)
    )


def column_sums(array):
    return jnp.sum(array, axis=0, keepdims=True)


def project_rows(width, value, vectors, lines, weights, fi, ka, va, qt):
    hat, _ = normed_parts(value.astype(F32))
    normed = (hat * vectors[0:1, :] + vectors[1:2, :]).astype(BF)
    fi[...] = normed
    half = WIDE // 2
    heads = width // HD
    keys = matmul(normed, weights[0][...]) + lines[0:1, :]
    values = matmul(normed, weights[1][...]) + lines[1:2, :]
    high = keys[:, half:]
    lane = lax.broadcasted_iota(jnp.int32, high.shape, 1) - (width - half)
    small = jnp.exp(-jnp.abs(high))
    mark = jnp.minimum(high, 0.0) - jnp.log1p(small)
    slope = jnp.where(high >= 0, small, 1.0) / (1.0 + small)
    ones = jnp.where((lane >= heads) & (lane < heads + 3), 1.0, 0.0)
    marked = (lane >= 0) & (lane < heads)
    ka[:, :half] = keys[:, :half].astype(BF)
    ka[:, half:] = jnp.where(lane < 0, high, jnp.where(marked, mark, ones)).astype(BF)
    va[:, :half] = values[:, :half].astype(BF)
    va[:, half:] = jnp.where(
        lane < 0, values[:, half:], jnp.where(marked, slope, ones)
    ).astype(BF)
    if qt is not None:
        query = (matmul(normed, weights[2][...]) + lines[2:3, :]).astype(BF).astype(F32)
        qt[...] = (query * HD ** (-0.5)).T[:width].astype(BF)


def project_own_kernel(ids, x, vectors, lines, wk, wv, wq, fi, ka, va, qt):
    del ids
    project_rows(qt.shape[0], x[...], vectors, lines, (wk, wv, wq), fi, ka, va, qt)


def project_kernel(sources, arrays, width, *refs):
    vectors, lines, wk, wv = refs[:4]
    fi, ka, va, held, sems = refs[7 + arrays :]
    step = pl.program_id(0)
    count, block = held.shape[:2]

    def copy(j):
        array, row = sources[j]
        return pltpu.make_async_copy(
            refs[4 + array].at[pl.ds(row, block), :], held.at[j], sems.at[j]
        )

    @pl.when(step == 0)
    def _():
        for j in range(count):
            copy(j).start()

    for j in range(count):

        @pl.when(step == j)
        def _(j=j):
            copy(j).wait()

    project_rows(width, held[step], vectors, lines, (wk, wv), fi, ka, va, None)


def project_shapes(total, model):
    return [
        jax.ShapeDtypeStruct((total, model), BF),
        jax.ShapeDtypeStruct((total, WIDE), BF),
        jax.ShapeDtypeStruct((total, WIDE), BF),
    ]


def project_specs(block, model, place):
    rows = lambda cols: pl.BlockSpec((block, cols), lambda j, *_: (place(j), 0))
    return [rows(model), rows(WIDE), rows(WIDE)]


def project_own(ids, x, vectors, lines, weights, width, total, block, after):
    rows, model = x.shape
    per = rows // 4 // block
    operands = [vectors, lines, *weights]
    return pl.pallas_call(
        ordered_after(project_own_kernel, 2 + len(operands), len(after)),
        grid_spec=pltpu.PrefetchScalarGridSpec(
            num_scalar_prefetch=1,
            grid=(rows // block,),
            in_specs=[
                pl.BlockSpec(
                    (block, model),
                    lambda j, ids: (
                        jnp.bitwise_xor(lax.div(j, per), ids[0]) * per + lax.rem(j, per),
                        0,
                    ),
                )
            ]
            + [whole(a) for a in operands]
            + [ANYWHERE] * len(after),
            out_specs=project_specs(block, model, lambda j: j)
            + [pl.BlockSpec((width, block), lambda j, *_: (0, j))],
        ),
        out_shape=project_shapes(total, model) + [jax.ShapeDtypeStruct((width, rows), BF)],
        compiler_params=vmem(32),
        cost_estimate=taking(8),
        name="project_own",
    )(ids, x, *operands, *after)


def project(arrays, sources, block, width, place, vectors, lines, weights, buffers, after=()):
    model = arrays[0].shape[1]
    total = buffers[0].shape[0]
    count, given = len(sources), len(arrays)
    operands = [vectors, lines, *weights]
    return pl.pallas_call(
        ordered_after(
            functools.partial(project_kernel, sources, given, width),
            len(operands) + given + 3,
            len(after),
        ),
        grid=(count,),
        in_specs=[whole(a) for a in operands] + [ANYWHERE] * (given + 3 + len(after)),
        out_specs=project_specs(block, model, place),
        out_shape=project_shapes(total, model),
        scratch_shapes=[
            pltpu.VMEM((count, block, model), BF),
            pltpu.SemaphoreType.DMA((count,)),
        ],
        input_output_aliases={len(operands) + given + i: i for i in range(3)},
        compiler_params=vmem(32),
        cost_estimate=taking(count),
        name="project",
    )(*operands, *arrays, *buffers, *after)


def head_diagonal(rows, tail):
    width = rows.shape[0]
    heads = width // HD
    columns = []
    for h in range(heads):
        parts = []
        if h > 0:
            parts.append(jnp.zeros((h * HD, KB), BF))
        parts.append(rows[h * HD : (h + 1) * HD])
        if h < heads - 1:
            parts.append(jnp.zeros(((heads - 1 - h) * HD, KB), BF))
        columns.append(jnp.concatenate(parts, axis=0))
    top = jnp.concatenate(columns, axis=1)
    rest = jnp.zeros((WIDE - width - 16, heads * KB), BF)
    return jnp.concatenate([top, tail.astype(BF), rest], axis=0)


def tail_rows(heads, marked, term):
    shape = (16, heads * KB)
    row = lax.broadcasted_iota(jnp.int32, shape, 0)
    column = lax.broadcasted_iota(jnp.int32, shape, 1) // KB
    tail = jnp.where(row == column, 1.0, 0.0) if marked else jnp.zeros(shape, F32)
    if term is not None:
        for piece in range(3):
            part = term.astype(BF).astype(F32)
            tail = jnp.where(row == heads + piece, part, tail)
            term = term - part
    return tail


def offsets_tile(heads):
    shape = (KB, heads * KB)
    key = lax.broadcasted_iota(jnp.int32, shape, 0)
    query = lax.rem(lax.broadcasted_iota(jnp.int32, shape, 1), KB)
    return key - query


def spots(ids, chosen, step, blocks):
    me, rank, per = ids[0], ids[1], blocks // 4
    natural = jnp.bitwise_xor(lax.div(step, per), me) * per + lax.rem(step, per)
    block = rank * blocks + natural
    picked = [chosen[natural, t] for t in (1, 2, 3)]
    starts = []
    for name in [jnp.maximum(block - 1, 0), block, *picked]:
        inner = lax.rem(name, blocks)
        place = (rank - lax.div(name, blocks)) * blocks + lax.rem(inner, per)
        place = place + jnp.bitwise_xor(lax.div(inner, per), me) * per
        starts.append(pl.multiple_of(place * KB, KB))
    first = jnp.where(block >= 1, KB - WINDOW, 2 * KB)
    return starts, [first] + [(block - c) * KB - WINDOW for c in picked]


def masks_of(gap, bounds):
    return [gap > bounds[0], gap <= 0] + [gap <= b for b in bounds[1:]]


def diagonal_of(full, heads):
    return jnp.concatenate(
        [full[h * HD : (h + 1) * HD, h * KB : (h + 1) * KB] for h in range(heads)], axis=0
    )


def attend_kernel(blocks, ids, chosen, ka, va, qt, *outs):
    *mixed, norm = outs
    step = pl.program_id(0)
    width = qt.shape[0]
    heads = width // HD

    def block_forward(at):
        query = qt[:, at * KB : (at + 1) * KB]
        plain = head_diagonal(query, tail_rows(heads, False, None))
        marked = head_diagonal(query, tail_rows(heads, True, None))
        starts, bounds = spots(ids, chosen, step * PAIR + at, blocks)
        tiles = [ka[pl.ds(s, KB), :] for s in starts]
        near = matmul(jnp.concatenate(tiles[:2], axis=0), plain)
        far = matmul(jnp.concatenate(tiles[1:], axis=0), marked)
        gap = offsets_tile(heads)
        scores = [near[:KB], jnp.where(gap > -WINDOW, near[KB:], far[:KB])]
        scores += [far[KB * (1 + t) : KB * (2 + t)] for t in range(3)]
        scores = [jnp.where(m, s, NEGATIVE) for m, s in zip(masks_of(gap, bounds), scores)]
        top = functools.reduce(jnp.maximum, scores)
        top = jnp.max(top, axis=0, keepdims=True)
        weights = [jnp.exp(s - top) for s in scores]
        total = jnp.sum(functools.reduce(jnp.add, weights), axis=0, keepdims=True)
        stacked = jnp.concatenate([w.astype(BF) for w in weights], axis=0)
        values = jnp.concatenate([va[pl.ds(s, KB), :] for s in starts], axis=0)
        full = rows_inner(values, stacked) / total
        return diagonal_of(full, heads).astype(BF), top + jnp.log(total)

    results = [block_forward(at) for at in range(PAIR)]
    for at, (_, line) in enumerate(results):
        norm[at] = line
    result = jnp.concatenate([value for value, _ in results], axis=1)
    for p in range(4):

        @pl.when(lax.div(step, blocks // 4 // PAIR) == p)
        def _(p=p):
            mixed[p][...] = result


def attend(ids, chosen, ka, va, qt, blocks):
    width = qt.shape[0]
    heads = width // HD
    per = blocks // 4
    turns = per // PAIR
    piece = lambda p: pl.BlockSpec(
        (width, PAIR * KB), lambda i, *_: (0, jnp.clip(i - turns * p, 0, turns - 1))
    )
    return pl.pallas_call(
        functools.partial(attend_kernel, blocks),
        grid_spec=pltpu.PrefetchScalarGridSpec(
            num_scalar_prefetch=2,
            grid=(blocks // PAIR,),
            in_specs=[
                whole(ka),
                whole(va),
                pl.BlockSpec((width, PAIR * KB), lambda i, *_: (0, i)),
            ],
            out_specs=[piece(p) for p in range(4)]
            + [pl.BlockSpec((PAIR, 1, heads * KB), lambda i, *_: (i, 0, 0))],
        ),
        out_shape=[jax.ShapeDtypeStruct((width, per * KB), BF)] * 4
        + [jax.ShapeDtypeStruct((blocks, 1, heads * KB), F32)],
        compiler_params=vmem(40),
        cost_estimate=taking(14),
        name="attend",
    )(ids, chosen, ka, va, qt)


def attend_back_kernel(
    blocks,
    ids,
    chosen,
    ka,
    va,
    qt,
    norm,
    *refs,
):
    grads = refs[:4]
    spread, query_grad, totals, key_sum, value_sum, grad_all, sems = refs[4:]
    step = pl.program_id(0)
    width = qt.shape[0]
    heads = width // HD
    per, steps = blocks // 4, blocks // PAIR

    def copy(j):
        return pltpu.make_async_copy(grads[j], grad_all.at[j], sems.at[j])

    @pl.when(step == 0)
    def _():
        for j in range(4):
            copy(j).start()
        key_sum[...] = jnp.zeros_like(key_sum)
        value_sum[...] = jnp.zeros_like(value_sum)
        totals[...] = jnp.zeros_like(totals)
        for j in range(4):
            copy(j).wait()

    def block_back(at):
        index = step * PAIR + at
        column = slice(at * KB, (at + 1) * KB)
        query = qt[:, column]
        lanes = pl.ds(pl.multiple_of(lax.rem(index, per) * KB, KB), KB)
        upstream = grad_all[lax.div(index, per), :, lanes]
        plain = head_diagonal(query, tail_rows(heads, False, -norm[at]))
        marked = head_diagonal(query, tail_rows(heads, True, -norm[at]))
        back = head_diagonal(upstream, tail_rows(heads, False, None))
        starts, bounds = spots(ids, chosen, index, blocks)
        tiles = [ka[pl.ds(s, KB), :] for s in starts]
        near = matmul(jnp.concatenate(tiles[:2], axis=0), plain)
        far = matmul(jnp.concatenate(tiles[1:], axis=0), marked)
        slopes = matmul(jnp.concatenate([va[pl.ds(s, KB), :] for s in starts], axis=0), back)
        gap = offsets_tile(heads)
        masks = masks_of(gap, bounds)
        window = gap > -WINDOW
        scores = [near[:KB], jnp.where(window, near[KB:], far[:KB])]
        scores += [far[KB * (1 + t) : KB * (2 + t)] for t in range(3)]
        probs = [jnp.where(m, jnp.exp(s), 0.0) for m, s in zip(masks, scores)]
        terms = [p * slopes[c * KB : (c + 1) * KB] for c, p in enumerate(probs)]
        delta = column_sums(functools.reduce(jnp.add, terms))
        signals = [t - p * delta for t, p in zip(terms, probs)]
        own = signals[1]
        near_signal = jnp.concatenate([signals[0], jnp.where(window, own, 0.0)], axis=0).astype(BF)
        far_exact = jnp.concatenate([jnp.where(window, 0.0, own)] + signals[2:], axis=0)
        far_signal = far_exact.astype(BF)
        signal = jnp.concatenate(signals, axis=0).astype(BF)
        prob = jnp.concatenate(probs, axis=0).astype(BF)
        near_keys = near_far(near_signal, plain)
        far_keys = near_far(far_signal, marked)
        value_parts = near_far(prob, back)
        key_parts = [near_keys[:KB], near_keys[KB:] + far_keys[:KB]]
        key_parts += [far_keys[KB * (1 + t) : KB * (2 + t)] for t in range(3)]
        value_parts = [value_parts[c * KB : (c + 1) * KB] for c in range(5)]
        rest = (far_exact - far_signal.astype(F32)).astype(BF)
        far_rest = near_far(rest, marked[WIDE // 2 :])
        far_rest = [far_rest[c * KB : (c + 1) * KB] for c in range(4)]
        keys = jnp.concatenate([tiles[0], tiles[1]] + tiles[2:], axis=0)
        full = diagonal_of(rows_inner(keys, signal), heads) * HD ** (-0.5)
        full = jnp.concatenate([full, jnp.zeros((WIDE - width, KB), F32)], axis=0).T
        return starts, key_parts, value_parts, far_rest, full

    @pl.when(step < steps)
    def _():
        results = [block_back(at) for at in range(PAIR)]
        for at, (starts, key_parts, value_parts, far_rest, full) in enumerate(results):
            for c, s in enumerate(starts):
                key_sum[pl.ds(s, KB), :] += key_parts[c]
                value_sum[pl.ds(s, KB), :] += value_parts[c]
                if c > 0:
                    key_sum[pl.ds(s, KB), WIDE // 2 :] += far_rest[c - 1]
            query_grad[at * KB : (at + 1) * KB, :] = full.astype(BF)
            totals[:, 2 * WIDE :] += column_sums(full)

    @pl.when(step >= steps)
    def _():
        rows = spread.shape[0]
        at = pl.ds(pl.multiple_of((step - steps) * rows, rows), rows)
        lane = lax.broadcasted_iota(jnp.int32, (rows, WIDE), 1)
        marks = (lane >= width) & (lane < width + heads)
        keys = jnp.where(lane < width, key_sum[at, :], 0.0)
        keys = jnp.where(marks, key_sum[at, :] * va[at, :].astype(F32), keys)
        values = jnp.where(lane < width, value_sum[at, :], 0.0)
        spread[:, :WIDE] = keys.astype(BF)
        spread[:, WIDE:] = values.astype(BF)
        totals[:, :WIDE] += column_sums(keys)
        totals[:, WIDE : 2 * WIDE] += column_sums(values)


def attend_back(ids, chosen, ka, va, qt, norm, grads, blocks, after=()):
    width = qt.shape[0]
    heads = width // HD
    total = ka.shape[0]
    rows = 8 * KB
    steps = blocks // PAIR
    last = lambda i: jnp.minimum(i, steps - 1)
    return pl.pallas_call(
        ordered_after(functools.partial(attend_back_kernel, blocks), 10, len(after)),
        grid_spec=pltpu.PrefetchScalarGridSpec(
            num_scalar_prefetch=2,
            grid=(steps + total // rows,),
            in_specs=[
                whole(ka),
                whole(va),
                pl.BlockSpec((width, PAIR * KB), lambda i, *_: (0, last(i))),
                pl.BlockSpec((PAIR, 1, heads * KB), lambda i, *_: (last(i), 0, 0)),
            ]
            + [ANYWHERE] * (4 + len(after)),
            out_specs=[
                pl.BlockSpec((rows, 2 * WIDE), lambda i, *_: (jnp.maximum(i - steps, 0), 0)),
                pl.BlockSpec((PAIR * KB, WIDE), lambda i, *_: (last(i), 0)),
                pl.BlockSpec((1, 3 * WIDE), lambda i, *_: (0, 0)),
            ],
            scratch_shapes=[
                pltpu.VMEM((total, WIDE), F32),
                pltpu.VMEM((total, WIDE), F32),
                pltpu.VMEM((4, width, blocks // 4 * KB), BF),
                pltpu.SemaphoreType.DMA((4,)),
            ],
        ),
        out_shape=[
            jax.ShapeDtypeStruct((total, 2 * WIDE), BF),
            jax.ShapeDtypeStruct((blocks * KB, WIDE), BF),
            jax.ShapeDtypeStruct((1, 3 * WIDE), F32),
        ],
        compiler_params=vmem(56),
        cost_estimate=taking(36),
        name="attend_back",
    )(ids, chosen, ka, va, qt, norm, *grads, *after)


def feed_forward_kernel(order, ids, vectors, tokens, upstream, *refs):
    features, outs, ups, downs = refs[:4], refs[4:8], refs[8:12], refs[12:16]
    mixed_grads = refs[16:20]
    output, hidden_grad, kept, sent, sums, up_biases = refs[20:26]
    out_all, up_all, down_all, hidden, hat, scale, second_in, feed, second_grad = refs[26:35]
    staged, staged_out, sems, out_sems = refs[35:]
    step = pl.program_id(0)
    width = features[0].shape[0]
    model = tokens.shape[1]

    def copies(j, turned=False):
        slot = order.index(j)
        up, down = (downs[j], ups[j]) if turned else (ups[j], downs[j])
        return [
            pltpu.make_async_copy(up, up_all.at[slot], sems.at[4 + slot]),
            pltpu.make_async_copy(down, down_all.at[slot], sems.at[8 + slot]),
        ]

    def leaving(slot, first=0, last=5):
        target = (sent if slot < 2 else kept).at[slot % 2]
        half, out_half = model // 2, width // 2
        spans = [(staged, 0, 0, half), (staged, half, half + out_half, half)]
        spans += [(staged, model, model + width, model)]
        spans += [(staged_out, 0, half, out_half), (staged_out, out_half, model + out_half, out_half)]
        return [
            pltpu.make_async_copy(
                source.at[slot, pl.ds(a, n), :], target.at[pl.ds(b, n), :], out_sems.at[slot, i]
            )
            for i, (source, a, b, n) in enumerate(spans)
            if first <= i < last
        ]

    def out_copy(j):
        return pltpu.make_async_copy(outs[j], out_all.at[j], sems.at[j])

    @pl.when(step == 0)
    def _():
        for j in range(4):
            out_copy(j).start()
        for j in order:
            if j < 2:
                for copy in copies(j):
                    copy.start()
            else:

                @pl.when(ids[2] == 0)
                def _(j=j):
                    for copy in copies(j):
                        copy.start()

                @pl.when(ids[2] != 0)
                def _(j=j):
                    for copy in copies(j, True):
                        copy.start()

        for j in range(4):
            out_copy(j).wait()
        branch = vectors[2:3, :]
        for j in range(4):
            branch = branch + rows_inner(features[j][...], out_all[j, :width, :])
        value = tokens[...].astype(F32) + branch
        hidden[...] = value
        normed, inverse = normed_parts(value)
        scale[...] = inverse
        hat[...] = normed
        second_in[...] = (normed * vectors[3:4, :] + vectors[4:5, :]).astype(BF)
        feed[...] = jnp.zeros_like(feed)
        second_grad[...] = jnp.zeros_like(second_grad)

    for slot, j in enumerate(order):

        @pl.when(step == slot)
        def _(j=j):
            for copy in copies(j):
                copy.wait()

    bias = jnp.zeros((1, model), F32)
    for slot, j in enumerate(order):
        lines = out_all[j, width : width + 16, :].astype(F32)
        bias = jnp.where(step == slot, lines[0:1] + lines[1:2], bias)
    up, down = up_all[step], down_all[step]
    pre = matmul(second_in[...], up) + bias
    slope = 0.7978845608028654
    square = pre * pre
    bend = jnp.tanh(slope * pre * (1.0 + 0.044715 * square))
    act = (0.5 * pre * (1.0 + bend)).astype(BF)
    derivative = 0.5 * (1.0 + bend) + 0.5 * pre * (1.0 - bend * bend) * slope * (
        1.0 + 3 * 0.044715 * square
    )
    feed[...] += matmul(act, down)
    pre_grad = near_far(upstream[...], down) * derivative
    pre_low = pre_grad.astype(BF)
    up_biases[0] = column_sums(pre_low.astype(F32))
    second_grad[...] += near_far(pre_low, up)
    up_grad = rows_inner(second_in[...], pre_low).astype(BF)
    down_grad = rows_inner(act, upstream[...]).astype(BF)

    staged[step, :model] = up_grad
    staged[step, model:] = down_grad
    for slot in range(4):

        @pl.when(step == slot)
        def _(slot=slot):
            for copy in leaving(slot, 0, 3):
                copy.start()

    @pl.when(step == 3)
    def _():
        output[...] = (hidden[...] + feed[...] + vectors[5:6, :]).astype(BF)
        grad = second_grad[...]
        normed = hat[...]
        upstream_f = upstream[...].astype(F32)
        back = upstream_f + norm_back(grad, normed, scale[...], vectors[3:4, :])
        hidden_grad[...] = back
        low = back.astype(BF)
        for j in range(4):
            mixed_grads[j][...] = near_far(out_all[j, :width, :], low).astype(BF)
            slot = order.index(j)
            staged_out[slot] = matmul(features[j][...], low).astype(BF)
            for copy in leaving(slot, 3, 5):
                copy.start()
        sums[...] = jnp.concatenate(
            [column_sums(a) for a in (grad * normed, grad, back, upstream_f)], axis=0
        )
        for slot in range(4):
            for copy in leaving(slot):
                copy.wait()


def feed_forward(ids, vectors, tokens, upstream, features, outs, ups, downs):
    width, quarter = features[0].shape
    model = tokens.shape[1]
    order = (1, 3, 0, 2)
    flat = lambda a: pl.BlockSpec(a.shape, lambda j, *_: (0,) * len(a.shape))
    mine = pl.BlockSpec(
        (quarter, model), lambda j, ids: (ids[0], 0), pipeline_mode=pl.Buffered(1)
    )
    shape = jax.ShapeDtypeStruct
    out_shape = [shape((width, quarter), BF)] * 4 + [
        shape((quarter, model), BF),
        shape((quarter, model), F32),
        shape((2, 2 * model + width, model), BF),
        shape((2, 2 * model + width, model), BF),
        shape((4, model), F32),
        shape((4, 1, model), F32),
    ]
    out_specs = [flat(a) for a in out_shape]
    out_specs[6] = out_specs[7] = ANYWHERE
    out_specs[9] = pl.BlockSpec((1, 1, model), lambda j, *_: (j, 0, 0))
    return pl.pallas_call(
        functools.partial(feed_forward_kernel, order),
        grid_spec=pltpu.PrefetchScalarGridSpec(
            num_scalar_prefetch=1,
            grid=(4,),
            in_specs=[whole(vectors), mine, mine]
            + [whole(a) for a in features]
            + [ANYWHERE] * 12,
            out_specs=out_specs,
            scratch_shapes=[
                pltpu.VMEM((4, width + 16, model), BF),
                pltpu.VMEM((4, model, model), BF),
                pltpu.VMEM((4, model, model), BF),
                pltpu.VMEM((quarter, model), F32),
                pltpu.VMEM((quarter, model), F32),
                pltpu.VMEM((quarter, 1), F32),
                pltpu.VMEM((quarter, model), BF),
                pltpu.VMEM((quarter, model), F32),
                pltpu.VMEM((quarter, model), F32),
                pltpu.VMEM((4, 2 * model, model), BF),
                pltpu.VMEM((4, width, model), BF),
                pltpu.SemaphoreType.DMA((12,)),
                pltpu.SemaphoreType.DMA((4, 5)),
            ],
        ),
        out_shape=out_shape,
        compiler_params=vmem(56),
        cost_estimate=taking(30),
        name="feed_forward",
    )(ids, vectors, tokens, upstream, *features, *outs, *ups, *downs)


def push_kernel(spread, wk, wv, *refs):
    kept, sent = refs[-2:]
    step = pl.program_id(0)
    part = near_far(spread[:, :WIDE], wk[...]) + near_far(spread[:, WIDE:], wv[...])
    if len(refs) > 2:
        part = part + near_far(refs[0][...], refs[1][...])
    part = part.astype(BF)

    @pl.when(step < 2)
    def _():
        sent[0] = part

    @pl.when(step >= 2)
    def _():
        kept[0] = part


def push(spread, weights, k, quarter, query_grad=None, after=()):
    wk, wv, wq = weights
    model = wk.shape[0]
    quarter_of = lambda j: 2 * j + 1 - jnp.where(j >= 2, 5, 0)
    operands = [spread, wk, wv]
    in_specs = [
        pl.BlockSpec((quarter, 2 * WIDE), lambda j: (4 * k + quarter_of(j), 0)),
        whole(wk),
        whole(wv),
    ]
    if query_grad is not None:
        operands += [query_grad, wq]
        in_specs += [pl.BlockSpec((quarter, WIDE), lambda j: (quarter_of(j), 0)), whole(wq)]
    return pl.pallas_call(
        ordered_after(push_kernel, len(operands), len(after)),
        grid=(4,),
        in_specs=in_specs + [ANYWHERE] * len(after),
        out_specs=[
            pl.BlockSpec((1, quarter, model), lambda j: (jnp.maximum(j - 2, 0), 0, 0)),
            pl.BlockSpec((1, quarter, model), lambda j: (jnp.minimum(j, 1), 0, 0)),
        ],
        out_shape=[jax.ShapeDtypeStruct((2, quarter, model), BF)] * 2,
        compiler_params=vmem(24),
        cost_estimate=taking(0.01),
        name="push",
    )(*operands, *after)


def finish_kernel(
    ids, vectors, tokens, arrived, mine, hidden_grad, sums, up_biases, totals, input_part, small
):
    first_grad = arrived[...].astype(F32) + mine[...].astype(F32)
    hat, scale = normed_parts(tokens[...].astype(F32))
    back = hidden_grad[...] + norm_back(first_grad, hat, scale, vectors[0:1, :])
    input_part[...] = back.astype(BF)
    small[...] = jnp.zeros_like(small)
    small[0:4, :] = sums[...]
    for slot, j in enumerate((1, 3, 0, 2)):
        small[pl.ds(4 + jnp.bitwise_xor(ids[0], j), 1), :] = up_biases[slot]
    small[pl.ds(8 + ids[0], 1), :] = totals[...]
    small[12:13, :] = column_sums(first_grad * hat)
    small[13:14, :] = column_sums(first_grad)


def finish(ids, vectors, tokens, arrived, mine, hidden_grad, sums, up_biases, totals, after):
    quarter, model = mine.shape
    operands = [arrived, mine, hidden_grad, sums, up_biases, totals]
    return pl.pallas_call(
        ordered_after(finish_kernel, 3 + len(operands), len(after)),
        grid_spec=pltpu.PrefetchScalarGridSpec(
            num_scalar_prefetch=1,
            grid=(1,),
            in_specs=[
                whole(vectors),
                pl.BlockSpec((quarter, model), lambda j, ids: (ids[0], 0)),
            ]
            + [whole(a) for a in operands]
            + [ANYWHERE] * len(after),
            out_specs=[
                pl.BlockSpec((quarter, model), lambda j, *_: (0, 0)),
                pl.BlockSpec((16, model), lambda j, *_: (0, 0)),
            ],
        ),
        out_shape=[
            jax.ShapeDtypeStruct((quarter, model), BF),
            jax.ShapeDtypeStruct((16, model), F32),
        ],
        compiler_params=vmem(32),
        cost_estimate=taking(0.01),
        name="finish",
    )(ids, vectors, tokens, *operands, *after)


def ordered_kernel(ids, *refs):
    *parts, out = refs
    for j, part in enumerate(parts):

        @pl.when(pl.program_id(0) == j)
        def _(part=part):
            out[...] = part[...].astype(out.dtype)


def ordered(ids, which, parts, kind):
    size, model = parts[0].shape
    count = len(parts)
    return pl.pallas_call(
        ordered_kernel,
        grid_spec=pltpu.PrefetchScalarGridSpec(
            num_scalar_prefetch=1,
            grid=(count,),
            in_specs=[whole(a) for a in parts],
            out_specs=pl.BlockSpec(
                (size, model), lambda j, ids: (jnp.bitwise_xor(ids[which], j), 0)
            ),
        ),
        out_shape=jax.ShapeDtypeStruct((count * size, model), kind),
        compiler_params=vmem(24),
        cost_estimate=taking(0.01),
        name="ordered",
    )(ids, *parts)


def combine_kernel(ids, first, kept, given, own_a, far_a, stay_b, leave_b):
    step, side = pl.program_id(0), ids[2]
    total = (kept[...].astype(F32) + given[...].astype(F32)).astype(BF)

    @pl.when(step < first)
    def _():
        own_a[...] = total[0]
        far_a[...] = total[1]

    @pl.when((step >= first) & (lax.div(step - first, 2) == side))
    def _():
        stay_b[...] = total

    @pl.when((step >= first) & (lax.div(step - first, 2) != side))
    def _():
        leave_b[...] = total


def combine(ids, kept, given, part):
    _, rows, model = kept.shape
    block = (rows - part) // 4
    first = part // block
    both = pl.BlockSpec((2, block, model), lambda i, ids: (0, i, 0))
    a_rows = pl.BlockSpec((block, model), lambda i, ids: (jnp.minimum(i, first - 1), 0))
    b_rows = lambda turn: pl.BlockSpec(
        (2, block, model),
        lambda i, ids: (
            0,
            jnp.clip(i - first - 2 * jnp.where(turn, 1 - ids[2], ids[2]), 0, 1),
            0,
        ),
    )
    shape = jax.ShapeDtypeStruct
    return pl.pallas_call(
        lambda ids, *refs: combine_kernel(ids, first, *refs),
        grid_spec=pltpu.PrefetchScalarGridSpec(
            num_scalar_prefetch=1,
            grid=(rows // block,),
            in_specs=[both, both],
            out_specs=[a_rows, a_rows, b_rows(False), b_rows(True)],
        ),
        out_shape=[shape((part, model), BF)] * 2 + [shape((2, 2 * block, model), BF)] * 2,
        compiler_params=vmem(24),
        cost_estimate=taking(6),
        name="combine",
    )(ids, kept, given)


def weight_sums_kernel(ids, first_in, spread, query_grad, stay, leave, held, held_query):
    step = pl.program_id(0)
    steps = pl.num_programs(0)
    turned = first_in[...].T
    rows = matmul(turned, spread[...])

    @pl.when(step == 0)
    def _():
        held[...] = rows
        held_query[...] = matmul(turned, query_grad[...])

    @pl.when(step > 0)
    def _():
        held[...] += rows

    @pl.when((step > 0) & (step < steps // 4))
    def _():
        held_query[...] += matmul(turned, query_grad[...])

    @pl.when(step == steps - 1)
    def _():
        half = stay.shape[0]
        width = (stay.shape[1] - WIDE) // 2
        for part in range(2):
            at = pl.ds(part * half, half)
            result = jnp.concatenate(
                [
                    held[at, :WIDE],
                    held[at, WIDE : WIDE + width],
                    held_query[at, :width],
                ],
                axis=1,
            ).astype(BF)

            @pl.when(ids[2] == part)
            def _(result=result):
                stay[...] = result

            @pl.when(ids[2] != part)
            def _(result=result):
                leave[...] = result


def weight_sums(ids, first_in, spread, query_grad, width, after):
    total, model = first_in.shape
    block = query_grad.shape[0] // 2
    shape = jax.ShapeDtypeStruct((model // 2, WIDE + 2 * width), BF)
    flat = pl.BlockSpec(shape.shape, lambda i, ids: (0, 0))
    return pl.pallas_call(
        ordered_after(weight_sums_kernel, 4, len(after)),
        grid_spec=pltpu.PrefetchScalarGridSpec(
            num_scalar_prefetch=1,
            grid=(total // block,),
            in_specs=[
                pl.BlockSpec((block, model), lambda i, ids: (i, 0)),
                pl.BlockSpec((block, 2 * WIDE), lambda i, ids: (i, 0)),
                pl.BlockSpec((block, WIDE), lambda i, ids: (jnp.minimum(i, 1), 0)),
            ]
            + [ANYWHERE] * len(after),
            out_specs=[flat, flat],
            scratch_shapes=[pltpu.VMEM((model, 2 * WIDE), F32), pltpu.VMEM((model, WIDE), F32)],
        ),
        out_shape=[shape, shape],
        compiler_params=vmem(32),
        cost_estimate=taking(0.01),
        name="weight_sums",
    )(ids, first_in, spread, query_grad, *after)


def first_sums_kernel(ids, own_a, came_a, stay_b, came_b, stay, away, keep, send):
    half = stay.shape[0]
    keep[...] = (stay_b[0].astype(F32) + came_b[0].astype(F32)).astype(BF)
    send[...] = (stay_b[1].astype(F32) + came_b[1].astype(F32)).astype(BF)
    for part in range(2):
        rows = pl.ds(part * half, half)
        total = (own_a[rows, :].astype(F32) + came_a[rows, :].astype(F32)).astype(BF)

        @pl.when(ids[2] == part)
        def _(total=total):
            stay[...] = total

        @pl.when(ids[2] != part)
        def _(total=total):
            away[...] = total


def first_sums(ids, own_a, came_a, stay_b, came_b):
    part, model = own_a.shape
    operands = [own_a, came_a, stay_b, came_b]
    shape = jax.ShapeDtypeStruct
    out_shape = [shape((part // 2, model), BF)] * 2 + [shape(stay_b.shape[1:], BF)] * 2
    return pl.pallas_call(
        first_sums_kernel,
        grid_spec=pltpu.PrefetchScalarGridSpec(
            num_scalar_prefetch=1,
            grid=(1,),
            in_specs=[whole(a) for a in operands],
            out_specs=[pl.BlockSpec(a.shape, lambda *_: (0, 0)) for a in out_shape],
        ),
        out_shape=out_shape,
        compiler_params=vmem(32),
        cost_estimate=taking(0.01),
        name="first_sums",
    )(ids, *operands)


def dense_kernel(ids, mine, theirs, up, down, out):
    half, out_half = up.shape[0], out.shape[0]
    for j, part in enumerate((mine, theirs)):

        @pl.when(pl.program_id(0) == j)
        def _(part=part):
            up[...] = part[:half, :].astype(F32)
            out[...] = part[half : half + out_half, :].astype(F32)
            down[...] = part[half + out_half :, :].astype(F32)


def dense_results(ids, mine, theirs, width):
    rows, model = mine.shape
    place = lambda size: pl.BlockSpec(
        (size, model), lambda j, ids: (jnp.bitwise_xor(ids[2], j), 0)
    )
    shape = jax.ShapeDtypeStruct
    return pl.pallas_call(
        dense_kernel,
        grid_spec=pltpu.PrefetchScalarGridSpec(
            num_scalar_prefetch=1,
            grid=(2,),
            in_specs=[whole(mine), whole(theirs)],
            out_specs=[place(model // 2), place(model // 2), place(width // 2)],
        ),
        out_shape=[shape((model, model), F32)] * 2 + [shape((width, model), F32)],
        compiler_params=vmem(32),
        cost_estimate=taking(0.01),
        name="dense_results",
    )(ids, mine, theirs)


def held_until(array, after):
    return pl.pallas_call(
        lambda *refs: None,
        in_specs=[ANYWHERE] * (1 + len(after)),
        out_specs=ANYWHERE,
        out_shape=jax.ShapeDtypeStruct(array.shape, array.dtype),
        input_output_aliases={0: 0},
        name="held",
    )(array, *after)


def swap(array, flip, axis="mp"):
    return lax.ppermute(array, axis, [(i, i ^ flip) for i in range(lax.axis_size(axis))])


def upward(array, ranks):
    return lax.ppermute(array, "seq", [(i, i + 1) for i in range(ranks - 1)])


def downward(array, ranks):
    return lax.ppermute(array, "seq", [(i + 1, i) for i in range(ranks - 1)])


def spread_over_mp(part):
    across = swap(part, 2)
    return [part, swap(part, 1), across, swap(across, 1)]


def body_resident(
    inputs,
    selection,
    gain1,
    shift1,
    w_qkv,
    b_qv,
    w_score,
    b_score,
    w_out,
    b_out,
    gain2,
    shift2,
    w_up,
    b_up,
    w_down,
    b_down,
    cotangent,
):
    ranks = lax.axis_size("seq")
    me, rank, side = lax.axis_index("mp"), lax.axis_index("seq"), lax.axis_index("dp")
    ids = jnp.stack([me, rank, side]).astype(jnp.int32)
    rows, model = inputs.shape[1:]
    quarter = rows // 4
    block = quarter // 2
    total = ranks * rows
    blocks = rows // KB
    width = w_qkv.shape[2]
    heads = width // HD

    own = lax.dynamic_slice_in_dim(inputs[0], me * quarter, quarter, 0)
    arriving = {}
    for h in range(2):
        part = own[h * block : (h + 1) * block]
        for k in range(1, ranks):
            part = upward(part, ranks)
            arriving[k, h] = part
    gathered = {}
    for k in range(1, ranks):
        for halves in ((0, 1),) if k < ranks - 1 else ((0,), (1,)):
            mine = jnp.concatenate([arriving[k, h] for h in halves], axis=0)
            mine = jnp.concatenate([mine, swap(mine, 2)], axis=0)
            gathered[k, halves] = [mine, swap(mine, 1)]

    b_high = b_up.astype(BF)
    b_low = (b_up - b_high.astype(F32)).astype(BF)
    out_rows = jnp.concatenate(
        [w_out, b_high[None], b_low[None], jnp.zeros((14, model), BF)], axis=0
    )
    w_outs = spread_over_mp(out_rows)
    first = swap(jnp.where(side == 0, w_up, w_down), 2)
    second = swap(first, 1, "dp")
    w_ups = [w_up, swap(w_up, 1), first, swap(first, 1)]
    w_downs = [w_down, swap(w_down, 1), second, swap(second, 1)]

    vectors = jnp.stack([gain1, shift1, b_out, gain2, shift2, b_down] + [gain1] * 2, axis=0)
    lines = jnp.pad(
        jnp.stack([jnp.pad(b_score, (width, WIDE - width - heads))[:width], b_qv[1], b_qv[0]]),
        ((0, 5), (0, WIDE - width)),
    )
    lines = lax.dynamic_update_slice(lines, b_score[None], (0, width))
    wide = lambda a: jnp.pad(a, ((0, 0), (0, WIDE - a.shape[1])))
    wq, wv = wide(w_qkv[:, 0]), wide(w_qkv[:, 2])
    wk = wide(jnp.concatenate([w_qkv[:, 1], w_score], axis=1))

    *buffers, qt = project_own(
        ids, inputs[0], vectors, lines, (wk, wv, wq), width, total, block, [arriving[ranks - 1, h] for h in range(2)]
    )
    for (k, halves), arrays in gathered.items():
        count = len(halves)
        buffers = project(
            arrays,
            [(j % 2, (j // 2 * count + i) * block) for j in range(4) for i in range(count)],
            block,
            width,
            lambda j, k=k, h=halves[0], count=count: 8 * k + (2 // count) * j + h,
            vectors,
            lines,
            (wk, wv),
            buffers,
            [(first, second)[k - 1]] if k < ranks - 1 else (),
        )
    first_in, ka, va = buffers

    chosen = selection[0]
    *mixed, norm = attend(ids, chosen, ka, va, qt, blocks)

    features = [mixed[0]] + [swap(mixed[j], j) for j in (1, 2, 3)]
    *mixed_grads, output, hidden_grad, kept, sent, sums, up_biases = feed_forward(
        ids, vectors, inputs[0], cotangent[0], features, w_outs, w_ups, w_downs
    )
    returned = [mixed_grads[0]] + [swap(mixed_grads[j], j) for j in (1, 2, 3)]

    part = model + width
    own_a, far_a, stay_b, leave_b = combine(ids, kept, swap(sent, 1), part)
    came_a, came_b = swap(far_a, 2), swap(leave_b, 1, "dp")

    weights = (wk, wv, wq)
    spread, query_grad, totals = attend_back(
        ids, chosen, ka, va, qt, norm, returned, blocks, (far_a, leave_b)
    )

    weights = (wk, wv, wq)
    stay_a, away_a, keep_b, send_b = first_sums(ids, own_a, came_a, stay_b, came_b)
    kept_3, sent_3 = push(spread, weights, 3, quarter, None, (away_a,))
    came_a, came_b, arrived_3 = swap(away_a, 1, "dp"), swap(send_b, 2), swap(sent_3, 1)
    qkv, qkv_leave = weight_sums(ids, first_in, spread, query_grad, width, (sent_3,))
    kept_2, sent_2 = push(spread, weights, 2, quarter, None, (qkv_leave,))
    dense = jnp.concatenate([stay_a + came_a, keep_b + came_b], axis=0)
    across = held_until(kept_3[1] + arrived_3[1], (dense, sent_2))
    dense = lax.psum(dense, "seq")
    sent_2, qkv_leave = held_until(sent_2, (across,)), held_until(qkv_leave, (across,))
    crossed_3, came_qkv, arrived_2 = swap(across, 2), swap(qkv_leave, 1, "dp"), swap(sent_2, 1)
    kept_1, sent_1 = push(spread, weights, 1, quarter, None, (across,))
    kept_0, sent_0 = push(spread, weights, 0, quarter, query_grad, (sent_1,))
    qkv = qkv + came_qkv
    across = kept_2[1] + arrived_2[1]
    carried = held_until(kept_3[0] + arrived_3[0] + crossed_3, (qkv, sent_0, across))
    carried = downward(carried, ranks)
    crossed_2, arrived_1, arrived_0 = swap(across, 2), swap(sent_1, 1), swap(sent_0, 1)
    mine = kept_2[0] + arrived_2[0] + crossed_2 + carried
    across = held_until(kept_1[1] + arrived_1[1], (mine,))
    output_parts = spread_over_mp(held_until(output, (mine,)))
    carried = downward(mine, ranks)
    crossed_1 = swap(across, 2)
    mine = kept_1[0] + arrived_1[0] + crossed_1 + carried
    across = held_until(kept_0[1] + arrived_0[1], (mine,))
    dense = held_until(dense, (across,))
    qkv = lax.psum(held_until(qkv, (dense,)), "seq")
    dense_theirs = swap(dense, 1, "dp")
    carried = downward(mine, ranks)
    crossed_0 = swap(across, 2)
    mine = kept_0[0] + arrived_0[0] + crossed_0

    output = ordered(ids, 0, output_parts, BF)
    input_part, small = finish(
        ids,
        vectors,
        inputs[0],
        carried,
        mine,
        hidden_grad,
        sums,
        up_biases,
        totals,
        (output, dense_theirs),
    )
    across = swap(input_part, 2)
    input_parts = [input_part, swap(input_part, 1), across]
    input_parts.append(swap(held_until(across, (qkv,)), 1))
    for flip in (1, 2):
        small = small + swap(small, flip)
    small = small + swap(small, 1, "dp")
    qkv_sum = ordered(ids, 2, [qkv, swap(qkv, 1, "dp")], F32)
    up_grad, down_grad, out_grad = dense_results(ids, dense, dense_theirs, width)
    for flip in (1, 2):
        small = small + swap(small, flip, "seq")
    input_grad = ordered(ids, 0, input_parts, BF)
    up_bias = lax.dynamic_slice_in_dim(small, 4 + me, 1, 0)[0]
    biases = lax.dynamic_slice_in_dim(small, 8 + me, 1, 0)[0]
    query_at, value_at = WIDE + width, WIDE
    qkv_grad = jnp.stack(
        [qkv_sum[:, query_at:], qkv_sum[:, :width], qkv_sum[:, value_at:query_at]], axis=1
    )
    qv_bias_grad = jnp.stack(
        [biases[2 * WIDE : 2 * WIDE + width], biases[WIDE : WIDE + width]], axis=0
    )
    return (
        output[None],
        input_grad[None],
        small[12],
        small[13],
        qkv_grad,
        qv_bias_grad,
        qkv_sum[:, width : width + heads],
        biases[width : width + heads],
        out_grad,
        small[2],
        small[0],
        small[1],
        up_grad,
        up_bias,
        down_grad,
        small[3],
    )


RESIDENT_TOKENS = 8192


def solution(mesh):
    def body(*args):
        tokens = args[0].shape[1] * mesh.shape["seq"]
        resident = mesh.shape["mp"] == 4 and mesh.shape["dp"] == 2
        resident = resident and mesh.shape["seq"] == 4 and tokens <= RESIDENT_TOKENS
        return (body_resident if resident else body_general)(*args)

    return jax.shard_map(
        body,
        mesh=mesh,
        in_specs=(
            P("dp", "seq", None),
            P("dp", "seq", None),
            P(),
            P(),
            P(None, None, "mp"),
            P(None, "mp"),
            P(None, "mp"),
            P("mp"),
            P("mp", None),
            P(),
            P(),
            P(),
            P(None, "mp"),
            P("mp"),
            P("mp", None),
            P(),
            P("dp", "seq", None),
        ),
        out_specs=(
            P("dp", "seq", None),
            P("dp", "seq", None),
            P(),
            P(),
            P(None, None, "mp"),
            P(None, "mp"),
            P(None, "mp"),
            P("mp"),
            P("mp", None),
            P(),
            P(),
            P(),
            P(None, "mp"),
            P("mp"),
            P("mp", None),
            P(),
        ),
        check_vma=False,
    )
```

```python
import functools

import jax
import jax.numpy as jnp
from jax import lax
from jax.experimental import pallas as pl
from jax.experimental.pallas import tpu as pltpu
from jax.sharding import PartitionSpec as P

HD = 64
KB = 128
WINDOW = 64


EPSILON = 1e-05
NEGATIVE = -1e30
HIGHEST = lax.Precision.HIGHEST


def layer_norm(value, gain, shift):
    center = jnp.mean(value, axis=-1, keepdims=True)
    centered = value - center
    spread = jnp.mean(centered * centered, axis=-1, keepdims=True)
    return centered * lax.rsqrt(spread + EPSILON) * gain + shift


def gelu_tanh(value):
    return jax.nn.gelu(value, approximate=True)


def rows_inner(left, right):
    return lax.dot_general(
        left, right, (((0,), (0,)), ((), ())), preferred_element_type=jnp.float32
    )


def cols_inner(left, right):
    return lax.dot_general(
        left, right, (((1,), (1,)), ((), ())), preferred_element_type=jnp.float32
    )


def block_masks(block_ids, picked_raw):
    offsets = jnp.arange(KB, dtype=jnp.int32)
    query_pos = block_ids[:, None] * KB + offsets
    key_pos = jnp.maximum(picked_raw, 0)[:, :, None] * KB + offsets
    slot_ids = jnp.arange(picked_raw.shape[1], dtype=jnp.int32)[None, None, :, None]
    query_at = query_pos[:, :, None, None]
    key_at = key_pos[:, None]
    window_mask = (
        (key_at <= query_at)
        & (key_at > query_at - WINDOW)
        & (slot_ids < 2)
        & (picked_raw >= 0)[:, None, :, None]
    )
    chosen_mask = (key_at <= query_at - WINDOW) & (slot_ids >= 2)
    return (window_mask, chosen_mask)


def block_scores(query_blocks, key_cand, mark_cand, window_mask, chosen_mask):
    logits = jnp.einsum(
        "gihd,gcjhd->ghicj", query_blocks, key_cand, preferred_element_type=jnp.float32
    ) * HD ** (-0.5)
    mark_term = mark_cand.astype(jnp.float32).transpose(0, 3, 1, 2)[:, :, None]
    return jnp.where(
        window_mask[:, None], logits, jnp.where(chosen_mask[:, None], logits + mark_term, NEGATIVE)
    )


def body_general(
    inputs,
    selection,
    gain1,
    shift1,
    w_qkv,
    b_qv,
    w_score,
    b_score,
    w_out,
    b_out,
    gain2,
    shift2,
    w_up,
    b_up,
    w_down,
    b_down,
    cotangent,
):
    seq_rank = lax.axis_index("seq")
    tokens = inputs[0].astype(jnp.float32)
    row_count = tokens.shape[0]
    local_blocks = row_count // KB
    local_width = w_qkv.shape[2]
    local_heads = local_width // HD
    scale = HD ** (-0.5)
    normed1, pull_norm1 = jax.vjp(layer_norm, tokens, gain1, shift1)
    first_in = normed1.astype(jnp.bfloat16)
    projected = jnp.einsum("td,dsk->tsk", first_in, w_qkv, preferred_element_type=jnp.float32)
    query_rows = (projected[:, 0] + b_qv[0]).astype(jnp.bfloat16)
    key_rows = projected[:, 1].astype(jnp.bfloat16)
    value_rows = (projected[:, 2] + b_qv[1]).astype(jnp.bfloat16)
    rating = jnp.dot(first_in, w_score, preferred_element_type=jnp.float32) + b_score
    marks = jax.nn.log_sigmoid(rating).astype(jnp.bfloat16)
    all_keys, all_values, all_marks = (
        lax.all_gather(key_rows, "seq", axis=0, tiled=True),
        lax.all_gather(value_rows, "seq", axis=0, tiled=True),
        lax.all_gather(marks, "seq", axis=0, tiled=True),
    )
    total_blocks = all_keys.shape[0] // KB
    key_blocks = all_keys.reshape(total_blocks, KB, local_heads, HD)
    value_blocks = all_values.reshape(total_blocks, KB, local_heads, HD)
    mark_blocks = all_marks.reshape(total_blocks, KB, local_heads)
    block_ids = seq_rank * local_blocks + jnp.arange(local_blocks, dtype=jnp.int32)
    picked_raw = jnp.concatenate([block_ids[:, None] - 1, block_ids[:, None], selection[0]], axis=1)
    picked = jnp.maximum(picked_raw, 0)
    key_cand = jnp.take(key_blocks, picked, axis=0)
    value_cand = jnp.take(value_blocks, picked, axis=0)
    mark_cand = jnp.take(mark_blocks, picked, axis=0)
    window_mask, chosen_mask = block_masks(block_ids, picked_raw)
    query_blocks = query_rows.reshape(local_blocks, KB, local_heads, HD)
    scores = block_scores(query_blocks, key_cand, mark_cand, window_mask, chosen_mask)
    highest = jnp.max(scores, axis=(3, 4), keepdims=True)
    exponent = jnp.exp(scores - highest)
    summed = jnp.sum(exponent, axis=(3, 4), keepdims=True)
    weights = exponent / summed
    log_norm = highest + jnp.log(summed)
    attended = jnp.einsum(
        "ghicj,gcjhd->gihd",
        weights.astype(jnp.bfloat16),
        value_cand,
        preferred_element_type=jnp.float32,
    )
    mixed = attended.reshape(row_count, local_width).astype(jnp.bfloat16)
    branch = lax.psum(jnp.dot(mixed, w_out, preferred_element_type=jnp.float32), "mp")
    hidden = tokens + branch + b_out
    normed2, pull_norm2 = jax.vjp(layer_norm, hidden, gain2, shift2)
    second_in = normed2.astype(jnp.bfloat16)
    pre = jnp.dot(second_in, w_up, preferred_element_type=jnp.float32) + b_up
    activated, pull_gelu = jax.vjp(gelu_tanh, pre)
    act_low = activated.astype(jnp.bfloat16)
    feed = lax.psum(
        jnp.dot(act_low, w_down, preferred_element_type=jnp.float32).astype(jnp.bfloat16), "mp"
    ).astype(jnp.float32)
    output = (hidden + feed + b_down).astype(jnp.bfloat16)
    upstream = cotangent[0]
    upstream_f = upstream.astype(jnp.float32)
    down_grad = rows_inner(act_low, upstream)
    down_bias_grad = jnp.sum(upstream_f, axis=0)
    act_grad = cols_inner(upstream, w_down)
    pre_grad = pull_gelu(act_grad)[0].astype(jnp.bfloat16)
    up_grad = rows_inner(second_in, pre_grad)
    up_bias_grad = jnp.sum(pre_grad.astype(jnp.float32), axis=0)
    second_grad = lax.psum(cols_inner(pre_grad, w_up), "mp")
    hidden_back, gain2_grad, shift2_grad = pull_norm2(second_grad)
    hidden_grad = upstream_f + hidden_back
    out_bias_grad = jnp.sum(hidden_grad, axis=0)
    branch_grad = hidden_grad.astype(jnp.bfloat16)
    out_grad = rows_inner(mixed, branch_grad)
    mixed_grad = cols_inner(branch_grad, w_out).astype(jnp.bfloat16)
    grad_blocks = mixed_grad.reshape(local_blocks, KB, local_heads, HD)
    again = block_scores(query_blocks, key_cand, mark_cand, window_mask, chosen_mask)
    prob_again = jnp.exp(again - log_norm)
    grad_prob = jnp.einsum(
        "gihd,gcjhd->ghicj", grad_blocks, value_cand, preferred_element_type=jnp.float32
    )
    delta = jnp.sum(prob_again * grad_prob, axis=(3, 4), keepdims=True)
    score_full = prob_again * (grad_prob - delta)
    score_low = score_full.astype(jnp.bfloat16)
    query_grad = (
        (
            jnp.einsum("ghicj,gcjhd->gihd", score_low, key_cand, preferred_element_type=jnp.float32)
            * scale
        )
        .reshape(row_count, local_width)
        .astype(jnp.bfloat16)
    )
    prob_low = prob_again.astype(jnp.bfloat16)
    key_part = (
        jnp.einsum("ghicj,gihd->gcjhd", score_low, query_blocks, preferred_element_type=jnp.float32)
        * scale
    )
    value_part = jnp.einsum(
        "ghicj,gihd->gcjhd", prob_low, grad_blocks, preferred_element_type=jnp.float32
    )
    mark_part = jnp.sum(jnp.where(chosen_mask[:, None], score_full, 0.0), axis=2).transpose(
        0, 2, 3, 1
    )
    key_spread = (
        jnp.zeros((total_blocks, KB, local_heads, HD), jnp.float32).at[picked].add(key_part)
    )
    value_spread = (
        jnp.zeros((total_blocks, KB, local_heads, HD), jnp.float32).at[picked].add(value_part)
    )
    mark_spread = jnp.zeros((total_blocks, KB, local_heads), jnp.float32).at[picked].add(mark_part)
    key_total, value_total, mark_total = (
        lax.psum_scatter(
            key_spread.reshape(total_blocks * KB, local_width),
            "seq",
            scatter_dimension=0,
            tiled=True,
        ),
        lax.psum_scatter(
            value_spread.reshape(total_blocks * KB, local_width),
            "seq",
            scatter_dimension=0,
            tiled=True,
        ),
        lax.psum_scatter(
            mark_spread.reshape(total_blocks * KB, local_heads),
            "seq",
            scatter_dimension=0,
            tiled=True,
        ),
    )
    key_grad = key_total.astype(jnp.bfloat16)
    value_grad = value_total.astype(jnp.bfloat16)
    rating_grad = mark_total * jax.nn.sigmoid(-rating)
    score_grad = lax.dot_general(
        first_in.astype(jnp.float32),
        rating_grad,
        (((0,), (0,)), ((), ())),
        precision=HIGHEST,
        preferred_element_type=jnp.float32,
    )
    score_bias_grad = jnp.sum(rating_grad, axis=0)
    stacked = jnp.stack([query_grad, key_grad, value_grad], axis=1)
    qkv_grad = jnp.einsum("td,tsk->dsk", first_in, stacked, preferred_element_type=jnp.float32)
    qv_bias_grad = jnp.stack(
        [
            jnp.sum(query_grad.astype(jnp.float32), axis=0),
            jnp.sum(value_grad.astype(jnp.float32), axis=0),
        ],
        axis=0,
    )
    first_part = jnp.einsum("tsk,dsk->td", stacked, w_qkv, preferred_element_type=jnp.float32)
    first_part = first_part + jnp.dot(rating_grad, w_score.astype(jnp.float32).T, precision=HIGHEST)
    first_grad = lax.psum(first_part.astype(jnp.bfloat16), "mp").astype(jnp.float32)
    token_back, gain1_grad, shift1_grad = pull_norm1(first_grad)
    input_grad = (hidden_grad + token_back).astype(jnp.bfloat16)
    summed_grads = lax.psum(
        (
            gain1_grad,
            shift1_grad,
            qkv_grad,
            qv_bias_grad,
            score_grad,
            score_bias_grad,
            out_grad,
            out_bias_grad,
            gain2_grad,
            shift2_grad,
            up_grad,
            up_bias_grad,
            down_grad,
            down_bias_grad,
        ),
        ("dp", "seq"),
    )
    return (
        output[None],
        input_grad[None],
        summed_grads[0],
        summed_grads[1],
        summed_grads[2],
        summed_grads[3],
        summed_grads[4],
        summed_grads[5],
        summed_grads[6],
        summed_grads[7],
        summed_grads[8],
        summed_grads[9],
        summed_grads[10],
        summed_grads[11],
        summed_grads[12],
        summed_grads[13],
    )


WIDE = 256
BF = jnp.bfloat16
F32 = jnp.float32
ANYWHERE = pl.BlockSpec(memory_space=pl.ANY)
PAIR = 4


def matmul(left, right):
    return jnp.dot(left, right, preferred_element_type=F32)


def near_far(left, right):
    return lax.dot_general(left, right, (((1,), (1,)), ((), ())), preferred_element_type=F32)


def taking(microseconds):
    return pl.CostEstimate(
        flops=int(microseconds * 1.1e9), bytes_accessed=int(microseconds * 1e5), transcendentals=0
    )


def vmem(mebibytes):
    return pltpu.CompilerParams(vmem_limit_bytes=mebibytes * 1024 * 1024)


def ordered_after(kernel, at, count):
    return lambda *refs: kernel(*refs[:at], *refs[at + count :])


def whole(array):
    shape = array.shape
    return pl.BlockSpec(shape, lambda *_: (0,) * len(shape), pipeline_mode=pl.Buffered(1))


def normed_parts(value):
    center = jnp.mean(value, axis=-1, keepdims=True)
    centered = value - center
    spread = jnp.mean(centered * centered, axis=-1, keepdims=True)
    scale = lax.rsqrt(spread + EPSILON)
    return centered * scale, scale


def norm_back(grad, hat, scale, gain):
    g = gain * grad
    return scale * (
        g
        - jnp.mean(g, axis=-1, keepdims=True)
        - hat * jnp.mean(g * hat, axis=-1, keepdims=True)
    )


def column_sums(array):
    return jnp.sum(array, axis=0, keepdims=True)


def project_rows(width, value, vectors, lines, weights, fi, ka, va, qt):
    hat, _ = normed_parts(value.astype(F32))
    normed = (hat * vectors[0:1, :] + vectors[1:2, :]).astype(BF)
    fi[...] = normed
    half = WIDE // 2
    heads = width // HD
    keys = matmul(normed, weights[0][...]) + lines[0:1, :]
    values = matmul(normed, weights[1][...]) + lines[1:2, :]
    high = keys[:, half:]
    lane = lax.broadcasted_iota(jnp.int32, high.shape, 1) - (width - half)
    small = jnp.exp(-jnp.abs(high))
    mark = jnp.minimum(high, 0.0) - jnp.log1p(small)
    slope = jnp.where(high >= 0, small, 1.0) / (1.0 + small)
    ones = jnp.where((lane >= heads) & (lane < heads + 3), 1.0, 0.0)
    marked = (lane >= 0) & (lane < heads)
    ka[:, :half] = keys[:, :half].astype(BF)
    ka[:, half:] = jnp.where(lane < 0, high, jnp.where(marked, mark, ones)).astype(BF)
    va[:, :half] = values[:, :half].astype(BF)
    va[:, half:] = jnp.where(
        lane < 0, values[:, half:], jnp.where(marked, slope, ones)
    ).astype(BF)
    if qt is not None:
        query = (matmul(normed, weights[2][...]) + lines[2:3, :]).astype(BF).astype(F32)
        qt[...] = (query * HD ** (-0.5)).T[:width].astype(BF)


def project_own_kernel(ids, x, vectors, lines, wk, wv, wq, fi, ka, va, qt):
    del ids
    project_rows(qt.shape[0], x[...], vectors, lines, (wk, wv, wq), fi, ka, va, qt)


def project_kernel(sources, arrays, width, *refs):
    vectors, lines, wk, wv = refs[:4]
    fi, ka, va, held, sems = refs[7 + arrays :]
    step = pl.program_id(0)
    count, block = held.shape[:2]

    def copy(j):
        array, row = sources[j]
        return pltpu.make_async_copy(
            refs[4 + array].at[pl.ds(row, block), :], held.at[j], sems.at[j]
        )

    @pl.when(step == 0)
    def _():
        for j in range(count):
            copy(j).start()

    for j in range(count):

        @pl.when(step == j)
        def _(j=j):
            copy(j).wait()

    project_rows(width, held[step], vectors, lines, (wk, wv), fi, ka, va, None)


def project_shapes(total, model):
    return [
        jax.ShapeDtypeStruct((total, model), BF),
        jax.ShapeDtypeStruct((total, WIDE), BF),
        jax.ShapeDtypeStruct((total, WIDE), BF),
    ]


def project_specs(block, model, place):
    rows = lambda cols: pl.BlockSpec((block, cols), lambda j, *_: (place(j), 0))
    return [rows(model), rows(WIDE), rows(WIDE)]


def project_own(ids, x, vectors, lines, weights, width, total, block, after):
    rows, model = x.shape
    per = rows // 4 // block
    operands = [vectors, lines, *weights]
    return pl.pallas_call(
        ordered_after(project_own_kernel, 2 + len(operands), len(after)),
        grid_spec=pltpu.PrefetchScalarGridSpec(
            num_scalar_prefetch=1,
            grid=(rows // block,),
            in_specs=[
                pl.BlockSpec(
                    (block, model),
                    lambda j, ids: (
                        jnp.bitwise_xor(lax.div(j, per), ids[0]) * per + lax.rem(j, per),
                        0,
                    ),
                )
            ]
            + [whole(a) for a in operands]
            + [ANYWHERE] * len(after),
            out_specs=project_specs(block, model, lambda j: j)
            + [pl.BlockSpec((width, block), lambda j, *_: (0, j))],
        ),
        out_shape=project_shapes(total, model) + [jax.ShapeDtypeStruct((width, rows), BF)],
        compiler_params=vmem(16),
        cost_estimate=taking(8),
        name="project_own",
    )(ids, x, *operands, *after)


def project(arrays, sources, block, width, place, vectors, lines, weights, buffers, after=()):
    model = arrays[0].shape[1]
    total = buffers[0].shape[0]
    count, given = len(sources), len(arrays)
    operands = [vectors, lines, *weights]
    return pl.pallas_call(
        ordered_after(
            functools.partial(project_kernel, sources, given, width),
            len(operands) + given + 3,
            len(after),
        ),
        grid=(count,),
        in_specs=[whole(a) for a in operands] + [ANYWHERE] * (given + 3 + len(after)),
        out_specs=project_specs(block, model, place),
        out_shape=project_shapes(total, model),
        scratch_shapes=[
            pltpu.VMEM((count, block, model), BF),
            pltpu.SemaphoreType.DMA((count,)),
        ],
        input_output_aliases={len(operands) + given + i: i for i in range(3)},
        compiler_params=vmem(18),
        cost_estimate=taking(count),
        name="project",
    )(*operands, *arrays, *buffers, *after)


def head_diagonal(rows, tail):
    width = rows.shape[0]
    heads = width // HD
    columns = []
    for h in range(heads):
        parts = []
        if h > 0:
            parts.append(jnp.zeros((h * HD, KB), BF))
        parts.append(rows[h * HD : (h + 1) * HD])
        if h < heads - 1:
            parts.append(jnp.zeros(((heads - 1 - h) * HD, KB), BF))
        columns.append(jnp.concatenate(parts, axis=0))
    top = jnp.concatenate(columns, axis=1)
    rest = jnp.zeros((WIDE - width - 16, heads * KB), BF)
    return jnp.concatenate([top, tail.astype(BF), rest], axis=0)


def tail_rows(heads, marked, term):
    shape = (16, heads * KB)
    row = lax.broadcasted_iota(jnp.int32, shape, 0)
    column = lax.broadcasted_iota(jnp.int32, shape, 1) // KB
    tail = jnp.where(row == column, 1.0, 0.0) if marked else jnp.zeros(shape, F32)
    if term is not None:
        for piece in range(3):
            part = term.astype(BF).astype(F32)
            tail = jnp.where(row == heads + piece, part, tail)
            term = term - part
    return tail


def offsets_tile(heads):
    shape = (KB, heads * KB)
    key = lax.broadcasted_iota(jnp.int32, shape, 0)
    query = lax.rem(lax.broadcasted_iota(jnp.int32, shape, 1), KB)
    return key - query


def spots(ids, chosen, step, blocks):
    me, rank, per = ids[0], ids[1], blocks // 4
    natural = jnp.bitwise_xor(lax.div(step, per), me) * per + lax.rem(step, per)
    block = rank * blocks + natural
    picked = [chosen[natural, t] for t in (1, 2, 3)]
    starts = []
    for name in [jnp.maximum(block - 1, 0), block, *picked]:
        inner = lax.rem(name, blocks)
        place = (rank - lax.div(name, blocks)) * blocks + lax.rem(inner, per)
        place = place + jnp.bitwise_xor(lax.div(inner, per), me) * per
        starts.append(pl.multiple_of(place * KB, KB))
    first = jnp.where(block >= 1, KB - WINDOW, 2 * KB)
    return starts, [first] + [(block - c) * KB - WINDOW for c in picked]


def masks_of(gap, bounds):
    return [gap > bounds[0], gap <= 0] + [gap <= b for b in bounds[1:]]


def diagonal_of(full, heads):
    return jnp.concatenate(
        [full[h * HD : (h + 1) * HD, h * KB : (h + 1) * KB] for h in range(heads)], axis=0
    )


def attend_kernel(blocks, ids, chosen, ka, va, qt, *outs):
    *mixed, norm = outs
    step = pl.program_id(0)
    width = qt.shape[0]
    heads = width // HD

    def block_forward(at):
        query = qt[:, at * KB : (at + 1) * KB]
        plain = head_diagonal(query, tail_rows(heads, False, None))
        marked = head_diagonal(query, tail_rows(heads, True, None))
        starts, bounds = spots(ids, chosen, step * PAIR + at, blocks)
        tiles = [ka[pl.ds(s, KB), :] for s in starts]
        near = matmul(jnp.concatenate(tiles[:2], axis=0), plain)
        far = matmul(jnp.concatenate(tiles[1:], axis=0), marked)
        gap = offsets_tile(heads)
        scores = [near[:KB], jnp.where(gap > -WINDOW, near[KB:], far[:KB])]
        scores += [far[KB * (1 + t) : KB * (2 + t)] for t in range(3)]
        scores = [jnp.where(m, s, NEGATIVE) for m, s in zip(masks_of(gap, bounds), scores)]
        top = functools.reduce(jnp.maximum, scores)
        top = jnp.max(top, axis=0, keepdims=True)
        weights = [jnp.exp(s - top) for s in scores]
        total = jnp.sum(functools.reduce(jnp.add, weights), axis=0, keepdims=True)
        stacked = jnp.concatenate([w.astype(BF) for w in weights], axis=0)
        values = jnp.concatenate([va[pl.ds(s, KB), :] for s in starts], axis=0)
        full = rows_inner(values, stacked) / total
        return diagonal_of(full, heads).astype(BF), top + jnp.log(total)

    results = [block_forward(at) for at in range(PAIR)]
    for at, (_, line) in enumerate(results):
        norm[at] = line
    result = jnp.concatenate([value for value, _ in results], axis=1)
    for p in range(4):

        @pl.when(lax.div(step, blocks // 4 // PAIR) == p)
        def _(p=p):
            mixed[p][...] = result


def attend(ids, chosen, ka, va, qt, blocks):
    width = qt.shape[0]
    heads = width // HD
    per = blocks // 4
    turns = per // PAIR
    piece = lambda p: pl.BlockSpec(
        (width, PAIR * KB), lambda i, *_: (0, jnp.clip(i - turns * p, 0, turns - 1))
    )
    return pl.pallas_call(
        functools.partial(attend_kernel, blocks),
        grid_spec=pltpu.PrefetchScalarGridSpec(
            num_scalar_prefetch=2,
            grid=(blocks // PAIR,),
            in_specs=[
                whole(ka),
                whole(va),
                pl.BlockSpec((width, PAIR * KB), lambda i, *_: (0, i)),
            ],
            out_specs=[piece(p) for p in range(4)]
            + [pl.BlockSpec((PAIR, 1, heads * KB), lambda i, *_: (i, 0, 0))],
        ),
        out_shape=[jax.ShapeDtypeStruct((width, per * KB), BF)] * 4
        + [jax.ShapeDtypeStruct((blocks, 1, heads * KB), F32)],
        compiler_params=vmem(30),
        cost_estimate=taking(14),
        name="attend",
    )(ids, chosen, ka, va, qt)


def attend_back_kernel(
    blocks,
    ids,
    chosen,
    ka,
    va,
    qt,
    norm,
    *refs,
):
    grads = refs[:4]
    spread, query_grad, totals, key_sum, value_sum, grad_all, sems = refs[4:]
    step = pl.program_id(0)
    width = qt.shape[0]
    heads = width // HD
    per, steps = blocks // 4, blocks // PAIR

    def copy(j):
        return pltpu.make_async_copy(grads[j], grad_all.at[j], sems.at[j])

    @pl.when(step == 0)
    def _():
        for j in range(4):
            copy(j).start()
        key_sum[...] = jnp.zeros_like(key_sum)
        value_sum[...] = jnp.zeros_like(value_sum)
        totals[...] = jnp.zeros_like(totals)
        for j in range(4):
            copy(j).wait()

    def block_back(at):
        index = step * PAIR + at
        column = slice(at * KB, (at + 1) * KB)
        query = qt[:, column]
        lanes = pl.ds(pl.multiple_of(lax.rem(index, per) * KB, KB), KB)
        upstream = grad_all[lax.div(index, per), :, lanes]
        plain = head_diagonal(query, tail_rows(heads, False, -norm[at]))
        marked = head_diagonal(query, tail_rows(heads, True, -norm[at]))
        back = head_diagonal(upstream, tail_rows(heads, False, None))
        starts, bounds = spots(ids, chosen, index, blocks)
        tiles = [ka[pl.ds(s, KB), :] for s in starts]
        near = matmul(jnp.concatenate(tiles[:2], axis=0), plain)
        far = matmul(jnp.concatenate(tiles[1:], axis=0), marked)
        slopes = matmul(jnp.concatenate([va[pl.ds(s, KB), :] for s in starts], axis=0), back)
        gap = offsets_tile(heads)
        masks = masks_of(gap, bounds)
        window = gap > -WINDOW
        scores = [near[:KB], jnp.where(window, near[KB:], far[:KB])]
        scores += [far[KB * (1 + t) : KB * (2 + t)] for t in range(3)]
        probs = [jnp.where(m, jnp.exp(s), 0.0) for m, s in zip(masks, scores)]
        terms = [p * slopes[c * KB : (c + 1) * KB] for c, p in enumerate(probs)]
        delta = column_sums(functools.reduce(jnp.add, terms))
        signals = [t - p * delta for t, p in zip(terms, probs)]
        own = signals[1]
        near_signal = jnp.concatenate([signals[0], jnp.where(window, own, 0.0)], axis=0).astype(BF)
        far_exact = jnp.concatenate([jnp.where(window, 0.0, own)] + signals[2:], axis=0)
        far_signal = far_exact.astype(BF)
        signal = jnp.concatenate(signals, axis=0).astype(BF)
        prob = jnp.concatenate(probs, axis=0).astype(BF)
        near_keys = near_far(near_signal, plain)
        far_keys = near_far(far_signal, marked)
        value_parts = near_far(prob, back)
        key_parts = [near_keys[:KB], near_keys[KB:] + far_keys[:KB]]
        key_parts += [far_keys[KB * (1 + t) : KB * (2 + t)] for t in range(3)]
        value_parts = [value_parts[c * KB : (c + 1) * KB] for c in range(5)]
        rest = (far_exact - far_signal.astype(F32)).astype(BF)
        far_rest = near_far(rest, marked[WIDE // 2 :])
        far_rest = [far_rest[c * KB : (c + 1) * KB] for c in range(4)]
        keys = jnp.concatenate([tiles[0], tiles[1]] + tiles[2:], axis=0)
        full = diagonal_of(rows_inner(keys, signal), heads) * HD ** (-0.5)
        full = jnp.concatenate([full, jnp.zeros((WIDE - width, KB), F32)], axis=0).T
        return starts, key_parts, value_parts, far_rest, full

    @pl.when(step < steps)
    def _():
        results = [block_back(at) for at in range(PAIR)]
        for at, (starts, key_parts, value_parts, far_rest, full) in enumerate(results):
            for c, s in enumerate(starts):
                key_sum[pl.ds(s, KB), :] += key_parts[c]
                value_sum[pl.ds(s, KB), :] += value_parts[c]
                if c > 0:
                    key_sum[pl.ds(s, KB), WIDE // 2 :] += far_rest[c - 1]
            query_grad[at * KB : (at + 1) * KB, :] = full.astype(BF)
            totals[:, 2 * WIDE :] += column_sums(full)

    @pl.when(step >= steps)
    def _():
        rows = spread.shape[0]
        at = pl.ds(pl.multiple_of((step - steps) * rows, rows), rows)
        lane = lax.broadcasted_iota(jnp.int32, (rows, WIDE), 1)
        marks = (lane >= width) & (lane < width + heads)
        keys = jnp.where(lane < width, key_sum[at, :], 0.0)
        keys = jnp.where(marks, key_sum[at, :] * va[at, :].astype(F32), keys)
        values = jnp.where(lane < width, value_sum[at, :], 0.0)
        spread[:, :WIDE] = keys.astype(BF)
        spread[:, WIDE:] = values.astype(BF)
        totals[:, :WIDE] += column_sums(keys)
        totals[:, WIDE : 2 * WIDE] += column_sums(values)


def attend_back(ids, chosen, ka, va, qt, norm, grads, blocks, after=()):
    width = qt.shape[0]
    heads = width // HD
    total = ka.shape[0]
    rows = 8 * KB
    steps = blocks // PAIR
    last = lambda i: jnp.minimum(i, steps - 1)
    return pl.pallas_call(
        ordered_after(functools.partial(attend_back_kernel, blocks), 10, len(after)),
        grid_spec=pltpu.PrefetchScalarGridSpec(
            num_scalar_prefetch=2,
            grid=(steps + total // rows,),
            in_specs=[
                whole(ka),
                whole(va),
                pl.BlockSpec((width, PAIR * KB), lambda i, *_: (0, last(i))),
                pl.BlockSpec((PAIR, 1, heads * KB), lambda i, *_: (last(i), 0, 0)),
            ]
            + [ANYWHERE] * (4 + len(after)),
            out_specs=[
                pl.BlockSpec((rows, 2 * WIDE), lambda i, *_: (jnp.maximum(i - steps, 0), 0)),
                pl.BlockSpec((PAIR * KB, WIDE), lambda i, *_: (last(i), 0)),
                pl.BlockSpec((1, 3 * WIDE), lambda i, *_: (0, 0)),
            ],
            scratch_shapes=[
                pltpu.VMEM((total, WIDE), F32),
                pltpu.VMEM((total, WIDE), F32),
                pltpu.VMEM((4, width, blocks // 4 * KB), BF),
                pltpu.SemaphoreType.DMA((4,)),
            ],
        ),
        out_shape=[
            jax.ShapeDtypeStruct((total, 2 * WIDE), BF),
            jax.ShapeDtypeStruct((blocks * KB, WIDE), BF),
            jax.ShapeDtypeStruct((1, 3 * WIDE), F32),
        ],
        compiler_params=vmem(56),
        cost_estimate=taking(36),
        name="attend_back",
    )(ids, chosen, ka, va, qt, norm, *grads, *after)


def feed_forward_kernel(order, ids, vectors, tokens, upstream, *refs):
    features, outs, ups, downs = refs[:4], refs[4:8], refs[8:12], refs[12:16]
    mixed_grads = refs[16:20]
    output, hidden_grad, kept, sent, sums, up_biases = refs[20:26]
    out_all, up_all, down_all, hidden, hat, scale, second_in, feed, second_grad = refs[26:35]
    staged, staged_out, sems, out_sems = refs[35:]
    step = pl.program_id(0)
    width = features[0].shape[0]
    model = tokens.shape[1]

    def copies(j, turned=False):
        slot = order.index(j)
        up, down = (downs[j], ups[j]) if turned else (ups[j], downs[j])
        return [
            pltpu.make_async_copy(up, up_all.at[slot], sems.at[4 + slot]),
            pltpu.make_async_copy(down, down_all.at[slot], sems.at[8 + slot]),
        ]

    def leaving(slot, first=0, last=5):
        target = (sent if slot < 2 else kept).at[slot % 2]
        half, out_half = model // 2, width // 2
        spans = [(staged, 0, 0, half), (staged, half, half + out_half, half)]
        spans += [(staged, model, model + width, model)]
        spans += [(staged_out, 0, half, out_half), (staged_out, out_half, model + out_half, out_half)]
        return [
            pltpu.make_async_copy(
                source.at[slot, pl.ds(a, n), :], target.at[pl.ds(b, n), :], out_sems.at[slot, i]
            )
            for i, (source, a, b, n) in enumerate(spans)
            if first <= i < last
        ]

    def out_copy(j):
        return pltpu.make_async_copy(outs[j], out_all.at[j], sems.at[j])

    @pl.when(step == 0)
    def _():
        for j in range(4):
            out_copy(j).start()
        for j in order:
            if j < 2:
                for copy in copies(j):
                    copy.start()
            else:

                @pl.when(ids[2] == 0)
                def _(j=j):
                    for copy in copies(j):
                        copy.start()

                @pl.when(ids[2] != 0)
                def _(j=j):
                    for copy in copies(j, True):
                        copy.start()

        for j in range(4):
            out_copy(j).wait()
        branch = vectors[2:3, :]
        for j in range(4):
            branch = branch + rows_inner(features[j][...], out_all[j, :width, :])
        value = tokens[...].astype(F32) + branch
        hidden[...] = value
        normed, inverse = normed_parts(value)
        scale[...] = inverse
        hat[...] = normed
        second_in[...] = (normed * vectors[3:4, :] + vectors[4:5, :]).astype(BF)
        feed[...] = jnp.zeros_like(feed)
        second_grad[...] = jnp.zeros_like(second_grad)

    for slot, j in enumerate(order):

        @pl.when(step == slot)
        def _(j=j):
            for copy in copies(j):
                copy.wait()

    bias = jnp.zeros((1, model), F32)
    for slot, j in enumerate(order):
        lines = out_all[j, width : width + 16, :].astype(F32)
        bias = jnp.where(step == slot, lines[0:1] + lines[1:2], bias)
    up, down = up_all[step], down_all[step]
    pre = matmul(second_in[...], up) + bias
    slope = 0.7978845608028654
    square = pre * pre
    bend = jnp.tanh(pre * (slope + slope * 0.044715 * square))
    share = 0.5 + 0.5 * bend
    act = (pre * share).astype(BF)
    derivative = share + pre * (share - share * share) * (
        2 * slope + 6 * slope * 0.044715 * square
    )
    feed[...] += matmul(act, down)
    pre_grad = near_far(upstream[...], down) * derivative
    pre_low = pre_grad.astype(BF)
    up_biases[0] = column_sums(pre_low.astype(F32))
    second_grad[...] += near_far(pre_low, up)
    up_grad = rows_inner(second_in[...], pre_low).astype(BF)
    down_grad = rows_inner(act, upstream[...]).astype(BF)

    staged[step, :model] = up_grad
    staged[step, model:] = down_grad
    for slot in range(4):

        @pl.when(step == slot)
        def _(slot=slot):
            for copy in leaving(slot, 0, 3):
                copy.start()

    @pl.when(step == 3)
    def _():
        output[...] = (hidden[...] + feed[...] + vectors[5:6, :]).astype(BF)
        grad = second_grad[...]
        normed = hat[...]
        upstream_f = upstream[...].astype(F32)
        back = upstream_f + norm_back(grad, normed, scale[...], vectors[3:4, :])
        hidden_grad[...] = back
        low = back.astype(BF)
        for j in range(4):
            mixed_grads[j][...] = near_far(out_all[j, :width, :], low).astype(BF)
            slot = order.index(j)
            staged_out[slot] = matmul(features[j][...], low).astype(BF)
            for copy in leaving(slot, 3, 5):
                copy.start()
        sums[...] = jnp.concatenate(
            [column_sums(a) for a in (grad * normed, grad, back, upstream_f)], axis=0
        )
        for slot in range(4):
            for copy in leaving(slot):
                copy.wait()


def feed_forward(ids, vectors, tokens, upstream, features, outs, ups, downs):
    width, quarter = features[0].shape
    model = tokens.shape[1]
    order = (1, 3, 0, 2)
    flat = lambda a: pl.BlockSpec(a.shape, lambda j, *_: (0,) * len(a.shape))
    mine = pl.BlockSpec(
        (quarter, model), lambda j, ids: (ids[0], 0), pipeline_mode=pl.Buffered(1)
    )
    shape = jax.ShapeDtypeStruct
    out_shape = [shape((width, quarter), BF)] * 4 + [
        shape((quarter, model), BF),
        shape((quarter, model), F32),
        shape((2, 2 * model + width, model), BF),
        shape((2, 2 * model + width, model), BF),
        shape((4, model), F32),
        shape((4, 1, model), F32),
    ]
    out_specs = [flat(a) for a in out_shape]
    out_specs[6] = out_specs[7] = ANYWHERE
    out_specs[9] = pl.BlockSpec((1, 1, model), lambda j, *_: (j, 0, 0))
    return pl.pallas_call(
        functools.partial(feed_forward_kernel, order),
        grid_spec=pltpu.PrefetchScalarGridSpec(
            num_scalar_prefetch=1,
            grid=(4,),
            in_specs=[whole(vectors), mine, mine]
            + [whole(a) for a in features]
            + [ANYWHERE] * 12,
            out_specs=out_specs,
            scratch_shapes=[
                pltpu.VMEM((4, width + 16, model), BF),
                pltpu.VMEM((4, model, model), BF),
                pltpu.VMEM((4, model, model), BF),
                pltpu.VMEM((quarter, model), F32),
                pltpu.VMEM((quarter, model), F32),
                pltpu.VMEM((quarter, 1), F32),
                pltpu.VMEM((quarter, model), BF),
                pltpu.VMEM((quarter, model), F32),
                pltpu.VMEM((quarter, model), F32),
                pltpu.VMEM((4, 2 * model, model), BF),
                pltpu.VMEM((4, width, model), BF),
                pltpu.SemaphoreType.DMA((12,)),
                pltpu.SemaphoreType.DMA((4, 5)),
            ],
        ),
        out_shape=out_shape,
        compiler_params=vmem(48),
        cost_estimate=taking(30),
        name="feed_forward",
    )(ids, vectors, tokens, upstream, *features, *outs, *ups, *downs)


def push_kernel(spread, wk, wv, *refs):
    kept, sent = refs[-2:]
    step = pl.program_id(0)
    part = near_far(spread[:, :WIDE], wk[...]) + near_far(spread[:, WIDE:], wv[...])
    if len(refs) > 2:
        part = part + near_far(refs[0][...], refs[1][...])
    part = part.astype(BF)

    @pl.when(step < 2)
    def _():
        sent[0] = part

    @pl.when(step >= 2)
    def _():
        kept[0] = part


def push(spread, weights, k, quarter, query_grad=None, after=()):
    wk, wv, wq = weights
    model = wk.shape[0]
    quarter_of = lambda j: 2 * j + 1 - jnp.where(j >= 2, 5, 0)
    operands = [spread, wk, wv]
    in_specs = [
        pl.BlockSpec((quarter, 2 * WIDE), lambda j: (4 * k + quarter_of(j), 0)),
        whole(wk),
        whole(wv),
    ]
    if query_grad is not None:
        operands += [query_grad, wq]
        in_specs += [pl.BlockSpec((quarter, WIDE), lambda j: (quarter_of(j), 0)), whole(wq)]
    return pl.pallas_call(
        ordered_after(push_kernel, len(operands), len(after)),
        grid=(4,),
        in_specs=in_specs + [ANYWHERE] * len(after),
        out_specs=[
            pl.BlockSpec((1, quarter, model), lambda j: (jnp.maximum(j - 2, 0), 0, 0)),
            pl.BlockSpec((1, quarter, model), lambda j: (jnp.minimum(j, 1), 0, 0)),
        ],
        out_shape=[jax.ShapeDtypeStruct((2, quarter, model), BF)] * 2,
        compiler_params=vmem(14),
        cost_estimate=taking(0.01),
        name="push",
    )(*operands, *after)


def finish_kernel(
    ids, vectors, tokens, arrived, mine, hidden_grad, sums, up_biases, totals, input_part, small
):
    first_grad = arrived[...].astype(F32) + mine[...].astype(F32)
    hat, scale = normed_parts(tokens[...].astype(F32))
    back = hidden_grad[...] + norm_back(first_grad, hat, scale, vectors[0:1, :])
    input_part[...] = back.astype(BF)
    small[...] = jnp.zeros_like(small)
    small[0:4, :] = sums[...]
    for slot, j in enumerate((1, 3, 0, 2)):
        small[pl.ds(4 + jnp.bitwise_xor(ids[0], j), 1), :] = up_biases[slot]
    small[pl.ds(8 + ids[0], 1), :] = totals[...]
    small[12:13, :] = column_sums(first_grad * hat)
    small[13:14, :] = column_sums(first_grad)


def finish(ids, vectors, tokens, arrived, mine, hidden_grad, sums, up_biases, totals, after):
    quarter, model = mine.shape
    operands = [arrived, mine, hidden_grad, sums, up_biases, totals]
    return pl.pallas_call(
        ordered_after(finish_kernel, 3 + len(operands), len(after)),
        grid_spec=pltpu.PrefetchScalarGridSpec(
            num_scalar_prefetch=1,
            grid=(1,),
            in_specs=[
                whole(vectors),
                pl.BlockSpec((quarter, model), lambda j, ids: (ids[0], 0)),
            ]
            + [whole(a) for a in operands]
            + [ANYWHERE] * len(after),
            out_specs=[
                pl.BlockSpec((quarter, model), lambda j, *_: (0, 0)),
                pl.BlockSpec((16, model), lambda j, *_: (0, 0)),
            ],
        ),
        out_shape=[
            jax.ShapeDtypeStruct((quarter, model), BF),
            jax.ShapeDtypeStruct((16, model), F32),
        ],
        compiler_params=vmem(20),
        cost_estimate=taking(0.01),
        name="finish",
    )(ids, vectors, tokens, *operands, *after)


def ordered_kernel(ids, *refs):
    *parts, out = refs
    for j, part in enumerate(parts):

        @pl.when(pl.program_id(0) == j)
        def _(part=part):
            out[...] = part[...].astype(out.dtype)


def ordered(ids, which, parts, kind):
    size, model = parts[0].shape
    count = len(parts)
    return pl.pallas_call(
        ordered_kernel,
        grid_spec=pltpu.PrefetchScalarGridSpec(
            num_scalar_prefetch=1,
            grid=(count,),
            in_specs=[whole(a) for a in parts],
            out_specs=pl.BlockSpec(
                (size, model), lambda j, ids: (jnp.bitwise_xor(ids[which], j), 0)
            ),
        ),
        out_shape=jax.ShapeDtypeStruct((count * size, model), kind),
        compiler_params=vmem(10),
        cost_estimate=taking(0.01),
        name="ordered",
    )(ids, *parts)


def combine_kernel(ids, first, kept, given, own_a, far_a, stay_b, leave_b):
    step, side = pl.program_id(0), ids[2]
    total = (kept[...].astype(F32) + given[...].astype(F32)).astype(BF)

    @pl.when(step < first)
    def _():
        own_a[...] = total[0]
        far_a[...] = total[1]

    @pl.when((step >= first) & (lax.div(step - first, 2) == side))
    def _():
        stay_b[...] = total

    @pl.when((step >= first) & (lax.div(step - first, 2) != side))
    def _():
        leave_b[...] = total


def combine(ids, kept, given, part):
    _, rows, model = kept.shape
    block = (rows - part) // 4
    first = part // block
    both = pl.BlockSpec((2, block, model), lambda i, ids: (0, i, 0))
    a_rows = pl.BlockSpec((block, model), lambda i, ids: (jnp.minimum(i, first - 1), 0))
    b_rows = lambda turn: pl.BlockSpec(
        (2, block, model),
        lambda i, ids: (
            0,
            jnp.clip(i - first - 2 * jnp.where(turn, 1 - ids[2], ids[2]), 0, 1),
            0,
        ),
    )
    shape = jax.ShapeDtypeStruct
    return pl.pallas_call(
        lambda ids, *refs: combine_kernel(ids, first, *refs),
        grid_spec=pltpu.PrefetchScalarGridSpec(
            num_scalar_prefetch=1,
            grid=(rows // block,),
            in_specs=[both, both],
            out_specs=[a_rows, a_rows, b_rows(False), b_rows(True)],
        ),
        out_shape=[shape((part, model), BF)] * 2 + [shape((2, 2 * block, model), BF)] * 2,
        compiler_params=vmem(10),
        cost_estimate=taking(6),
        name="combine",
    )(ids, kept, given)


def weight_sums_kernel(ids, first_in, spread, query_grad, stay, leave, held, held_query):
    step = pl.program_id(0)
    steps = pl.num_programs(0)
    turned = first_in[...].T
    rows = matmul(turned, spread[...])

    @pl.when(step == 0)
    def _():
        held[...] = rows
        held_query[...] = matmul(turned, query_grad[...])

    @pl.when(step > 0)
    def _():
        held[...] += rows

    @pl.when((step > 0) & (step < steps // 4))
    def _():
        held_query[...] += matmul(turned, query_grad[...])

    @pl.when(step == steps - 1)
    def _():
        half = stay.shape[0]
        width = (stay.shape[1] - WIDE) // 2
        for part in range(2):
            at = pl.ds(part * half, half)
            result = jnp.concatenate(
                [
                    held[at, :WIDE],
                    held[at, WIDE : WIDE + width],
                    held_query[at, :width],
                ],
                axis=1,
            ).astype(BF)

            @pl.when(ids[2] == part)
            def _(result=result):
                stay[...] = result

            @pl.when(ids[2] != part)
            def _(result=result):
                leave[...] = result


def weight_sums(ids, first_in, spread, query_grad, width, after):
    total, model = first_in.shape
    block = query_grad.shape[0] // 2
    shape = jax.ShapeDtypeStruct((model // 2, WIDE + 2 * width), BF)
    flat = pl.BlockSpec(shape.shape, lambda i, ids: (0, 0))
    return pl.pallas_call(
        ordered_after(weight_sums_kernel, 4, len(after)),
        grid_spec=pltpu.PrefetchScalarGridSpec(
            num_scalar_prefetch=1,
            grid=(total // block,),
            in_specs=[
                pl.BlockSpec((block, model), lambda i, ids: (i, 0)),
                pl.BlockSpec((block, 2 * WIDE), lambda i, ids: (i, 0)),
                pl.BlockSpec((block, WIDE), lambda i, ids: (jnp.minimum(i, 1), 0)),
            ]
            + [ANYWHERE] * len(after),
            out_specs=[flat, flat],
            scratch_shapes=[pltpu.VMEM((model, 2 * WIDE), F32), pltpu.VMEM((model, WIDE), F32)],
        ),
        out_shape=[shape, shape],
        compiler_params=vmem(22),
        cost_estimate=taking(0.01),
        name="weight_sums",
    )(ids, first_in, spread, query_grad, *after)


def first_sums_kernel(ids, own_a, came_a, stay_b, came_b, stay, away, keep, send):
    half = stay.shape[0]
    keep[...] = (stay_b[0].astype(F32) + came_b[0].astype(F32)).astype(BF)
    send[...] = (stay_b[1].astype(F32) + came_b[1].astype(F32)).astype(BF)
    for part in range(2):
        rows = pl.ds(part * half, half)
        total = (own_a[rows, :].astype(F32) + came_a[rows, :].astype(F32)).astype(BF)

        @pl.when(ids[2] == part)
        def _(total=total):
            stay[...] = total

        @pl.when(ids[2] != part)
        def _(total=total):
            away[...] = total


def first_sums(ids, own_a, came_a, stay_b, came_b):
    part, model = own_a.shape
    operands = [own_a, came_a, stay_b, came_b]
    shape = jax.ShapeDtypeStruct
    out_shape = [shape((part // 2, model), BF)] * 2 + [shape(stay_b.shape[1:], BF)] * 2
    return pl.pallas_call(
        first_sums_kernel,
        grid_spec=pltpu.PrefetchScalarGridSpec(
            num_scalar_prefetch=1,
            grid=(1,),
            in_specs=[whole(a) for a in operands],
            out_specs=[pl.BlockSpec(a.shape, lambda *_: (0, 0)) for a in out_shape],
        ),
        out_shape=out_shape,
        compiler_params=vmem(18),
        cost_estimate=taking(0.01),
        name="first_sums",
    )(ids, *operands)


def dense_kernel(ids, mine, theirs, up, down, out):
    half, out_half = up.shape[0], out.shape[0]
    for j, part in enumerate((mine, theirs)):

        @pl.when(pl.program_id(0) == j)
        def _(part=part):
            up[...] = part[:half, :].astype(F32)
            out[...] = part[half : half + out_half, :].astype(F32)
            down[...] = part[half + out_half :, :].astype(F32)


def dense_results(ids, mine, theirs, width):
    rows, model = mine.shape
    place = lambda size: pl.BlockSpec(
        (size, model), lambda j, ids: (jnp.bitwise_xor(ids[2], j), 0)
    )
    shape = jax.ShapeDtypeStruct
    return pl.pallas_call(
        dense_kernel,
        grid_spec=pltpu.PrefetchScalarGridSpec(
            num_scalar_prefetch=1,
            grid=(2,),
            in_specs=[whole(mine), whole(theirs)],
            out_specs=[place(model // 2), place(model // 2), place(width // 2)],
        ),
        out_shape=[shape((model, model), F32)] * 2 + [shape((width, model), F32)],
        compiler_params=vmem(14),
        cost_estimate=taking(0.01),
        name="dense_results",
    )(ids, mine, theirs)


def held_until(array, after):
    return pl.pallas_call(
        lambda *refs: None,
        in_specs=[ANYWHERE] * (1 + len(after)),
        out_specs=ANYWHERE,
        out_shape=jax.ShapeDtypeStruct(array.shape, array.dtype),
        input_output_aliases={0: 0},
        name="held",
    )(array, *after)


def swap(array, flip, axis="mp"):
    return lax.ppermute(array, axis, [(i, i ^ flip) for i in range(lax.axis_size(axis))])


def upward(array, ranks):
    return lax.ppermute(array, "seq", [(i, i + 1) for i in range(ranks - 1)])


def downward(array, ranks):
    return lax.ppermute(array, "seq", [(i + 1, i) for i in range(ranks - 1)])


def spread_over_mp(part):
    across = swap(part, 2)
    return [part, swap(part, 1), across, swap(across, 1)]


def body_resident(
    inputs,
    selection,
    gain1,
    shift1,
    w_qkv,
    b_qv,
    w_score,
    b_score,
    w_out,
    b_out,
    gain2,
    shift2,
    w_up,
    b_up,
    w_down,
    b_down,
    cotangent,
):
    ranks = lax.axis_size("seq")
    me, rank, side = lax.axis_index("mp"), lax.axis_index("seq"), lax.axis_index("dp")
    ids = jnp.stack([me, rank, side]).astype(jnp.int32)
    rows, model = inputs.shape[1:]
    quarter = rows // 4
    block = quarter // 2
    total = ranks * rows
    blocks = rows // KB
    width = w_qkv.shape[2]
    heads = width // HD

    own = lax.dynamic_slice_in_dim(inputs[0], me * quarter, quarter, 0)
    arriving = {}
    for h in range(2):
        part = own[h * block : (h + 1) * block]
        for k in range(1, ranks):
            part = upward(part, ranks)
            arriving[k, h] = part
    gathered = {}
    for k in range(1, ranks):
        for halves in ((0, 1),) if k < ranks - 1 else ((0,), (1,)):
            mine = jnp.concatenate([arriving[k, h] for h in halves], axis=0)
            mine = jnp.concatenate([mine, swap(mine, 2)], axis=0)
            gathered[k, halves] = [mine, swap(mine, 1)]

    b_high = b_up.astype(BF)
    b_low = (b_up - b_high.astype(F32)).astype(BF)
    out_rows = jnp.concatenate(
        [w_out, b_high[None], b_low[None], jnp.zeros((14, model), BF)], axis=0
    )
    w_outs = spread_over_mp(out_rows)
    first = swap(jnp.where(side == 0, w_up, w_down), 2)
    second = swap(first, 1, "dp")
    w_ups = [w_up, swap(w_up, 1), first, swap(first, 1)]
    w_downs = [w_down, swap(w_down, 1), second, swap(second, 1)]

    vectors = jnp.stack([gain1, shift1, b_out, gain2, shift2, b_down] + [gain1] * 2, axis=0)
    lines = jnp.pad(
        jnp.stack([jnp.pad(b_score, (width, WIDE - width - heads))[:width], b_qv[1], b_qv[0]]),
        ((0, 5), (0, WIDE - width)),
    )
    lines = lax.dynamic_update_slice(lines, b_score[None], (0, width))
    wide = lambda a: jnp.pad(a, ((0, 0), (0, WIDE - a.shape[1])))
    wq, wv = wide(w_qkv[:, 0]), wide(w_qkv[:, 2])
    wk = wide(jnp.concatenate([w_qkv[:, 1], w_score], axis=1))

    *buffers, qt = project_own(
        ids, inputs[0], vectors, lines, (wk, wv, wq), width, total, block, [arriving[ranks - 1, h] for h in range(2)]
    )
    for (k, halves), arrays in gathered.items():
        count = len(halves)
        buffers = project(
            arrays,
            [(j % 2, (j // 2 * count + i) * block) for j in range(4) for i in range(count)],
            block,
            width,
            lambda j, k=k, h=halves[0], count=count: 8 * k + (2 // count) * j + h,
            vectors,
            lines,
            (wk, wv),
            buffers,
            [(first, second)[k - 1]] if k < ranks - 1 else (),
        )
    first_in, ka, va = buffers

    chosen = selection[0]
    *mixed, norm = attend(ids, chosen, ka, va, qt, blocks)

    features = [mixed[0]] + [swap(mixed[j], j) for j in (1, 2, 3)]
    *mixed_grads, output, hidden_grad, kept, sent, sums, up_biases = feed_forward(
        ids, vectors, inputs[0], cotangent[0], features, w_outs, w_ups, w_downs
    )
    returned = [mixed_grads[0]] + [swap(mixed_grads[j], j) for j in (1, 2, 3)]

    part = model + width
    own_a, far_a, stay_b, leave_b = combine(ids, kept, swap(sent, 1), part)
    came_a, came_b = swap(far_a, 2), swap(leave_b, 1, "dp")

    weights = (wk, wv, wq)
    spread, query_grad, totals = attend_back(
        ids, chosen, ka, va, qt, norm, returned, blocks, (far_a, leave_b)
    )

    weights = (wk, wv, wq)
    stay_a, away_a, keep_b, send_b = first_sums(ids, own_a, came_a, stay_b, came_b)
    kept_3, sent_3 = push(spread, weights, 3, quarter, None, (away_a,))
    came_a, came_b, arrived_3 = swap(away_a, 1, "dp"), swap(send_b, 2), swap(sent_3, 1)
    qkv, qkv_leave = weight_sums(ids, first_in, spread, query_grad, width, (sent_3,))
    kept_2, sent_2 = push(spread, weights, 2, quarter, None, (qkv_leave,))
    dense = jnp.concatenate([stay_a + came_a, keep_b + came_b], axis=0)
    across = held_until(kept_3[1] + arrived_3[1], (dense, sent_2))
    dense = lax.psum(dense, "seq")
    sent_2, qkv_leave = held_until(sent_2, (across,)), held_until(qkv_leave, (across,))
    crossed_3, came_qkv, arrived_2 = swap(across, 2), swap(qkv_leave, 1, "dp"), swap(sent_2, 1)
    kept_1, sent_1 = push(spread, weights, 1, quarter, None, (across,))
    kept_0, sent_0 = push(spread, weights, 0, quarter, query_grad, (sent_1,))
    qkv = qkv + came_qkv
    across = kept_2[1] + arrived_2[1]
    carried = held_until(kept_3[0] + arrived_3[0] + crossed_3, (qkv, sent_0, across))
    carried = downward(carried, ranks)
    crossed_2, arrived_1, arrived_0 = swap(across, 2), swap(sent_1, 1), swap(sent_0, 1)
    mine = kept_2[0] + arrived_2[0] + crossed_2 + carried
    across = held_until(kept_1[1] + arrived_1[1], (mine,))
    output_parts = spread_over_mp(held_until(output, (mine,)))
    carried = downward(mine, ranks)
    crossed_1 = swap(across, 2)
    mine = kept_1[0] + arrived_1[0] + crossed_1 + carried
    across = held_until(kept_0[1] + arrived_0[1], (mine,))
    dense = held_until(dense, (across,))
    qkv = lax.psum(held_until(qkv, (dense,)), "seq")
    dense_theirs = swap(dense, 1, "dp")
    carried = downward(mine, ranks)
    crossed_0 = swap(across, 2)
    mine = kept_0[0] + arrived_0[0] + crossed_0

    output = ordered(ids, 0, output_parts, BF)
    input_part, small = finish(
        ids,
        vectors,
        inputs[0],
        carried,
        mine,
        hidden_grad,
        sums,
        up_biases,
        totals,
        (output, dense_theirs),
    )
    across = swap(input_part, 2)
    input_parts = [input_part, swap(input_part, 1), across]
    input_parts.append(swap(held_until(across, (qkv,)), 1))
    for flip in (1, 2):
        small = small + swap(small, flip)
    small = small + swap(small, 1, "dp")
    qkv_sum = ordered(ids, 2, [qkv, swap(qkv, 1, "dp")], F32)
    up_grad, down_grad, out_grad = dense_results(ids, dense, dense_theirs, width)
    for flip in (1, 2):
        small = small + swap(small, flip, "seq")
    input_grad = ordered(ids, 0, input_parts, BF)
    up_bias = lax.dynamic_slice_in_dim(small, 4 + me, 1, 0)[0]
    biases = lax.dynamic_slice_in_dim(small, 8 + me, 1, 0)[0]
    query_at, value_at = WIDE + width, WIDE
    qkv_grad = jnp.stack(
        [qkv_sum[:, query_at:], qkv_sum[:, :width], qkv_sum[:, value_at:query_at]], axis=1
    )
    qv_bias_grad = jnp.stack(
        [biases[2 * WIDE : 2 * WIDE + width], biases[WIDE : WIDE + width]], axis=0
    )
    return (
        output[None],
        input_grad[None],
        small[12],
        small[13],
        qkv_grad,
        qv_bias_grad,
        qkv_sum[:, width : width + heads],
        biases[width : width + heads],
        out_grad,
        small[2],
        small[0],
        small[1],
        up_grad,
        up_bias,
        down_grad,
        small[3],
    )


RESIDENT_TOKENS = 8192


def solution(mesh):
    def body(*args):
        tokens = args[0].shape[1] * mesh.shape["seq"]
        resident = mesh.shape["mp"] == 4 and mesh.shape["dp"] == 2
        resident = resident and mesh.shape["seq"] == 4 and tokens <= RESIDENT_TOKENS
        return (body_resident if resident else body_general)(*args)

    return jax.shard_map(
        body,
        mesh=mesh,
        in_specs=(
            P("dp", "seq", None),
            P("dp", "seq", None),
            P(),
            P(),
            P(None, None, "mp"),
            P(None, "mp"),
            P(None, "mp"),
            P("mp"),
            P("mp", None),
            P(),
            P(),
            P(),
            P(None, "mp"),
            P("mp"),
            P("mp", None),
            P(),
            P("dp", "seq", None),
        ),
        out_specs=(
            P("dp", "seq", None),
            P("dp", "seq", None),
            P(),
            P(),
            P(None, None, "mp"),
            P(None, "mp"),
            P(None, "mp"),
            P("mp"),
            P("mp", None),
            P(),
            P(),
            P(),
            P(None, "mp"),
            P("mp"),
            P("mp", None),
            P(),
        ),
        check_vma=False,
    )
```

```python
import functools

import jax
import jax.numpy as jnp
from jax import lax
from jax.experimental import pallas as pl
from jax.experimental.pallas import tpu as pltpu
from jax.sharding import PartitionSpec as P

HD = 64
KB = 128
WINDOW = 64


EPSILON = 1e-05
NEGATIVE = -1e30
HIGHEST = lax.Precision.HIGHEST


def layer_norm(value, gain, shift):
    center = jnp.mean(value, axis=-1, keepdims=True)
    centered = value - center
    spread = jnp.mean(centered * centered, axis=-1, keepdims=True)
    return centered * lax.rsqrt(spread + EPSILON) * gain + shift


def gelu_tanh(value):
    return jax.nn.gelu(value, approximate=True)


def rows_inner(left, right):
    return lax.dot_general(
        left, right, (((0,), (0,)), ((), ())), preferred_element_type=jnp.float32
    )


def cols_inner(left, right):
    return lax.dot_general(
        left, right, (((1,), (1,)), ((), ())), preferred_element_type=jnp.float32
    )


def block_masks(block_ids, picked_raw):
    offsets = jnp.arange(KB, dtype=jnp.int32)
    query_pos = block_ids[:, None] * KB + offsets
    key_pos = jnp.maximum(picked_raw, 0)[:, :, None] * KB + offsets
    slot_ids = jnp.arange(picked_raw.shape[1], dtype=jnp.int32)[None, None, :, None]
    query_at = query_pos[:, :, None, None]
    key_at = key_pos[:, None]
    window_mask = (
        (key_at <= query_at)
        & (key_at > query_at - WINDOW)
        & (slot_ids < 2)
        & (picked_raw >= 0)[:, None, :, None]
    )
    chosen_mask = (key_at <= query_at - WINDOW) & (slot_ids >= 2)
    return (window_mask, chosen_mask)


def block_scores(query_blocks, key_cand, mark_cand, window_mask, chosen_mask):
    logits = jnp.einsum(
        "gihd,gcjhd->ghicj", query_blocks, key_cand, preferred_element_type=jnp.float32
    ) * HD ** (-0.5)
    mark_term = mark_cand.astype(jnp.float32).transpose(0, 3, 1, 2)[:, :, None]
    return jnp.where(
        window_mask[:, None], logits, jnp.where(chosen_mask[:, None], logits + mark_term, NEGATIVE)
    )


def body_general(
    inputs,
    selection,
    gain1,
    shift1,
    w_qkv,
    b_qv,
    w_score,
    b_score,
    w_out,
    b_out,
    gain2,
    shift2,
    w_up,
    b_up,
    w_down,
    b_down,
    cotangent,
):
    seq_rank = lax.axis_index("seq")
    tokens = inputs[0].astype(jnp.float32)
    row_count = tokens.shape[0]
    local_blocks = row_count // KB
    local_width = w_qkv.shape[2]
    local_heads = local_width // HD
    scale = HD ** (-0.5)
    normed1, pull_norm1 = jax.vjp(layer_norm, tokens, gain1, shift1)
    first_in = normed1.astype(jnp.bfloat16)
    projected = jnp.einsum("td,dsk->tsk", first_in, w_qkv, preferred_element_type=jnp.float32)
    query_rows = (projected[:, 0] + b_qv[0]).astype(jnp.bfloat16)
    key_rows = projected[:, 1].astype(jnp.bfloat16)
    value_rows = (projected[:, 2] + b_qv[1]).astype(jnp.bfloat16)
    rating = jnp.dot(first_in, w_score, preferred_element_type=jnp.float32) + b_score
    marks = jax.nn.log_sigmoid(rating).astype(jnp.bfloat16)
    all_keys, all_values, all_marks = (
        lax.all_gather(key_rows, "seq", axis=0, tiled=True),
        lax.all_gather(value_rows, "seq", axis=0, tiled=True),
        lax.all_gather(marks, "seq", axis=0, tiled=True),
    )
    total_blocks = all_keys.shape[0] // KB
    key_blocks = all_keys.reshape(total_blocks, KB, local_heads, HD)
    value_blocks = all_values.reshape(total_blocks, KB, local_heads, HD)
    mark_blocks = all_marks.reshape(total_blocks, KB, local_heads)
    block_ids = seq_rank * local_blocks + jnp.arange(local_blocks, dtype=jnp.int32)
    picked_raw = jnp.concatenate([block_ids[:, None] - 1, block_ids[:, None], selection[0]], axis=1)
    picked = jnp.maximum(picked_raw, 0)
    key_cand = jnp.take(key_blocks, picked, axis=0)
    value_cand = jnp.take(value_blocks, picked, axis=0)
    mark_cand = jnp.take(mark_blocks, picked, axis=0)
    window_mask, chosen_mask = block_masks(block_ids, picked_raw)
    query_blocks = query_rows.reshape(local_blocks, KB, local_heads, HD)
    scores = block_scores(query_blocks, key_cand, mark_cand, window_mask, chosen_mask)
    highest = jnp.max(scores, axis=(3, 4), keepdims=True)
    exponent = jnp.exp(scores - highest)
    summed = jnp.sum(exponent, axis=(3, 4), keepdims=True)
    weights = exponent / summed
    log_norm = highest + jnp.log(summed)
    attended = jnp.einsum(
        "ghicj,gcjhd->gihd",
        weights.astype(jnp.bfloat16),
        value_cand,
        preferred_element_type=jnp.float32,
    )
    mixed = attended.reshape(row_count, local_width).astype(jnp.bfloat16)
    branch = lax.psum(jnp.dot(mixed, w_out, preferred_element_type=jnp.float32), "mp")
    hidden = tokens + branch + b_out
    normed2, pull_norm2 = jax.vjp(layer_norm, hidden, gain2, shift2)
    second_in = normed2.astype(jnp.bfloat16)
    pre = jnp.dot(second_in, w_up, preferred_element_type=jnp.float32) + b_up
    activated, pull_gelu = jax.vjp(gelu_tanh, pre)
    act_low = activated.astype(jnp.bfloat16)
    feed = lax.psum(
        jnp.dot(act_low, w_down, preferred_element_type=jnp.float32).astype(jnp.bfloat16), "mp"
    ).astype(jnp.float32)
    output = (hidden + feed + b_down).astype(jnp.bfloat16)
    upstream = cotangent[0]
    upstream_f = upstream.astype(jnp.float32)
    down_grad = rows_inner(act_low, upstream)
    down_bias_grad = jnp.sum(upstream_f, axis=0)
    act_grad = cols_inner(upstream, w_down)
    pre_grad = pull_gelu(act_grad)[0].astype(jnp.bfloat16)
    up_grad = rows_inner(second_in, pre_grad)
    up_bias_grad = jnp.sum(pre_grad.astype(jnp.float32), axis=0)
    second_grad = lax.psum(cols_inner(pre_grad, w_up), "mp")
    hidden_back, gain2_grad, shift2_grad = pull_norm2(second_grad)
    hidden_grad = upstream_f + hidden_back
    out_bias_grad = jnp.sum(hidden_grad, axis=0)
    branch_grad = hidden_grad.astype(jnp.bfloat16)
    out_grad = rows_inner(mixed, branch_grad)
    mixed_grad = cols_inner(branch_grad, w_out).astype(jnp.bfloat16)
    grad_blocks = mixed_grad.reshape(local_blocks, KB, local_heads, HD)
    again = block_scores(query_blocks, key_cand, mark_cand, window_mask, chosen_mask)
    prob_again = jnp.exp(again - log_norm)
    grad_prob = jnp.einsum(
        "gihd,gcjhd->ghicj", grad_blocks, value_cand, preferred_element_type=jnp.float32
    )
    delta = jnp.sum(prob_again * grad_prob, axis=(3, 4), keepdims=True)
    score_full = prob_again * (grad_prob - delta)
    score_low = score_full.astype(jnp.bfloat16)
    query_grad = (
        (
            jnp.einsum("ghicj,gcjhd->gihd", score_low, key_cand, preferred_element_type=jnp.float32)
            * scale
        )
        .reshape(row_count, local_width)
        .astype(jnp.bfloat16)
    )
    prob_low = prob_again.astype(jnp.bfloat16)
    key_part = (
        jnp.einsum("ghicj,gihd->gcjhd", score_low, query_blocks, preferred_element_type=jnp.float32)
        * scale
    )
    value_part = jnp.einsum(
        "ghicj,gihd->gcjhd", prob_low, grad_blocks, preferred_element_type=jnp.float32
    )
    mark_part = jnp.sum(jnp.where(chosen_mask[:, None], score_full, 0.0), axis=2).transpose(
        0, 2, 3, 1
    )
    key_spread = (
        jnp.zeros((total_blocks, KB, local_heads, HD), jnp.float32).at[picked].add(key_part)
    )
    value_spread = (
        jnp.zeros((total_blocks, KB, local_heads, HD), jnp.float32).at[picked].add(value_part)
    )
    mark_spread = jnp.zeros((total_blocks, KB, local_heads), jnp.float32).at[picked].add(mark_part)
    key_total, value_total, mark_total = (
        lax.psum_scatter(
            key_spread.reshape(total_blocks * KB, local_width),
            "seq",
            scatter_dimension=0,
            tiled=True,
        ),
        lax.psum_scatter(
            value_spread.reshape(total_blocks * KB, local_width),
            "seq",
            scatter_dimension=0,
            tiled=True,
        ),
        lax.psum_scatter(
            mark_spread.reshape(total_blocks * KB, local_heads),
            "seq",
            scatter_dimension=0,
            tiled=True,
        ),
    )
    key_grad = key_total.astype(jnp.bfloat16)
    value_grad = value_total.astype(jnp.bfloat16)
    rating_grad = mark_total * jax.nn.sigmoid(-rating)
    score_grad = lax.dot_general(
        first_in.astype(jnp.float32),
        rating_grad,
        (((0,), (0,)), ((), ())),
        precision=HIGHEST,
        preferred_element_type=jnp.float32,
    )
    score_bias_grad = jnp.sum(rating_grad, axis=0)
    stacked = jnp.stack([query_grad, key_grad, value_grad], axis=1)
    qkv_grad = jnp.einsum("td,tsk->dsk", first_in, stacked, preferred_element_type=jnp.float32)
    qv_bias_grad = jnp.stack(
        [
            jnp.sum(query_grad.astype(jnp.float32), axis=0),
            jnp.sum(value_grad.astype(jnp.float32), axis=0),
        ],
        axis=0,
    )
    first_part = jnp.einsum("tsk,dsk->td", stacked, w_qkv, preferred_element_type=jnp.float32)
    first_part = first_part + jnp.dot(rating_grad, w_score.astype(jnp.float32).T, precision=HIGHEST)
    first_grad = lax.psum(first_part.astype(jnp.bfloat16), "mp").astype(jnp.float32)
    token_back, gain1_grad, shift1_grad = pull_norm1(first_grad)
    input_grad = (hidden_grad + token_back).astype(jnp.bfloat16)
    summed_grads = lax.psum(
        (
            gain1_grad,
            shift1_grad,
            qkv_grad,
            qv_bias_grad,
            score_grad,
            score_bias_grad,
            out_grad,
            out_bias_grad,
            gain2_grad,
            shift2_grad,
            up_grad,
            up_bias_grad,
            down_grad,
            down_bias_grad,
        ),
        ("dp", "seq"),
    )
    return (
        output[None],
        input_grad[None],
        summed_grads[0],
        summed_grads[1],
        summed_grads[2],
        summed_grads[3],
        summed_grads[4],
        summed_grads[5],
        summed_grads[6],
        summed_grads[7],
        summed_grads[8],
        summed_grads[9],
        summed_grads[10],
        summed_grads[11],
        summed_grads[12],
        summed_grads[13],
    )


WIDE = 256
BF = jnp.bfloat16
F32 = jnp.float32
ANYWHERE = pl.BlockSpec(memory_space=pl.ANY)
PAIR = 4


def matmul(left, right):
    return jnp.dot(left, right, preferred_element_type=F32)


def near_far(left, right):
    return lax.dot_general(left, right, (((1,), (1,)), ((), ())), preferred_element_type=F32)


def taking(microseconds):
    return pl.CostEstimate(
        flops=int(microseconds * 1.1e9), bytes_accessed=int(microseconds * 1e5), transcendentals=0
    )


def vmem(mebibytes):
    return pltpu.CompilerParams(vmem_limit_bytes=mebibytes * 1024 * 1024)


def ordered_after(kernel, at, count):
    return lambda *refs: kernel(*refs[:at], *refs[at + count :])


def whole(array):
    shape = array.shape
    return pl.BlockSpec(shape, lambda *_: (0,) * len(shape), pipeline_mode=pl.Buffered(1))


def normed_parts(value):
    center = jnp.mean(value, axis=-1, keepdims=True)
    centered = value - center
    spread = jnp.mean(centered * centered, axis=-1, keepdims=True)
    scale = lax.rsqrt(spread + EPSILON)
    return centered * scale, scale


def norm_back(grad, hat, scale, gain):
    g = gain * grad
    return scale * (
        g
        - jnp.mean(g, axis=-1, keepdims=True)
        - hat * jnp.mean(g * hat, axis=-1, keepdims=True)
    )


def column_sums(array):
    return jnp.sum(array, axis=0, keepdims=True)


def project_rows(width, value, vectors, lines, weights, fi, ka, va, qt):
    hat, _ = normed_parts(value.astype(F32))
    normed = (hat * vectors[0:1, :] + vectors[1:2, :]).astype(BF)
    fi[...] = normed
    half = WIDE // 2
    heads = width // HD
    keys = matmul(normed, weights[0][...]) + lines[0:1, :]
    values = matmul(normed, weights[1][...]) + lines[1:2, :]
    high = keys[:, half:]
    lane = lax.broadcasted_iota(jnp.int32, high.shape, 1) - (width - half)
    small = jnp.exp(-jnp.abs(high))
    mark = jnp.minimum(high, 0.0) - jnp.log1p(small)
    slope = jnp.where(high >= 0, small, 1.0) / (1.0 + small)
    ones = jnp.where((lane >= heads) & (lane < heads + 3), 1.0, 0.0)
    marked = (lane >= 0) & (lane < heads)
    ka[:, :half] = keys[:, :half].astype(BF)
    ka[:, half:] = jnp.where(lane < 0, high, jnp.where(marked, mark, ones)).astype(BF)
    va[:, :half] = values[:, :half].astype(BF)
    va[:, half:] = jnp.where(
        lane < 0, values[:, half:], jnp.where(marked, slope, ones)
    ).astype(BF)
    if qt is not None:
        query = (matmul(normed, weights[2][...]) + lines[2:3, :]).astype(BF).astype(F32)
        qt[...] = (query * HD ** (-0.5)).T[:width].astype(BF)


def project_own_kernel(ids, x, vectors, lines, wk, wv, wq, fi, ka, va, qt):
    del ids
    project_rows(qt.shape[0], x[...], vectors, lines, (wk, wv, wq), fi, ka, va, qt)


def project_kernel(sources, arrays, width, *refs):
    vectors, lines, wk, wv = refs[:4]
    fi, ka, va, held, sems = refs[7 + arrays :]
    step = pl.program_id(0)
    count, block = held.shape[:2]

    def copy(j):
        array, row = sources[j]
        return pltpu.make_async_copy(
            refs[4 + array].at[pl.ds(row, block), :], held.at[j], sems.at[j]
        )

    @pl.when(step == 0)
    def _():
        for j in range(count):
            copy(j).start()

    for j in range(count):

        @pl.when(step == j)
        def _(j=j):
            copy(j).wait()

    project_rows(width, held[step], vectors, lines, (wk, wv), fi, ka, va, None)


def project_shapes(total, model):
    return [
        jax.ShapeDtypeStruct((total, model), BF),
        jax.ShapeDtypeStruct((total, WIDE), BF),
        jax.ShapeDtypeStruct((total, WIDE), BF),
    ]


def project_specs(block, model, place):
    rows = lambda cols: pl.BlockSpec((block, cols), lambda j, *_: (place(j), 0))
    return [rows(model), rows(WIDE), rows(WIDE)]


def project_own(ids, x, vectors, lines, weights, width, total, block, after):
    rows, model = x.shape
    per = rows // 4 // block
    operands = [vectors, lines, *weights]
    return pl.pallas_call(
        ordered_after(project_own_kernel, 2 + len(operands), len(after)),
        grid_spec=pltpu.PrefetchScalarGridSpec(
            num_scalar_prefetch=1,
            grid=(rows // block,),
            in_specs=[
                pl.BlockSpec(
                    (block, model),
                    lambda j, ids: (
                        jnp.bitwise_xor(lax.div(j, per), ids[0]) * per + lax.rem(j, per),
                        0,
                    ),
                )
            ]
            + [whole(a) for a in operands]
            + [ANYWHERE] * len(after),
            out_specs=project_specs(block, model, lambda j: j)
            + [pl.BlockSpec((width, block), lambda j, *_: (0, j))],
        ),
        out_shape=project_shapes(total, model) + [jax.ShapeDtypeStruct((width, rows), BF)],
        compiler_params=vmem(16),
        cost_estimate=taking(8),
        name="project_own",
    )(ids, x, *operands, *after)


def project(arrays, sources, block, width, place, vectors, lines, weights, buffers, after=()):
    model = arrays[0].shape[1]
    total = buffers[0].shape[0]
    count, given = len(sources), len(arrays)
    operands = [vectors, lines, *weights]
    return pl.pallas_call(
        ordered_after(
            functools.partial(project_kernel, sources, given, width),
            len(operands) + given + 3,
            len(after),
        ),
        grid=(count,),
        in_specs=[whole(a) for a in operands] + [ANYWHERE] * (given + 3 + len(after)),
        out_specs=project_specs(block, model, place),
        out_shape=project_shapes(total, model),
        scratch_shapes=[
            pltpu.VMEM((count, block, model), BF),
            pltpu.SemaphoreType.DMA((count,)),
        ],
        input_output_aliases={len(operands) + given + i: i for i in range(3)},
        compiler_params=vmem(18),
        cost_estimate=taking(count),
        name="project",
    )(*operands, *arrays, *buffers, *after)


def head_diagonal(rows, tail):
    width = rows.shape[0]
    heads = width // HD
    columns = []
    for h in range(heads):
        parts = []
        if h > 0:
            parts.append(jnp.zeros((h * HD, KB), BF))
        parts.append(rows[h * HD : (h + 1) * HD])
        if h < heads - 1:
            parts.append(jnp.zeros(((heads - 1 - h) * HD, KB), BF))
        columns.append(jnp.concatenate(parts, axis=0))
    top = jnp.concatenate(columns, axis=1)
    rest = jnp.zeros((WIDE - width - 16, heads * KB), BF)
    return jnp.concatenate([top, tail.astype(BF), rest], axis=0)


def tail_rows(heads, marked, term):
    shape = (16, heads * KB)
    row = lax.broadcasted_iota(jnp.int32, shape, 0)
    column = lax.broadcasted_iota(jnp.int32, shape, 1) // KB
    tail = jnp.where(row == column, 1.0, 0.0) if marked else jnp.zeros(shape, F32)
    if term is not None:
        for piece in range(3):
            part = term.astype(BF).astype(F32)
            tail = jnp.where(row == heads + piece, part, tail)
            term = term - part
    return tail


def offsets_tile(heads):
    shape = (KB, heads * KB)
    key = lax.broadcasted_iota(jnp.int32, shape, 0)
    query = lax.rem(lax.broadcasted_iota(jnp.int32, shape, 1), KB)
    return key - query


def spots(ids, chosen, step, blocks):
    me, rank, per = ids[0], ids[1], blocks // 4
    natural = jnp.bitwise_xor(lax.div(step, per), me) * per + lax.rem(step, per)
    block = rank * blocks + natural
    picked = [chosen[natural, t] for t in (1, 2, 3)]
    starts = []
    for name in [jnp.maximum(block - 1, 0), block, *picked]:
        inner = lax.rem(name, blocks)
        place = (rank - lax.div(name, blocks)) * blocks + lax.rem(inner, per)
        place = place + jnp.bitwise_xor(lax.div(inner, per), me) * per
        starts.append(pl.multiple_of(place * KB, KB))
    first = jnp.where(block >= 1, KB - WINDOW, 2 * KB)
    return starts, [first] + [(block - c) * KB - WINDOW for c in picked]


def masks_of(gap, bounds):
    return [gap > bounds[0], gap <= 0] + [gap <= b for b in bounds[1:]]


def diagonal_of(full, heads):
    return jnp.concatenate(
        [full[h * HD : (h + 1) * HD, h * KB : (h + 1) * KB] for h in range(heads)], axis=0
    )


def attend_kernel(blocks, ids, chosen, ka, va, qt, *outs):
    *mixed, norm = outs
    step = pl.program_id(0)
    width = qt.shape[0]
    heads = width // HD

    def block_forward(at):
        query = qt[:, at * KB : (at + 1) * KB]
        plain = head_diagonal(query, tail_rows(heads, False, None))
        marked = head_diagonal(query, tail_rows(heads, True, None))
        starts, bounds = spots(ids, chosen, step * PAIR + at, blocks)
        tiles = [ka[pl.ds(s, KB), :] for s in starts]
        near = matmul(jnp.concatenate(tiles[:2], axis=0), plain)
        far = matmul(jnp.concatenate(tiles[1:], axis=0), marked)
        gap = offsets_tile(heads)
        scores = [near[:KB], jnp.where(gap > -WINDOW, near[KB:], far[:KB])]
        scores += [far[KB * (1 + t) : KB * (2 + t)] for t in range(3)]
        scores = [jnp.where(m, s, NEGATIVE) for m, s in zip(masks_of(gap, bounds), scores)]
        top = functools.reduce(jnp.maximum, scores)
        top = jnp.max(top, axis=0, keepdims=True)
        weights = [jnp.exp(s - top) for s in scores]
        total = jnp.sum(functools.reduce(jnp.add, weights), axis=0, keepdims=True)
        stacked = jnp.concatenate([w.astype(BF) for w in weights], axis=0)
        values = jnp.concatenate([va[pl.ds(s, KB), :] for s in starts], axis=0)
        full = rows_inner(values, stacked) / total
        return diagonal_of(full, heads).astype(BF), top + jnp.log(total)

    results = [block_forward(at) for at in range(PAIR)]
    for at, (_, line) in enumerate(results):
        norm[at] = line
    result = jnp.concatenate([value for value, _ in results], axis=1)
    for p in range(4):

        @pl.when(lax.div(step, blocks // 4 // PAIR) == p)
        def _(p=p):
            mixed[p][...] = result


def attend(ids, chosen, ka, va, qt, blocks):
    width = qt.shape[0]
    heads = width // HD
    per = blocks // 4
    turns = per // PAIR
    piece = lambda p: pl.BlockSpec(
        (width, PAIR * KB), lambda i, *_: (0, jnp.clip(i - turns * p, 0, turns - 1))
    )
    return pl.pallas_call(
        functools.partial(attend_kernel, blocks),
        grid_spec=pltpu.PrefetchScalarGridSpec(
            num_scalar_prefetch=2,
            grid=(blocks // PAIR,),
            in_specs=[
                whole(ka),
                whole(va),
                pl.BlockSpec((width, PAIR * KB), lambda i, *_: (0, i)),
            ],
            out_specs=[piece(p) for p in range(4)]
            + [pl.BlockSpec((PAIR, 1, heads * KB), lambda i, *_: (i, 0, 0))],
        ),
        out_shape=[jax.ShapeDtypeStruct((width, per * KB), BF)] * 4
        + [jax.ShapeDtypeStruct((blocks, 1, heads * KB), F32)],
        compiler_params=vmem(30),
        cost_estimate=taking(14),
        name="attend",
    )(ids, chosen, ka, va, qt)


def attend_back_kernel(
    blocks,
    ids,
    chosen,
    ka,
    va,
    qt,
    norm,
    *refs,
):
    grads = refs[:4]
    spread, query_grad, totals, key_sum, value_sum, grad_all, sems = refs[4:]
    step = pl.program_id(0)
    width = qt.shape[0]
    heads = width // HD
    per, steps = blocks // 4, blocks // PAIR

    def copy(j):
        return pltpu.make_async_copy(grads[j], grad_all.at[j], sems.at[j])

    @pl.when(step == 0)
    def _():
        for j in range(4):
            copy(j).start()
        key_sum[...] = jnp.zeros_like(key_sum)
        value_sum[...] = jnp.zeros_like(value_sum)
        totals[...] = jnp.zeros_like(totals)
        for j in range(4):
            copy(j).wait()

    def block_back(at):
        index = step * PAIR + at
        column = slice(at * KB, (at + 1) * KB)
        query = qt[:, column]
        lanes = pl.ds(pl.multiple_of(lax.rem(index, per) * KB, KB), KB)
        upstream = grad_all[lax.div(index, per), :, lanes]
        plain = head_diagonal(query, tail_rows(heads, False, -norm[at]))
        marked = head_diagonal(query, tail_rows(heads, True, -norm[at]))
        back = head_diagonal(upstream, tail_rows(heads, False, None))
        starts, bounds = spots(ids, chosen, index, blocks)
        tiles = [ka[pl.ds(s, KB), :] for s in starts]
        near = matmul(jnp.concatenate(tiles[:2], axis=0), plain)
        far = matmul(jnp.concatenate(tiles[1:], axis=0), marked)
        slopes = matmul(jnp.concatenate([va[pl.ds(s, KB), :] for s in starts], axis=0), back)
        gap = offsets_tile(heads)
        masks = masks_of(gap, bounds)
        window = gap > -WINDOW
        scores = [near[:KB], jnp.where(window, near[KB:], far[:KB])]
        scores += [far[KB * (1 + t) : KB * (2 + t)] for t in range(3)]
        probs = [jnp.where(m, jnp.exp(s), 0.0) for m, s in zip(masks, scores)]
        terms = [p * slopes[c * KB : (c + 1) * KB] for c, p in enumerate(probs)]
        delta = column_sums(functools.reduce(jnp.add, terms))
        signals = [t - p * delta for t, p in zip(terms, probs)]
        own = signals[1]
        near_signal = jnp.concatenate([signals[0], jnp.where(window, own, 0.0)], axis=0).astype(BF)
        far_signal = jnp.concatenate(
            [jnp.where(window, 0.0, own)] + signals[2:], axis=0
        ).astype(BF)
        signal = jnp.concatenate(signals, axis=0).astype(BF)
        prob = jnp.concatenate(probs, axis=0).astype(BF)
        near_keys = near_far(near_signal, plain)
        far_keys = near_far(far_signal, marked)
        value_parts = near_far(prob, back)
        key_parts = [near_keys[:KB], near_keys[KB:] + far_keys[:KB]]
        key_parts += [far_keys[KB * (1 + t) : KB * (2 + t)] for t in range(3)]
        value_parts = [value_parts[c * KB : (c + 1) * KB] for c in range(5)]
        keys = jnp.concatenate([tiles[0], tiles[1]] + tiles[2:], axis=0)
        full = diagonal_of(rows_inner(keys, signal), heads) * HD ** (-0.5)
        full = jnp.concatenate([full, jnp.zeros((WIDE - width, KB), F32)], axis=0).T
        return starts, key_parts, value_parts, full

    @pl.when(step < steps)
    def _():
        results = [block_back(at) for at in range(PAIR)]
        for at, (starts, key_parts, value_parts, full) in enumerate(results):
            for c, s in enumerate(starts):
                key_sum[pl.ds(s, KB), :] += key_parts[c]
                value_sum[pl.ds(s, KB), :] += value_parts[c]
            query_grad[at * KB : (at + 1) * KB, :] = full.astype(BF)
            totals[:, 2 * WIDE :] += column_sums(full)

    @pl.when(step >= steps)
    def _():
        rows = spread.shape[0]
        at = pl.ds(pl.multiple_of((step - steps) * rows, rows), rows)
        lane = lax.broadcasted_iota(jnp.int32, (rows, WIDE), 1)
        marks = (lane >= width) & (lane < width + heads)
        keys = jnp.where(lane < width, key_sum[at, :], 0.0)
        keys = jnp.where(marks, key_sum[at, :] * va[at, :].astype(F32), keys)
        values = jnp.where(lane < width, value_sum[at, :], 0.0)
        spread[:, :WIDE] = keys.astype(BF)
        spread[:, WIDE:] = values.astype(BF)
        totals[:, :WIDE] += column_sums(keys)
        totals[:, WIDE : 2 * WIDE] += column_sums(values)


def attend_back(ids, chosen, ka, va, qt, norm, grads, blocks, after=()):
    width = qt.shape[0]
    heads = width // HD
    total = ka.shape[0]
    rows = 8 * KB
    steps = blocks // PAIR
    last = lambda i: jnp.minimum(i, steps - 1)
    return pl.pallas_call(
        ordered_after(functools.partial(attend_back_kernel, blocks), 10, len(after)),
        grid_spec=pltpu.PrefetchScalarGridSpec(
            num_scalar_prefetch=2,
            grid=(steps + total // rows,),
            in_specs=[
                whole(ka),
                whole(va),
                pl.BlockSpec((width, PAIR * KB), lambda i, *_: (0, last(i))),
                pl.BlockSpec((PAIR, 1, heads * KB), lambda i, *_: (last(i), 0, 0)),
            ]
            + [ANYWHERE] * (4 + len(after)),
            out_specs=[
                pl.BlockSpec((rows, 2 * WIDE), lambda i, *_: (jnp.maximum(i - steps, 0), 0)),
                pl.BlockSpec((PAIR * KB, WIDE), lambda i, *_: (last(i), 0)),
                pl.BlockSpec((1, 3 * WIDE), lambda i, *_: (0, 0)),
            ],
            scratch_shapes=[
                pltpu.VMEM((total, WIDE), F32),
                pltpu.VMEM((total, WIDE), F32),
                pltpu.VMEM((4, width, blocks // 4 * KB), BF),
                pltpu.SemaphoreType.DMA((4,)),
            ],
        ),
        out_shape=[
            jax.ShapeDtypeStruct((total, 2 * WIDE), BF),
            jax.ShapeDtypeStruct((blocks * KB, WIDE), BF),
            jax.ShapeDtypeStruct((1, 3 * WIDE), F32),
        ],
        compiler_params=vmem(56),
        cost_estimate=taking(36),
        name="attend_back",
    )(ids, chosen, ka, va, qt, norm, *grads, *after)


def feed_forward_kernel(order, ids, vectors, tokens, upstream, *refs):
    features, outs, ups, downs = refs[:4], refs[4:8], refs[8:12], refs[12:16]
    mixed_grads = refs[16:20]
    output, hidden_grad, kept, sent, sums, up_biases = refs[20:26]
    out_all, up_all, down_all, hidden, hat, scale, second_in, feed, second_grad = refs[26:35]
    staged, staged_out, sems, out_sems = refs[35:]
    step = pl.program_id(0)
    width = features[0].shape[0]
    model = tokens.shape[1]

    def copies(j, turned=False):
        slot = order.index(j)
        up, down = (downs[j], ups[j]) if turned else (ups[j], downs[j])
        return [
            pltpu.make_async_copy(up, up_all.at[slot], sems.at[4 + slot]),
            pltpu.make_async_copy(down, down_all.at[slot], sems.at[8 + slot]),
        ]

    def leaving(slot, first=0, last=5):
        target = (sent if slot < 2 else kept).at[slot % 2]
        half, out_half = model // 2, width // 2
        spans = [(staged, 0, 0, half), (staged, half, half + out_half, half)]
        spans += [(staged, model, model + width, model)]
        spans += [(staged_out, 0, half, out_half), (staged_out, out_half, model + out_half, out_half)]
        return [
            pltpu.make_async_copy(
                source.at[slot, pl.ds(a, n), :], target.at[pl.ds(b, n), :], out_sems.at[slot, i]
            )
            for i, (source, a, b, n) in enumerate(spans)
            if first <= i < last
        ]

    def out_copy(j):
        return pltpu.make_async_copy(outs[j], out_all.at[j], sems.at[j])

    @pl.when(step == 0)
    def _():
        for j in range(4):
            out_copy(j).start()
        for j in order:
            if j < 2:
                for copy in copies(j):
                    copy.start()
            else:

                @pl.when(ids[2] == 0)
                def _(j=j):
                    for copy in copies(j):
                        copy.start()

                @pl.when(ids[2] != 0)
                def _(j=j):
                    for copy in copies(j, True):
                        copy.start()

        for j in range(4):
            out_copy(j).wait()
        branch = vectors[2:3, :]
        for j in range(4):
            branch = branch + rows_inner(features[j][...], out_all[j, :width, :])
        value = tokens[...].astype(F32) + branch
        hidden[...] = value
        normed, inverse = normed_parts(value)
        scale[...] = inverse
        hat[...] = normed
        second_in[...] = (normed * vectors[3:4, :] + vectors[4:5, :]).astype(BF)
        feed[...] = jnp.zeros_like(feed)
        second_grad[...] = jnp.zeros_like(second_grad)

    for slot, j in enumerate(order):

        @pl.when(step == slot)
        def _(j=j):
            for copy in copies(j):
                copy.wait()

    bias = jnp.zeros((1, model), F32)
    for slot, j in enumerate(order):
        lines = out_all[j, width : width + 16, :].astype(F32)
        bias = jnp.where(step == slot, lines[0:1] + lines[1:2], bias)
    up, down = up_all[step], down_all[step]
    pre = matmul(second_in[...], up) + bias
    slope = 0.7978845608028654
    square = pre * pre
    bend = jnp.tanh(pre * (slope + slope * 0.044715 * square))
    share = 0.5 + 0.5 * bend
    act = (pre * share).astype(BF)
    derivative = share + pre * (share - share * share) * (
        2 * slope + 6 * slope * 0.044715 * square
    )
    feed[...] += matmul(act, down)
    pre_grad = near_far(upstream[...], down) * derivative
    pre_low = pre_grad.astype(BF)
    up_biases[0] = column_sums(pre_low.astype(F32))
    second_grad[...] += near_far(pre_low, up)
    up_grad = rows_inner(second_in[...], pre_low).astype(BF)
    down_grad = rows_inner(act, upstream[...]).astype(BF)

    staged[step, :model] = up_grad
    staged[step, model:] = down_grad
    for slot in range(4):

        @pl.when(step == slot)
        def _(slot=slot):
            for copy in leaving(slot, 0, 3):
                copy.start()

    @pl.when(step == 3)
    def _():
        output[...] = (hidden[...] + feed[...] + vectors[5:6, :]).astype(BF)
        grad = second_grad[...]
        normed = hat[...]
        upstream_f = upstream[...].astype(F32)
        back = upstream_f + norm_back(grad, normed, scale[...], vectors[3:4, :])
        hidden_grad[...] = back
        low = back.astype(BF)
        for j in range(4):
            mixed_grads[j][...] = near_far(out_all[j, :width, :], low).astype(BF)
            slot = order.index(j)
            staged_out[slot] = matmul(features[j][...], low).astype(BF)
            for copy in leaving(slot, 3, 5):
                copy.start()
        sums[...] = jnp.concatenate(
            [column_sums(a) for a in (grad * normed, grad, back, upstream_f)], axis=0
        )
        for slot in range(4):
            for copy in leaving(slot):
                copy.wait()


def feed_forward(ids, vectors, tokens, upstream, features, outs, ups, downs):
    width, quarter = features[0].shape
    model = tokens.shape[1]
    order = (1, 3, 0, 2)
    flat = lambda a: pl.BlockSpec(a.shape, lambda j, *_: (0,) * len(a.shape))
    mine = pl.BlockSpec(
        (quarter, model), lambda j, ids: (ids[0], 0), pipeline_mode=pl.Buffered(1)
    )
    shape = jax.ShapeDtypeStruct
    out_shape = [shape((width, quarter), BF)] * 4 + [
        shape((quarter, model), BF),
        shape((quarter, model), F32),
        shape((2, 2 * model + width, model), BF),
        shape((2, 2 * model + width, model), BF),
        shape((4, model), F32),
        shape((4, 1, model), F32),
    ]
    out_specs = [flat(a) for a in out_shape]
    out_specs[6] = out_specs[7] = ANYWHERE
    out_specs[9] = pl.BlockSpec((1, 1, model), lambda j, *_: (j, 0, 0))
    return pl.pallas_call(
        functools.partial(feed_forward_kernel, order),
        grid_spec=pltpu.PrefetchScalarGridSpec(
            num_scalar_prefetch=1,
            grid=(4,),
            in_specs=[whole(vectors), mine, mine]
            + [whole(a) for a in features]
            + [ANYWHERE] * 12,
            out_specs=out_specs,
            scratch_shapes=[
                pltpu.VMEM((4, width + 16, model), BF),
                pltpu.VMEM((4, model, model), BF),
                pltpu.VMEM((4, model, model), BF),
                pltpu.VMEM((quarter, model), F32),
                pltpu.VMEM((quarter, model), F32),
                pltpu.VMEM((quarter, 1), F32),
                pltpu.VMEM((quarter, model), BF),
                pltpu.VMEM((quarter, model), F32),
                pltpu.VMEM((quarter, model), F32),
                pltpu.VMEM((4, 2 * model, model), BF),
                pltpu.VMEM((4, width, model), BF),
                pltpu.SemaphoreType.DMA((12,)),
                pltpu.SemaphoreType.DMA((4, 5)),
            ],
        ),
        out_shape=out_shape,
        compiler_params=vmem(48),
        cost_estimate=taking(30),
        name="feed_forward",
    )(ids, vectors, tokens, upstream, *features, *outs, *ups, *downs)


def push_kernel(spread, wk, wv, *refs):
    kept, sent = refs[-2:]
    step = pl.program_id(0)
    part = near_far(spread[:, :WIDE], wk[...]) + near_far(spread[:, WIDE:], wv[...])
    if len(refs) > 2:
        part = part + near_far(refs[0][...], refs[1][...])
    part = part.astype(BF)

    @pl.when(step < 2)
    def _():
        sent[0] = part

    @pl.when(step >= 2)
    def _():
        kept[0] = part


def push(spread, weights, k, quarter, query_grad=None, after=()):
    wk, wv, wq = weights
    model = wk.shape[0]
    quarter_of = lambda j: 2 * j + 1 - jnp.where(j >= 2, 5, 0)
    operands = [spread, wk, wv]
    in_specs = [
        pl.BlockSpec((quarter, 2 * WIDE), lambda j: (4 * k + quarter_of(j), 0)),
        whole(wk),
        whole(wv),
    ]
    if query_grad is not None:
        operands += [query_grad, wq]
        in_specs += [pl.BlockSpec((quarter, WIDE), lambda j: (quarter_of(j), 0)), whole(wq)]
    return pl.pallas_call(
        ordered_after(push_kernel, len(operands), len(after)),
        grid=(4,),
        in_specs=in_specs + [ANYWHERE] * len(after),
        out_specs=[
            pl.BlockSpec((1, quarter, model), lambda j: (jnp.maximum(j - 2, 0), 0, 0)),
            pl.BlockSpec((1, quarter, model), lambda j: (jnp.minimum(j, 1), 0, 0)),
        ],
        out_shape=[jax.ShapeDtypeStruct((2, quarter, model), BF)] * 2,
        compiler_params=vmem(14),
        cost_estimate=taking(0.01),
        name="push",
    )(*operands, *after)


def finish_kernel(
    ids, vectors, tokens, arrived, mine, hidden_grad, sums, up_biases, totals, input_part, small
):
    first_grad = arrived[...].astype(F32) + mine[...].astype(F32)
    hat, scale = normed_parts(tokens[...].astype(F32))
    back = hidden_grad[...] + norm_back(first_grad, hat, scale, vectors[0:1, :])
    input_part[...] = back.astype(BF)
    small[...] = jnp.zeros_like(small)
    small[0:4, :] = sums[...]
    for slot, j in enumerate((1, 3, 0, 2)):
        small[pl.ds(4 + jnp.bitwise_xor(ids[0], j), 1), :] = up_biases[slot]
    small[pl.ds(8 + ids[0], 1), :] = totals[...]
    small[12:13, :] = column_sums(first_grad * hat)
    small[13:14, :] = column_sums(first_grad)


def finish(ids, vectors, tokens, arrived, mine, hidden_grad, sums, up_biases, totals, after):
    quarter, model = mine.shape
    operands = [arrived, mine, hidden_grad, sums, up_biases, totals]
    return pl.pallas_call(
        ordered_after(finish_kernel, 3 + len(operands), len(after)),
        grid_spec=pltpu.PrefetchScalarGridSpec(
            num_scalar_prefetch=1,
            grid=(1,),
            in_specs=[
                whole(vectors),
                pl.BlockSpec((quarter, model), lambda j, ids: (ids[0], 0)),
            ]
            + [whole(a) for a in operands]
            + [ANYWHERE] * len(after),
            out_specs=[
                pl.BlockSpec((quarter, model), lambda j, *_: (0, 0)),
                pl.BlockSpec((16, model), lambda j, *_: (0, 0)),
            ],
        ),
        out_shape=[
            jax.ShapeDtypeStruct((quarter, model), BF),
            jax.ShapeDtypeStruct((16, model), F32),
        ],
        compiler_params=vmem(20),
        cost_estimate=taking(0.01),
        name="finish",
    )(ids, vectors, tokens, *operands, *after)


def ordered_kernel(ids, *refs):
    *parts, out = refs
    for j, part in enumerate(parts):

        @pl.when(pl.program_id(0) == j)
        def _(part=part):
            out[...] = part[...].astype(out.dtype)


def ordered(ids, which, parts, kind):
    size, model = parts[0].shape
    count = len(parts)
    return pl.pallas_call(
        ordered_kernel,
        grid_spec=pltpu.PrefetchScalarGridSpec(
            num_scalar_prefetch=1,
            grid=(count,),
            in_specs=[whole(a) for a in parts],
            out_specs=pl.BlockSpec(
                (size, model), lambda j, ids: (jnp.bitwise_xor(ids[which], j), 0)
            ),
        ),
        out_shape=jax.ShapeDtypeStruct((count * size, model), kind),
        compiler_params=vmem(10),
        cost_estimate=taking(0.01),
        name="ordered",
    )(ids, *parts)


def combine_kernel(ids, first, kept, given, own_a, far_a, stay_b, leave_b):
    step, side = pl.program_id(0), ids[2]
    total = (kept[...].astype(F32) + given[...].astype(F32)).astype(BF)

    @pl.when(step < first)
    def _():
        own_a[...] = total[0]
        far_a[...] = total[1]

    @pl.when((step >= first) & (lax.div(step - first, 2) == side))
    def _():
        stay_b[...] = total

    @pl.when((step >= first) & (lax.div(step - first, 2) != side))
    def _():
        leave_b[...] = total


def combine(ids, kept, given, part):
    _, rows, model = kept.shape
    block = (rows - part) // 4
    first = part // block
    both = pl.BlockSpec((2, block, model), lambda i, ids: (0, i, 0))
    a_rows = pl.BlockSpec((block, model), lambda i, ids: (jnp.minimum(i, first - 1), 0))
    b_rows = lambda turn: pl.BlockSpec(
        (2, block, model),
        lambda i, ids: (
            0,
            jnp.clip(i - first - 2 * jnp.where(turn, 1 - ids[2], ids[2]), 0, 1),
            0,
        ),
    )
    shape = jax.ShapeDtypeStruct
    return pl.pallas_call(
        lambda ids, *refs: combine_kernel(ids, first, *refs),
        grid_spec=pltpu.PrefetchScalarGridSpec(
            num_scalar_prefetch=1,
            grid=(rows // block,),
            in_specs=[both, both],
            out_specs=[a_rows, a_rows, b_rows(False), b_rows(True)],
        ),
        out_shape=[shape((part, model), BF)] * 2 + [shape((2, 2 * block, model), BF)] * 2,
        compiler_params=vmem(10),
        cost_estimate=taking(6),
        name="combine",
    )(ids, kept, given)


def weight_sums_kernel(ids, first_in, spread, query_grad, stay, leave, held, held_query):
    step = pl.program_id(0)
    steps = pl.num_programs(0)
    turned = first_in[...].T
    rows = matmul(turned, spread[...])

    @pl.when(step == 0)
    def _():
        held[...] = rows
        held_query[...] = matmul(turned, query_grad[...])

    @pl.when(step > 0)
    def _():
        held[...] += rows

    @pl.when((step > 0) & (step < steps // 4))
    def _():
        held_query[...] += matmul(turned, query_grad[...])

    @pl.when(step == steps - 1)
    def _():
        half = stay.shape[0]
        width = (stay.shape[1] - WIDE) // 2
        for part in range(2):
            at = pl.ds(part * half, half)
            result = jnp.concatenate(
                [
                    held[at, :WIDE],
                    held[at, WIDE : WIDE + width],
                    held_query[at, :width],
                ],
                axis=1,
            ).astype(BF)

            @pl.when(ids[2] == part)
            def _(result=result):
                stay[...] = result

            @pl.when(ids[2] != part)
            def _(result=result):
                leave[...] = result


def weight_sums(ids, first_in, spread, query_grad, width, after):
    total, model = first_in.shape
    block = query_grad.shape[0] // 2
    shape = jax.ShapeDtypeStruct((model // 2, WIDE + 2 * width), BF)
    flat = pl.BlockSpec(shape.shape, lambda i, ids: (0, 0))
    return pl.pallas_call(
        ordered_after(weight_sums_kernel, 4, len(after)),
        grid_spec=pltpu.PrefetchScalarGridSpec(
            num_scalar_prefetch=1,
            grid=(total // block,),
            in_specs=[
                pl.BlockSpec((block, model), lambda i, ids: (i, 0)),
                pl.BlockSpec((block, 2 * WIDE), lambda i, ids: (i, 0)),
                pl.BlockSpec((block, WIDE), lambda i, ids: (jnp.minimum(i, 1), 0)),
            ]
            + [ANYWHERE] * len(after),
            out_specs=[flat, flat],
            scratch_shapes=[pltpu.VMEM((model, 2 * WIDE), F32), pltpu.VMEM((model, WIDE), F32)],
        ),
        out_shape=[shape, shape],
        compiler_params=vmem(22),
        cost_estimate=taking(0.01),
        name="weight_sums",
    )(ids, first_in, spread, query_grad, *after)


def first_sums_kernel(ids, own_a, came_a, stay_b, came_b, stay, away, keep, send):
    half = stay.shape[0]
    keep[...] = (stay_b[0].astype(F32) + came_b[0].astype(F32)).astype(BF)
    send[...] = (stay_b[1].astype(F32) + came_b[1].astype(F32)).astype(BF)
    for part in range(2):
        rows = pl.ds(part * half, half)
        total = (own_a[rows, :].astype(F32) + came_a[rows, :].astype(F32)).astype(BF)

        @pl.when(ids[2] == part)
        def _(total=total):
            stay[...] = total

        @pl.when(ids[2] != part)
        def _(total=total):
            away[...] = total


def first_sums(ids, own_a, came_a, stay_b, came_b):
    part, model = own_a.shape
    operands = [own_a, came_a, stay_b, came_b]
    shape = jax.ShapeDtypeStruct
    out_shape = [shape((part // 2, model), BF)] * 2 + [shape(stay_b.shape[1:], BF)] * 2
    return pl.pallas_call(
        first_sums_kernel,
        grid_spec=pltpu.PrefetchScalarGridSpec(
            num_scalar_prefetch=1,
            grid=(1,),
            in_specs=[whole(a) for a in operands],
            out_specs=[pl.BlockSpec(a.shape, lambda *_: (0, 0)) for a in out_shape],
        ),
        out_shape=out_shape,
        compiler_params=vmem(18),
        cost_estimate=taking(0.01),
        name="first_sums",
    )(ids, *operands)


def dense_kernel(ids, mine, theirs, up, down, out):
    half, out_half = up.shape[0], out.shape[0]
    for j, part in enumerate((mine, theirs)):

        @pl.when(pl.program_id(0) == j)
        def _(part=part):
            up[...] = part[:half, :].astype(F32)
            out[...] = part[half : half + out_half, :].astype(F32)
            down[...] = part[half + out_half :, :].astype(F32)


def dense_results(ids, mine, theirs, width):
    rows, model = mine.shape
    place = lambda size: pl.BlockSpec(
        (size, model), lambda j, ids: (jnp.bitwise_xor(ids[2], j), 0)
    )
    shape = jax.ShapeDtypeStruct
    return pl.pallas_call(
        dense_kernel,
        grid_spec=pltpu.PrefetchScalarGridSpec(
            num_scalar_prefetch=1,
            grid=(2,),
            in_specs=[whole(mine), whole(theirs)],
            out_specs=[place(model // 2), place(model // 2), place(width // 2)],
        ),
        out_shape=[shape((model, model), F32)] * 2 + [shape((width, model), F32)],
        compiler_params=vmem(14),
        cost_estimate=taking(0.01),
        name="dense_results",
    )(ids, mine, theirs)


def held_until(array, after):
    return pl.pallas_call(
        lambda *refs: None,
        in_specs=[ANYWHERE] * (1 + len(after)),
        out_specs=ANYWHERE,
        out_shape=jax.ShapeDtypeStruct(array.shape, array.dtype),
        input_output_aliases={0: 0},
        name="held",
    )(array, *after)


def swap(array, flip, axis="mp"):
    return lax.ppermute(array, axis, [(i, i ^ flip) for i in range(lax.axis_size(axis))])


def upward(array, ranks):
    return lax.ppermute(array, "seq", [(i, i + 1) for i in range(ranks - 1)])


def downward(array, ranks):
    return lax.ppermute(array, "seq", [(i + 1, i) for i in range(ranks - 1)])


def spread_over_mp(part):
    across = swap(part, 2)
    return [part, swap(part, 1), across, swap(across, 1)]


def body_resident(
    inputs,
    selection,
    gain1,
    shift1,
    w_qkv,
    b_qv,
    w_score,
    b_score,
    w_out,
    b_out,
    gain2,
    shift2,
    w_up,
    b_up,
    w_down,
    b_down,
    cotangent,
):
    ranks = lax.axis_size("seq")
    me, rank, side = lax.axis_index("mp"), lax.axis_index("seq"), lax.axis_index("dp")
    ids = jnp.stack([me, rank, side]).astype(jnp.int32)
    rows, model = inputs.shape[1:]
    quarter = rows // 4
    block = quarter // 2
    total = ranks * rows
    blocks = rows // KB
    width = w_qkv.shape[2]
    heads = width // HD

    own = lax.dynamic_slice_in_dim(inputs[0], me * quarter, quarter, 0)
    arriving = {}
    for h in range(2):
        part = own[h * block : (h + 1) * block]
        for k in range(1, ranks):
            part = upward(part, ranks)
            arriving[k, h] = part
    gathered = {}
    for k in range(1, ranks):
        for halves in ((0, 1),) if k < ranks - 1 else ((0,), (1,)):
            mine = jnp.concatenate([arriving[k, h] for h in halves], axis=0)
            mine = jnp.concatenate([mine, swap(mine, 2)], axis=0)
            gathered[k, halves] = [mine, swap(mine, 1)]

    b_high = b_up.astype(BF)
    b_low = (b_up - b_high.astype(F32)).astype(BF)
    out_rows = jnp.concatenate(
        [w_out, b_high[None], b_low[None], jnp.zeros((14, model), BF)], axis=0
    )
    w_outs = spread_over_mp(out_rows)
    first = swap(jnp.where(side == 0, w_up, w_down), 2)
    second = swap(first, 1, "dp")
    w_ups = [w_up, swap(w_up, 1), first, swap(first, 1)]
    w_downs = [w_down, swap(w_down, 1), second, swap(second, 1)]

    vectors = jnp.stack([gain1, shift1, b_out, gain2, shift2, b_down] + [gain1] * 2, axis=0)
    lines = jnp.pad(
        jnp.stack([jnp.pad(b_score, (width, WIDE - width - heads))[:width], b_qv[1], b_qv[0]]),
        ((0, 5), (0, WIDE - width)),
    )
    lines = lax.dynamic_update_slice(lines, b_score[None], (0, width))
    wide = lambda a: jnp.pad(a, ((0, 0), (0, WIDE - a.shape[1])))
    wq, wv = wide(w_qkv[:, 0]), wide(w_qkv[:, 2])
    wk = wide(jnp.concatenate([w_qkv[:, 1], w_score], axis=1))

    *buffers, qt = project_own(
        ids, inputs[0], vectors, lines, (wk, wv, wq), width, total, block, [arriving[ranks - 1, h] for h in range(2)]
    )
    for (k, halves), arrays in gathered.items():
        count = len(halves)
        buffers = project(
            arrays,
            [(j % 2, (j // 2 * count + i) * block) for j in range(4) for i in range(count)],
            block,
            width,
            lambda j, k=k, h=halves[0], count=count: 8 * k + (2 // count) * j + h,
            vectors,
            lines,
            (wk, wv),
            buffers,
            [(first, second)[k - 1]] if k < ranks - 1 else (),
        )
    first_in, ka, va = buffers

    chosen = selection[0]
    *mixed, norm = attend(ids, chosen, ka, va, qt, blocks)

    features = [mixed[0]] + [swap(mixed[j], j) for j in (1, 2, 3)]
    *mixed_grads, output, hidden_grad, kept, sent, sums, up_biases = feed_forward(
        ids, vectors, inputs[0], cotangent[0], features, w_outs, w_ups, w_downs
    )
    returned = [mixed_grads[0]] + [swap(mixed_grads[j], j) for j in (1, 2, 3)]

    part = model + width
    own_a, far_a, stay_b, leave_b = combine(ids, kept, swap(sent, 1), part)
    came_a, came_b = swap(far_a, 2), swap(leave_b, 1, "dp")

    weights = (wk, wv, wq)
    spread, query_grad, totals = attend_back(
        ids, chosen, ka, va, qt, norm, returned, blocks, (far_a, leave_b)
    )

    weights = (wk, wv, wq)
    stay_a, away_a, keep_b, send_b = first_sums(ids, own_a, came_a, stay_b, came_b)
    kept_3, sent_3 = push(spread, weights, 3, quarter, None, (away_a,))
    came_a, came_b, arrived_3 = swap(away_a, 1, "dp"), swap(send_b, 2), swap(sent_3, 1)
    qkv, qkv_leave = weight_sums(ids, first_in, spread, query_grad, width, (sent_3,))
    kept_2, sent_2 = push(spread, weights, 2, quarter, None, (qkv_leave,))
    dense = jnp.concatenate([stay_a + came_a, keep_b + came_b], axis=0)
    across = held_until(kept_3[1] + arrived_3[1], (dense, sent_2))
    dense = lax.psum(dense, "seq")
    sent_2, qkv_leave = held_until(sent_2, (across,)), held_until(qkv_leave, (across,))
    crossed_3, came_qkv, arrived_2 = swap(across, 2), swap(qkv_leave, 1, "dp"), swap(sent_2, 1)
    kept_1, sent_1 = push(spread, weights, 1, quarter, None, (across,))
    kept_0, sent_0 = push(spread, weights, 0, quarter, query_grad, (sent_1,))
    qkv = qkv + came_qkv
    across = kept_2[1] + arrived_2[1]
    carried = held_until(kept_3[0] + arrived_3[0] + crossed_3, (qkv, sent_0, across))
    carried = downward(carried, ranks)
    crossed_2, arrived_1, arrived_0 = swap(across, 2), swap(sent_1, 1), swap(sent_0, 1)
    mine = kept_2[0] + arrived_2[0] + crossed_2 + carried
    across = held_until(kept_1[1] + arrived_1[1], (mine,))
    output_parts = spread_over_mp(held_until(output, (mine,)))
    carried = downward(mine, ranks)
    crossed_1 = swap(across, 2)
    mine = kept_1[0] + arrived_1[0] + crossed_1 + carried
    across = held_until(kept_0[1] + arrived_0[1], (mine,))
    dense = held_until(dense, (across,))
    qkv = lax.psum(held_until(qkv, (dense,)), "seq")
    dense_theirs = swap(dense, 1, "dp")
    carried = downward(mine, ranks)
    crossed_0 = swap(across, 2)
    mine = kept_0[0] + arrived_0[0] + crossed_0

    output = ordered(ids, 0, output_parts, BF)
    input_part, small = finish(
        ids,
        vectors,
        inputs[0],
        carried,
        mine,
        hidden_grad,
        sums,
        up_biases,
        totals,
        (output, dense_theirs),
    )
    across = swap(input_part, 2)
    input_parts = [input_part, swap(input_part, 1), across]
    input_parts.append(swap(held_until(across, (qkv,)), 1))
    for flip in (1, 2):
        small = small + swap(small, flip)
    small = small + swap(small, 1, "dp")
    qkv_sum = ordered(ids, 2, [qkv, swap(qkv, 1, "dp")], F32)
    up_grad, down_grad, out_grad = dense_results(ids, dense, dense_theirs, width)
    for flip in (1, 2):
        small = small + swap(small, flip, "seq")
    input_grad = ordered(ids, 0, input_parts, BF)
    up_bias = lax.dynamic_slice_in_dim(small, 4 + me, 1, 0)[0]
    biases = lax.dynamic_slice_in_dim(small, 8 + me, 1, 0)[0]
    query_at, value_at = WIDE + width, WIDE
    qkv_grad = jnp.stack(
        [qkv_sum[:, query_at:], qkv_sum[:, :width], qkv_sum[:, value_at:query_at]], axis=1
    )
    qv_bias_grad = jnp.stack(
        [biases[2 * WIDE : 2 * WIDE + width], biases[WIDE : WIDE + width]], axis=0
    )
    return (
        output[None],
        input_grad[None],
        small[12],
        small[13],
        qkv_grad,
        qv_bias_grad,
        qkv_sum[:, width : width + heads],
        biases[width : width + heads],
        out_grad,
        small[2],
        small[0],
        small[1],
        up_grad,
        up_bias,
        down_grad,
        small[3],
    )


RESIDENT_TOKENS = 8192


def solution(mesh):
    def body(*args):
        tokens = args[0].shape[1] * mesh.shape["seq"]
        resident = mesh.shape["mp"] == 4 and mesh.shape["dp"] == 2
        resident = resident and mesh.shape["seq"] == 4 and tokens <= RESIDENT_TOKENS
        return (body_resident if resident else body_general)(*args)

    return jax.shard_map(
        body,
        mesh=mesh,
        in_specs=(
            P("dp", "seq", None),
            P("dp", "seq", None),
            P(),
            P(),
            P(None, None, "mp"),
            P(None, "mp"),
            P(None, "mp"),
            P("mp"),
            P("mp", None),
            P(),
            P(),
            P(),
            P(None, "mp"),
            P("mp"),
            P("mp", None),
            P(),
            P("dp", "seq", None),
        ),
        out_specs=(
            P("dp", "seq", None),
            P("dp", "seq", None),
            P(),
            P(),
            P(None, None, "mp"),
            P(None, "mp"),
            P(None, "mp"),
            P("mp"),
            P("mp", None),
            P(),
            P(),
            P(),
            P(None, "mp"),
            P("mp"),
            P("mp", None),
            P(),
        ),
        check_vma=False,
    )
```
